32 devices in a mesh: branch: 2 (over core), pts: 16 (over z, y, x).
Axes of the slice: x: 2, y: 2, z: 4, core: 2. Of those that a mesh axis runs over, the one named last changes fastest.
Arguments:
- tokens: bfloat16 [32768, 128], P('pts'), may hold values from -6 to 6
- funcs: float32 [2, 3, 65536], P('branch', None, 'pts'), may hold values from -6 to 6
- item_counts: int32 [4], replicated, may hold values from 1 to 16384, 32768 in all
- func_counts: int32 [2, 4], P('branch'), may hold values from 1 to 32768, as said below
- gate_ints: int32 [32768, 4], P('pts'), may hold values from 2 to 8
- cotangent: float32 [32768, 128], P('pts'), may hold values from -6 to 6
- shared_master: float32 [297088], P('pts')
- shared_m: float32 [297088], P('pts'), may hold values from -7.964851 to 7.964851
- shared_v: float32 [297088], P('pts'), may hold values from 0.32768 to 1.31072
- branch_master: float32 [2, 49792], P('branch', 'pts')
- branch_m: float32 [2, 49792], P('branch', 'pts'), may hold values from -7.964851 to 7.964851
- branch_v: float32 [2, 49792], P('branch', 'pts'), may hold values from 0.32768 to 1.31072
Outputs:
- output: bfloat16 [32768, 128], P('pts')
- token_grad: float32 [32768, 128], P('pts')
- new_shared: float32 [297088], P('pts')
- new_shared_m: float32 [297088], P('pts')
- new_shared_v: float32 [297088], P('pts')
- new_branch: float32 [2, 49792], P('branch', 'pts')
- new_branch_m: float32 [2, 49792], P('branch', 'pts')
- new_branch_v: float32 [2, 49792], P('branch', 'pts')
The draws below stay inside these ranges and needn't reach their ends.
Inputs may be any that keep to these rules, and one draw needn't show every extreme that they name: `func_counts`: row b sums to 65536 // (b + 1); sample slots past that sum are padding of no item; one item of function 0 holds exactly the largest count.
All inputs are finite; a program needn't handle non-finite values.
Results may differ from the reference program's by a relative error of at most 0.0085.
The reference program's roundings to bfloat16 on the way count: a program that leaves them out, or rounds other values in their place, can miss the bound.
Values may be sent and summed in bfloat16 or wider, within the bound.
No kernel may reach another device: no remote copies, remote signals or barrier semaphores. Data moves between devices by JAX's collectives and lax.ppermute only.
A program may use at most 128 MiB of HBM per device.

```python
import math
import jax
import jax.numpy as jnp
import numpy as np
from jax import lax

D = 128
H = 8
HD = 16
FF = 256
E = 4
FIN = 3
STEP = 10
TOK_DEV = 2048
NB = 2
ITEMS = 4
TOKENS = 32768
FSAMP = 65536
SH_LEN = 297088
BR_LEN = 49792


def shared_scales():
    return [((D,), 0, 0.4), ((D,), 1, 0.3), ((D, D), 1, D ** (-0.5)), ((D, D), 1, 2.0 * D ** (-0.5)), ((D,), 1, 0.1), ((D,), 0, 0.4), ((D,), 1, 0.3), ((E, D, FF), 1, D ** (-0.5)), ((E, FF), 1, 0.1), ((E, FF, D), 1, 2.0 * FF ** (-0.5)), ((E, D), 1, 0.1)]


def branch_scales():
    return [((FIN, D), 1, 1.0), ((D,), 1, 0.3), ((D, D), 1, D ** (-0.5)), ((D,), 1, 0.3), ((D, 2 * D), 1, 2.0 * D ** (-0.5))]


def draw_segments(key, layout, total):
    pieces = []
    used = 0
    for number, (dims, kind_flag, level) in enumerate(layout):
        sub_key = jax.random.fold_in(key, number)
        amount = math.prod(dims)
        if kind_flag == 0:
            piece = 1.0 + level * jax.random.uniform(sub_key, (amount,), jnp.float32, -1.0, 1.0)
        else:
            piece = level * jnp.clip(jax.random.normal(sub_key, (amount,), jnp.float32), -4.0, 4.0)
        pieces.append(piece)
        used += amount
    tail_key = jax.random.fold_in(key, 1000)
    pieces.append(0.05 * jax.random.normal(tail_key, (total - used,), jnp.float32))
    return jnp.concatenate(pieces)


def draw_shared_master(key, part):
    key = jax.random.fold_in(key, 5)
    return draw_segments(key, shared_scales(), SH_LEN)


def draw_branch_master(key, part):
    key = jax.random.fold_in(key, 7)
    rows = [draw_segments(jax.random.fold_in(key, branch_no), branch_scales(), BR_LEN) for branch_no in range(NB)]
    return jnp.stack(rows)


def even_counts(key, amount, pieces):
    share = amount // pieces
    extra = amount - share * pieces
    reach = share // 4
    jitter = jax.random.randint(key, (pieces,), -reach, reach + 1).astype(jnp.int32)
    index = jnp.arange(pieces, dtype=jnp.int32)
    partner = jnp.where(index % 2 == 1, index - 1, index)
    paired = index < 2 * (pieces // 2)
    signs = jnp.where(index % 2 == 1, -1, 1).astype(jnp.int32)
    moved = jnp.where(paired, signs * jitter[partner], 0).astype(jnp.int32)
    return (share + moved + (index < extra).astype(jnp.int32)).astype(jnp.int32)


def draw_func_counts(key, part):
    key = jax.random.fold_in(key, 11)
    most_count = 2 * (FSAMP // ITEMS)
    rows = []
    for branch_no in range(NB):
        total_slots = FSAMP // (branch_no + 1)
        row_key = jax.random.fold_in(key, branch_no)
        if branch_no == 0:
            others = even_counts(row_key, total_slots - most_count, ITEMS - 1)
            place = jax.random.randint(jax.random.fold_in(row_key, 50), (), 0, ITEMS).astype(jnp.int32)
            index = jnp.arange(ITEMS, dtype=jnp.int32)
            source = jnp.clip(jnp.where(index > place, index - 1, index), 0, ITEMS - 2)
            row = jnp.where(index == place, most_count, others[source]).astype(jnp.int32)
        else:
            row = even_counts(row_key, total_slots, ITEMS)
        rows.append(row)
    return jnp.stack(rows).astype(jnp.int32)


def touch_ends(values, rng, least, top_value):
    longest = values.shape.index(max(values.shape))
    spots = []
    for shift in (0, 1):
        where = [jax.random.randint(jax.random.fold_in(rng, axis), (), 0, length) for axis, length in enumerate(values.shape)]
        where[longest] = (where[longest] + shift) % values.shape[longest]
        spots.append(tuple(where))
    return values.at[spots[0]].set(least).at[spots[1]].set(top_value)


def block_levels(stream_key, shape, cuts, least, top_value):
    def one(dim, parts):
        steps = jax.random.uniform(jax.random.fold_in(jax.random.fold_in(stream_key, 6), dim), (parts,), jnp.float32, least / len(cuts), top_value / len(cuts))
        return jnp.repeat(jnp.exp(steps), shape[dim] // parts).reshape((-1,) + (1,) * (len(shape) - dim - 1))

    level = one(*cuts[0])
    for cut in cuts[1:]:
        level = level * one(*cut)
    return level


def length_profile(count, total, limit, lean):
    loads = [(1 << 20) // math.isqrt(grade ** lean) + 1 for grade in range(2, count + 1)]
    surplus, given = total - limit - (count - 1), [1] * (count - 1)
    while surplus > 0:
        candidates = [i for i in range(count - 1) if given[i] < limit]
        whole, remaining = sum([loads[i] for i in candidates]), surplus
        for i in candidates:
            more = min(limit - given[i], max(1, remaining * loads[i] // whole), surplus)
            given[i] = given[i] + more
            surplus = surplus - more
    return np.array([limit] + given)


def uneven(rng, count, total, bound, skew):
    if count == 2:
        one = jax.random.randint(rng, (), max(1, total - bound), min(bound, total - 1) + 1)
        return jnp.stack([one, total - one])
    tallies = jnp.asarray(length_profile(count, total, bound, skew), jnp.int32)
    pairs = (count - 1) // 2
    giver, sink = tallies[1:1 + 2 * pairs:2], tallies[2:2 + 2 * pairs:2]
    slack = jnp.minimum(giver - 1, bound - sink)
    moved = jax.random.randint(jax.random.fold_in(rng, 1), (pairs,), 0, 1 << 20) % (slack + 1)
    tallies = tallies.at[1:1 + 2 * pairs:2].set(giver - moved).at[2:2 + 2 * pairs:2].set(sink + moved)
    return tallies[jax.random.permutation(jax.random.fold_in(rng, 2), count)]


def gaussian(rng, shape, scale, limit, cuts=(), kind=jnp.bfloat16):
    values = jax.random.normal(rng, shape, jnp.float32) * scale
    if len(cuts) > 0:
        values = block_levels(rng, shape, cuts, -0.22, 0.18) * values
    return jnp.clip(values, min=-limit, max=limit).astype(kind)


def setup_inputs(seed: int = 0) -> dict:
    key_of = jax.random.split(jax.random.key(seed), 13)
    return {
        "tokens": gaussian(key_of[0], (TOKENS, D), 1.0, 6.0, ((0, 16),)),
        "funcs": gaussian(key_of[1], (NB, FIN, FSAMP), 1.0, 6.0, ((0, 2), (2, 16)), jnp.float32),
        "item_counts": uneven(key_of[2], ITEMS, TOKENS, 8 * TOK_DEV, 2).astype(jnp.int32),
        "func_counts": draw_func_counts(jax.random.fold_in(key_of[12], 71), 0),
        "gate_ints": touch_ends(jax.random.randint(key_of[4], (TOKENS, E), 2, 9), jax.random.fold_in(key_of[4], 1), 2, 8).astype(jnp.int32),
        "cotangent": gaussian(key_of[5], (TOKENS, D), 1.0, 6.0, ((0, 16),), jnp.float32),
        "shared_master": draw_shared_master(jax.random.fold_in(key_of[12], 71), 0),
        "shared_m": gaussian(key_of[7], (SH_LEN,), (0.011 * TOKENS ** 0.5), 7.964851, ((0, 16),), jnp.float32),
        "shared_v": jnp.clip(jnp.exp(math.log(1.31072) - 1.3862944 * jax.random.uniform(key_of[8], (SH_LEN,), jnp.float32) ** block_levels(key_of[8], (SH_LEN,), ((0, 16),), -0.2, 0.2)), 0.32768, 1.31072),
        "branch_master": draw_branch_master(jax.random.fold_in(key_of[12], 71), 0),
        "branch_m": gaussian(key_of[10], (NB, BR_LEN), (0.011 * TOKENS ** 0.5), 7.964851, ((0, 2), (1, 16)), jnp.float32),
        "branch_v": jnp.clip(jnp.exp(math.log(1.31072) - 1.3862944 * jax.random.uniform(key_of[11], (NB, BR_LEN), jnp.float32) ** block_levels(key_of[11], (NB, BR_LEN), ((0, 2), (1, 16)), -0.2, 0.2)), 0.32768, 1.31072),
    }


EPS_NORM = 1e-05
BETA_ONE = 0.9
BETA_TWO = 0.999
RATE_LEARN = 0.1
DECAY_RATE = 0.01
EPS_ADAM = 1e-08
precise = lax.Precision.HIGHEST

@jax.custom_vjp
def low(v):
    return lax.optimization_barrier(v.astype(jnp.bfloat16)).astype(jnp.float32)

@jax.custom_vjp
def low_back(v):
    return v

def low_keep(v):
    return (low(v), None)

def low_pass(kept, grad):
    return (grad,)

def back_keep(v):
    return (v, None)

def back_low(kept, grad):
    return (low(grad),)
low.defvjp(low_keep, low_pass)
low_back.defvjp(back_keep, back_low)

def shared_layout():
    return [(D,), (D,), (D, D), (D, D), (D,), (D,), (D,), (E, D, FF), (E, FF), (E, FF, D), (E, D)]

def branch_layout():
    return [(FIN, D), (D,), (D, D), (D,), (D, 2 * D)]

def unpack(vector, layout):
    pieces = []
    offset = 0
    for dims in layout:
        amount = math.prod(dims)
        pieces.append(vector[offset:offset + amount].reshape(dims))
        offset += amount
    return pieces

def matmul(left, right):
    return jnp.dot(left, right, precision=precise, preferred_element_type=jnp.float32)

def layer_norm(values, norm_gain, norm_shift):
    centre = values - lax.optimization_barrier(jnp.mean(values, axis=-1, keepdims=True))
    spread = lax.optimization_barrier(jnp.mean(centre * centre, axis=-1, keepdims=True))
    return centre * lax.rsqrt(spread + EPS_NORM) * norm_gain + norm_shift

def segment_table(counts, length):
    item_ends = jnp.cumsum(counts)
    item_starts = item_ends - counts
    position = jnp.arange(length, dtype=jnp.int32)[:, None]
    return ((position >= item_starts[None, :]) & (position < item_ends[None, :])).astype(jnp.float32)

def forward(tokens_in, shared_w, branch_w, funcs, point_hot, sample_hots, gates):
    gain_one, shift_one, query_w, output_w, output_b, gain_two, shift_two, expert_up, expert_up_b, expert_down, expert_down_b = unpack(shared_w, shared_layout())
    row_total = tokens_in.shape[0]
    normed = layer_norm(tokens_in, gain_one, shift_one)
    query = low_back(matmul(low(normed), query_w))
    query_soft = low(jax.nn.softmax(query.reshape(row_total, H, HD), axis=-1))
    spread_q = point_hot[:, :, None, None] * query_soft[:, None]
    merged = jnp.zeros((row_total, H, HD), jnp.float32)
    for branch_no in range(NB):
        input_w, input_b, hidden_w, hidden_b, pair_w = unpack(branch_w[branch_no], branch_layout())
        samples = funcs[branch_no].T
        first = low(jax.nn.gelu(matmul(samples, input_w) + input_b))
        second = low(jax.nn.gelu(low_back(matmul(first, hidden_w) + hidden_b)))
        pair = low_back(matmul(second, pair_w))
        keys = low(jax.nn.softmax(pair[:, :D].reshape(-1, H, HD), axis=-1))
        values = low(pair[:, D:].reshape(-1, H, HD))
        weighted = sample_hots[branch_no][:, :, None, None] * keys[:, None]
        summary = jnp.einsum('jiha,jhc->ihac', weighted, values, precision=precise)
        totals = lax.optimization_barrier(jnp.sum(weighted, axis=0))
        numer = jnp.einsum('tiha,ihac->thc', spread_q, summary, precision=precise)
        denom = jnp.einsum('tiha,iha->th', spread_q, totals, precision=precise)
        merged = merged + numer / denom[:, :, None]
    attended = (merged / NB).reshape(row_total, D)
    projected = low_back(matmul(low(attended), output_w) + output_b)
    residual = tokens_in + projected
    normed_two = low(layer_norm(residual, gain_two, shift_two))
    mixture = jnp.zeros_like(residual)
    for expert_no in range(E):
        inner = low_back(matmul(normed_two, expert_up[expert_no]) + expert_up_b[expert_no])
        active = low(jax.nn.gelu(inner))
        result = low_back(matmul(active, expert_down[expert_no]) + expert_down_b[expert_no])
        mixture = mixture + gates[:, expert_no:expert_no + 1] * result
    return residual + mixture

def adam_step(master, moment_one, moment_two, grad):
    first = BETA_ONE * moment_one + (1.0 - BETA_ONE) * grad
    second = BETA_TWO * moment_two + (1.0 - BETA_TWO) * grad * grad
    first_hat = first / (1.0 - BETA_ONE ** STEP)
    second_hat = second / (1.0 - BETA_TWO ** STEP)
    fresh = master - RATE_LEARN * (first_hat / (jnp.sqrt(second_hat) + EPS_ADAM) + DECAY_RATE * master)
    return (fresh, first, second)

def reference(tokens, funcs, item_counts, func_counts, gate_ints, cotangent, shared_master, shared_m, shared_v, branch_master, branch_m, branch_v):
    shared_w = shared_master.astype(jnp.bfloat16).astype(jnp.float32)
    branch_w = branch_master.astype(jnp.bfloat16).astype(jnp.float32)
    point_hot = segment_table(item_counts, TOKENS)
    sample_hots = [segment_table(func_counts[branch_no], FSAMP) for branch_no in range(NB)]
    gate_vals = gate_ints.astype(jnp.float32)
    gates = gate_vals / lax.optimization_barrier(jnp.sum(gate_vals, axis=1, keepdims=True))

    def closed(tokens_in, shared_in, branch_in):
        return forward(tokens_in, shared_in, branch_in, funcs, point_hot, sample_hots, gates)
    output, pullback = jax.vjp(closed, tokens.astype(jnp.float32), shared_w, branch_w)
    token_grad, shared_grad, branch_grad = pullback(cotangent)
    new_shared, new_shared_m, new_shared_v = adam_step(shared_master, shared_m, shared_v, shared_grad)
    new_branch, new_branch_m, new_branch_v = adam_step(branch_master, branch_m, branch_v, branch_grad)
    return (output.astype(jnp.bfloat16), token_grad, new_shared, new_shared_m, new_shared_v, new_branch, new_branch_m, new_branch_v)
```

```python
import functools
import math

import jax
import jax.numpy as jnp
from jax import lax
from jax.experimental import pallas as pl
from jax.experimental.pallas import tpu as pltpu
from jax.sharding import PartitionSpec as P

D = 128
H = 8
HD = 16
FF = 256
E = 4
FIN = 3
STEP = 10

EPS_NORM = 1e-05
BETA_ONE = 0.9
BETA_TWO = 0.999
RATE_LEARN = 0.1
DECAY_RATE = 0.01
EPS_ADAM = 1e-08

LANES = 128
VMEM_LIMIT = 56 * 1024 * 1024
SAMPLE_TILE = 512
TOKEN_TILE = 512

F32 = jnp.float32
BF16 = jnp.bfloat16

ROW_GAIN_ONE = 0
ROW_SHIFT_ONE = 1
ROW_QUERY = 2
ROW_OUT = ROW_QUERY + D
ROW_OUT_B = ROW_OUT + D
ROW_GAIN_TWO = ROW_OUT_B + 1
ROW_SHIFT_TWO = ROW_GAIN_TWO + 1
ROW_UP = ROW_SHIFT_TWO + 1
ROW_UP_B = ROW_UP + E * D * 2
ROW_DOWN = ROW_UP_B + E * 2
ROW_DOWN_B = ROW_DOWN + E * FF
SHARED_ROWS = ROW_DOWN_B + E

ROW_IN = 0
ROW_IN_B = ROW_IN + FIN
ROW_HID = ROW_IN_B + 1
ROW_HID_B = ROW_HID + D
ROW_PAIR = ROW_HID_B + 1
BRANCH_ROWS = ROW_PAIR + 2 * D

COL_GAIN_ONE = 0
COL_SHIFT_ONE = 1
COL_OUT_B = 2
COL_GAIN_TWO = 3
COL_SHIFT_TWO = 4
COL_UP_B = 5
COL_DOWN_B = COL_UP_B + 2 * E

TANH_C = math.sqrt(2.0 / math.pi)
TANH_CUBE = 0.044715


def up_to(amount, unit):
    return -(-amount // unit) * unit


def adam_step(master, moment_one, moment_two, grad):
    first = BETA_ONE * moment_one + (1.0 - BETA_ONE) * grad
    second = BETA_TWO * moment_two + (1.0 - BETA_TWO) * grad * grad
    first_hat = first / (1.0 - BETA_ONE**STEP)
    second_hat = second / (1.0 - BETA_TWO**STEP)
    fresh = master - RATE_LEARN * (
        first_hat / (jnp.sqrt(second_hat) + EPS_ADAM) + DECAY_RATE * master
    )
    return (fresh, first, second)


def dot_nn(left, right):
    return jnp.dot(left, right, preferred_element_type=F32)


def dot_nt(left, right):
    return lax.dot_general(left, right, (((1,), (1,)), ((), ())), preferred_element_type=F32)


def head_sum(values):
    split = values.reshape(H, HD, values.shape[1])
    total = jnp.sum(split, axis=1, keepdims=True)
    return jnp.broadcast_to(total, split.shape).reshape(values.shape)


def head_softmax(values):
    split = values.reshape(H, HD, values.shape[1])
    top = jnp.max(split, axis=1, keepdims=True)
    raised = jnp.exp(split - top)
    total = jnp.sum(raised, axis=1, keepdims=True)
    return (raised * (1.0 / total)).reshape(values.shape)


def gelu_parts(inner):
    square = inner * inner
    bend = TANH_C + (TANH_C * TANH_CUBE) * square
    curve = jnp.tanh(inner * bend)
    gate = 0.5 + 0.5 * curve
    slope = (TANH_C) + (3.0 * TANH_C * TANH_CUBE) * square
    grad = gate + inner * (0.5 - 0.5 * curve * curve) * slope
    return inner * gate, grad


def wide(tile, length):
    if length == tile.shape[1]:
        return tile
    return jnp.concatenate([tile] * (length // tile.shape[1]), axis=1)


def column(matrix, index, length):
    return jnp.broadcast_to(matrix[:, index : index + 1], (matrix.shape[0], length))


def fold_lanes(values):
    total = values[:, :LANES]
    for start in range(LANES, values.shape[1], LANES):
        total = total + values[:, start : start + LANES]
    return total


def lane_total_row(values):
    return jnp.sum(jnp.transpose(values), axis=0, keepdims=True)


def head_mask():
    row = lax.broadcasted_iota(jnp.int32, (D, D), 0) // HD
    col = lax.broadcasted_iota(jnp.int32, (D, D), 1) // HD
    return (row == col).astype(F32)


def fold_heads(values, mask):
    return jnp.sum((values * mask).reshape(H, HD, D), axis=0)


def spread_heads(compact, mask):
    return jnp.concatenate([compact] * H, axis=0) * mask


def store_starts(counts, starts, items):
    if items <= 8:
        total = jnp.int32(0)
        for item in range(items):
            starts[item] = total
            total = total + counts(item)
        starts[items] = total
    else:
        def step(item, total):
            starts[item] = total
            return total + counts(item)

        starts[items] = lax.fori_loop(0, items, step, jnp.int32(0))


def item_span(starts, items, begin, end):
    def step(item, span):
        low, high = span
        return (
            low + (starts[item + 1] <= begin).astype(jnp.int32),
            high + (starts[item] < end).astype(jnp.int32),
        )

    span = (jnp.int32(0), jnp.int32(0))
    if items <= 8:
        for item in range(items):
            span = step(item, span)
        return span
    return lax.fori_loop(0, items, step, span)


def item_row(starts, item, begin, length):
    position = begin + lax.broadcasted_iota(jnp.int32, (1, length), 1)
    return ((position >= starts[item]) & (position < starts[item + 1])).astype(F32)


def over_items(starts, items, begin, length, visit):
    low, high = item_span(starts, items, begin, begin + length)
    visit(jnp.minimum(low, items - 1), True)

    def step(item, carry):
        visit(item, False)
        return carry

    lax.fori_loop(low + 1, high, step, 0)


def put_shard(vec_ref, tmp_ref, number, shard, height):
    row, shift = divmod(number * shard, LANES)
    touched = (shift + shard - 1) // LANES + 1
    if shift == 0:
        vec_ref[row : row + touched, :] = tmp_ref[8 : 8 + touched, :]
        return
    if number == 0:
        tmp_ref[7:8, :] = jnp.zeros((1, LANES), F32)
    else:
        tmp_ref[7:8, :] = vec_ref[row : row + 1, :]
    lane = lax.broadcasted_iota(jnp.int32, (touched, LANES), 1)
    vec_ref[row : row + touched, :] = jnp.where(
        lane >= shift, tmp_ref[8 : 8 + touched, :], tmp_ref[7 : 7 + touched, :]
    )


def turned(block, amount):
    amount = amount % LANES
    return block if amount == 0 else pltpu.roll(block, amount, 1)


def take_shard(vec_ref, number, shard, height):
    row, shift = divmod(number * shard, LANES)
    here = vec_ref[row : row + height, :]
    if shift == 0:
        return here
    after = vec_ref[row + 1 : row + 1 + height, :]
    lane = lax.broadcasted_iota(jnp.int32, (height, LANES), 1)
    return turned(jnp.where(lane >= shift, here, after), LANES - shift)


def sample_forward_kernel(
    plan,
    scal_ref,
    count_ref,
    recv_ref,
    func_ref,
    msg_ref,
    keys_ref,
    vals_ref,
    first_ref,
    second_ref,
    slope_one_ref,
    slope_two_ref,
    hid_ref,
    pair_ref,
    vec_ref,
    tmp_ref,
    col_ref,
    hid_t_ref,
    pair_t_ref,
    acc_ref,
    starts,
):
    tile, items, parts, shard, height, slots = plan
    step = pl.program_id(0)

    @pl.when(step == 0)
    def _():
        store_starts(lambda item: count_ref[0, item], starts, items)
        acc_ref[...] = jnp.zeros(acc_ref.shape, F32)
        for number in range(parts):
            shift = (number * shard) % LANES
            tmp_ref[8 : 8 + height, :] = turned(recv_ref[number].astype(F32), shift)
            put_shard(vec_ref, tmp_ref, number, shard, height)
        for slot, row in enumerate((0, 1, 2, ROW_IN_B, ROW_HID_B)):
            col_ref[slot] = jnp.transpose(
                jnp.broadcast_to(vec_ref[row : row + 1, :], (D, D))
            )
        hid = vec_ref[ROW_HID : ROW_HID + D, :]
        hid_ref[...] = hid.astype(BF16)
        hid_t_ref[...] = jnp.transpose(hid).astype(BF16)
        for part in range(2):
            piece = vec_ref[pl.ds(ROW_PAIR + part, D, stride=2), :]
            pair_ref[:, part * D : (part + 1) * D] = piece.astype(BF16)
            pair_t_ref[part * D : (part + 1) * D, :] = jnp.transpose(piece).astype(BF16)

    funcs = func_ref[0]
    first_in = wide(col_ref[3], tile)
    for part in range(FIN):
        first_in = first_in + wide(col_ref[part], tile) * funcs[part : part + 1, :]
    first, slope_one = gelu_parts(first_in)
    first = first.astype(BF16)
    first_ref[...] = first
    slope_one_ref[...] = slope_one.astype(slope_one_ref.dtype)
    second_in = dot_nn(hid_t_ref[...], first) + wide(col_ref[4], tile)
    second, slope_two = gelu_parts(second_in)
    second = second.astype(BF16)
    second_ref[...] = second
    slope_two_ref[...] = slope_two.astype(slope_two_ref.dtype)
    pair = dot_nn(pair_t_ref[...], second)
    keys = head_softmax(pair[:D])
    keys_ref[...] = keys.astype(BF16)
    vals = pair[D:].astype(BF16)
    vals_ref[...] = vals
    vals_ones = jnp.concatenate([vals, jnp.ones((16, tile), BF16)], axis=0)
    begin = scal_ref[1] * slots + step * tile

    def visit(item, _):
        masked = (keys * item_row(starts, item, begin, tile)).astype(BF16)
        acc_ref[item] += dot_nt(vals_ones, masked)

    over_items(starts, items, begin, tile, visit)

    @pl.when(step == pl.num_programs(0) - 1)
    def _():
        mask = head_mask()
        msg_ref[items * HD :, :] = jnp.zeros((msg_ref.shape[0] - items * HD, LANES), F32)
        for item in range(items):
            msg_ref[item * HD : (item + 1) * HD, :] = fold_heads(acc_ref[item, :D, :], mask)
            msg_ref[items * HD + item : items * HD + item + 1, :] = acc_ref[item, D : D + 1, :]


def weight_kernel(
    plan,
    scal_ref,
    own_ref,
    other_ref,
    query_ref,
    query_t_ref,
    out_ref,
    out_t_ref,
    up_ref,
    up_t_ref,
    down_ref,
    down_t_ref,
    cols_ref,
    vec_ref,
    tmp_ref,
):
    parts, shard, half, offset = plan
    core = scal_ref[0]
    own_at = pl.multiple_of(8 + core * half, 8)
    other_at = pl.multiple_of(8 + (1 - core) * half, 8)
    for number in range(parts):
        shift = (number * shard) % LANES
        tmp_ref[pl.ds(own_at, half), :] = turned(
            own_ref[number, offset : offset + half, :].astype(F32), shift
        )
        tmp_ref[pl.ds(other_at, half), :] = turned(
            other_ref[number, offset : offset + half, :].astype(F32), shift
        )
        put_shard(vec_ref, tmp_ref, number, shard, 2 * half)
    query = vec_ref[ROW_QUERY : ROW_QUERY + D, :]
    query_ref[...] = query.astype(BF16)
    query_t_ref[...] = jnp.transpose(query).astype(BF16)
    out = vec_ref[ROW_OUT : ROW_OUT + D, :]
    out_ref[...] = out.astype(BF16)
    out_t_ref[...] = jnp.transpose(out).astype(BF16)
    for expert in range(E):
        for part in range(2):
            up = vec_ref[pl.ds(ROW_UP + expert * 2 * D + part, D, stride=2), :]
            up_ref[expert, :, part * D : (part + 1) * D] = up.astype(BF16)
            up_t_ref[expert, part * D : (part + 1) * D, :] = jnp.transpose(up).astype(BF16)
            row = ROW_DOWN + expert * FF + part * D
            down = vec_ref[row : row + D, :]
            down_ref[expert, part * D : (part + 1) * D, :] = down.astype(BF16)
            down_t_ref[expert, :, part * D : (part + 1) * D] = jnp.transpose(down).astype(BF16)
    tmp_ref[0:D, :] = jnp.zeros((D, LANES), F32)
    rows = [ROW_GAIN_ONE, ROW_SHIFT_ONE, ROW_OUT_B, ROW_GAIN_TWO, ROW_SHIFT_TWO]
    rows += [ROW_UP_B + number for number in range(2 * E)]
    rows += [ROW_DOWN_B + number for number in range(E)]
    for slot, row in enumerate(rows):
        tmp_ref[slot : slot + 1, :] = vec_ref[row : row + 1, :]
    cols_ref[...] = jnp.transpose(tmp_ref[0:D, :])


def norm_unit(values):
    centre = values - jnp.sum(values, axis=0, keepdims=True) * (1.0 / D)
    spread = jnp.sum(centre * centre, axis=0, keepdims=True) * (1.0 / D)
    scale = lax.rsqrt(spread + EPS_NORM)
    return centre * scale, scale


def norm_back(grad_unit, unit, scale):
    mean_one = jnp.sum(grad_unit, axis=0, keepdims=True) * (1.0 / D)
    mean_two = jnp.sum(grad_unit * unit, axis=0, keepdims=True) * (1.0 / D)
    return scale * (grad_unit - mean_one - unit * mean_two)


def query_kernel(
    scal_ref,
    token_ref,
    cot_ref,
    query_t_ref,
    cols_ref,
    token_t_ref,
    cot_t_ref,
    unit_ref,
    scale_ref,
    norm_ref,
    soft_ref,
):
    tokens = jnp.transpose(token_ref[...].astype(F32))
    length = tokens.shape[1]
    token_t_ref[...] = tokens.astype(BF16)
    cot_t_ref[...] = jnp.transpose(cot_ref[...])
    unit, scale = norm_unit(tokens)
    unit_ref[...] = unit
    scale_ref[...] = jnp.broadcast_to(scale, scale_ref.shape)
    cols = cols_ref[...]
    norm = (unit * column(cols, COL_GAIN_ONE, length) + column(cols, COL_SHIFT_ONE, length)).astype(
        BF16
    )
    norm_ref[...] = norm
    soft_ref[...] = head_softmax(dot_nn(query_t_ref[...], norm))


def token_kernel(
    plan,
    scal_ref,
    count_ref,
    own_ref,
    other_ref,
    gate_ref,
    token_t_ref,
    cot_t_ref,
    unit_ref,
    scale_ref,
    norm_ref,
    soft_ref,
    query_ref,
    out_w_ref,
    out_t_ref,
    up_ref,
    up_t_ref,
    down_ref,
    down_t_ref,
    cols_ref,
    output_ref,
    grad_ref,
    own_msg_ref,
    other_msg_ref,
    g_query_ref,
    g_out_ref,
    g_up_ref,
    g_down_ref,
    g_vec_ref,
    left_ref,
    back_ref,
    acc_ref,
    mix_ref,
    pull_ref,
    starts,
):
    tile, items, slots, steps = plan
    step = pl.program_id(0)
    first_row = scal_ref[1] * slots + scal_ref[0] * (tile * steps)

    @pl.when(step == 0)
    def _():
        store_starts(lambda item: count_ref[item], starts, items)
        acc_ref[...] = jnp.zeros(acc_ref.shape, F32)
        g_query_ref[...] = jnp.zeros(g_query_ref.shape, F32)
        g_out_ref[...] = jnp.zeros(g_out_ref.shape, F32)
        g_up_ref[...] = jnp.zeros(g_up_ref.shape, F32)
        g_down_ref[...] = jnp.zeros(g_down_ref.shape, F32)
        g_vec_ref[...] = jnp.zeros(g_vec_ref.shape, F32)
        mask = head_mask()
        low, high = item_span(starts, items, first_row, first_row + tile * steps)

        def build(item, carry):
            at = pl.multiple_of(item * HD, HD)
            for slot, source in enumerate((own_ref, other_ref)):
                block = spread_heads(source[pl.ds(at, HD), :], mask)
                total = source[pl.ds(items * HD + item, 1), :] * mask
                for kind, piece in enumerate((block, total)):
                    row = (2 * kind + slot) * D
                    high_part = piece.astype(BF16)
                    left_ref[item, row : row + D, :D] = high_part
                    left_ref[item, row : row + D, D:] = (piece - high_part.astype(F32)).astype(BF16)
                    turned_piece = jnp.transpose(piece)
                    if kind == 1:
                        turned_piece = turned_piece * (1.0 / HD)
                    back_ref[item, :, row : row + D] = turned_piece.astype(BF16)
            return carry

        lax.fori_loop(low, high, build, 0)

    cols = cols_ref[...]
    begin = first_row + step * tile
    soft = soft_ref[...]
    soft_low = soft.astype(BF16)
    soft_vals = soft_low.astype(F32)

    def forward(item, opening):
        masked = (soft_vals * item_row(starts, item, begin, tile)).astype(BF16)
        fresh = dot_nn(left_ref[item], jnp.concatenate([masked, masked], axis=0))
        mix_ref[...] = fresh if opening else mix_ref[...] + fresh

    over_items(starts, items, begin, tile, forward)
    numer_one, numer_two = mix_ref[:D, :], mix_ref[D : 2 * D, :]
    inv_one, inv_two = 1.0 / mix_ref[2 * D : 3 * D, :], 1.0 / mix_ref[3 * D :, :]
    own_one, own_two = numer_one * inv_one, numer_two * inv_two
    attended = (0.5 * (own_one + own_two)).astype(BF16)
    cot = cot_t_ref[...]
    residual = (
        token_t_ref[...].astype(F32)
        + dot_nn(out_t_ref[...], attended)
        + column(cols, COL_OUT_B, tile)
    )
    unit, scale = norm_unit(residual)
    gain_two = column(cols, COL_GAIN_TWO, tile)
    norm = (unit * gain_two + column(cols, COL_SHIFT_TWO, tile)).astype(BF16)
    ones = jnp.ones((16, tile), BF16)
    norm_ones = jnp.concatenate([norm, ones], axis=0)
    gates = gate_ref[...].astype(F32)
    gates = gates / jnp.sum(gates, axis=0, keepdims=True)
    mixture = residual
    grad_norm = jnp.zeros((D, tile), F32)
    for expert in range(E):
        bias = jnp.concatenate(
            [column(cols, COL_UP_B + 2 * expert + part, tile) for part in range(2)], axis=0
        )
        inner = dot_nn(up_t_ref[expert], norm) + bias
        active, slope = gelu_parts(inner)
        active = active.astype(BF16)
        result = dot_nn(down_t_ref[expert], active) + column(cols, COL_DOWN_B + expert, tile)
        gate = gates[expert : expert + 1, :]
        mixture = mixture + gate * result
        grad_result = (gate * cot).astype(BF16)
        g_down_ref[expert] += dot_nt(jnp.concatenate([active, ones], axis=0), grad_result)
        grad_inner = (slope * dot_nn(down_ref[expert], grad_result)).astype(BF16)
        g_up_ref[expert] += dot_nt(norm_ones, grad_inner)
        grad_norm = grad_norm + dot_nn(up_ref[expert], grad_inner)
    output_ref[...] = jnp.transpose(mixture).astype(BF16)
    g_vec_ref[2] += fold_lanes(grad_norm * unit)
    g_vec_ref[3] += fold_lanes(grad_norm)
    grad_residual = cot + norm_back(grad_norm * gain_two, unit, scale)
    grad_proj = grad_residual.astype(BF16)
    g_out_ref[...] += dot_nt(jnp.concatenate([attended, ones], axis=0), grad_proj)
    grad_own = 0.5 * dot_nn(out_w_ref[...], grad_proj)
    grad_one, grad_two = grad_own * inv_one, grad_own * inv_two
    sum_one = -head_sum(grad_one * own_one)
    sum_two = -head_sum(grad_two * own_two)
    grads = jnp.concatenate([grad_one, grad_two, sum_one, sum_two], axis=0).astype(BF16)

    def backward(item, opening):
        row = item_row(starts, item, begin, tile)
        masked = (soft_vals * row).astype(BF16)
        acc_ref[item] += dot_nt(grads, masked)
        fresh = row * dot_nn(back_ref[item], grads)
        pull_ref[...] = fresh if opening else pull_ref[...] + fresh

    over_items(starts, items, begin, tile, backward)
    pull = pull_ref[...]
    grad_query = (soft * (pull - head_sum(pull * soft))).astype(BF16)
    g_query_ref[...] += dot_nt(norm_ref[...], grad_query)
    grad_norm_one = dot_nn(query_ref[...], grad_query)
    unit_one = unit_ref[...]
    g_vec_ref[0] += fold_lanes(grad_norm_one * unit_one)
    g_vec_ref[1] += fold_lanes(grad_norm_one)
    grad_token = grad_residual + norm_back(
        grad_norm_one * column(cols, COL_GAIN_ONE, tile), unit_one, scale_ref[0:1, :]
    )
    grad_ref[...] = jnp.transpose(grad_token)

    @pl.when(step == steps - 1)
    def _():
        mask = head_mask()
        for slot, target in enumerate((own_msg_ref, other_msg_ref)):
            target[items * HD :, :] = jnp.zeros((target.shape[0] - items * HD, LANES), F32)
            for item in range(items):
                full = acc_ref[item, slot * D : (slot + 1) * D, :]
                target[item * HD : (item + 1) * HD, :] = fold_heads(full, mask)
                sums = acc_ref[item, (2 + slot) * D : (3 + slot) * D, :]
                target[items * HD + item : items * HD + item + 1, :] = fold_heads(sums, mask)[0:1]


def pack_kernel(
    plan,
    scal_ref,
    g_query_ref,
    g_out_ref,
    g_up_ref,
    g_down_ref,
    g_vec_ref,
    own_ref,
    other_ref,
    vec_ref,
    tmp_ref,
):
    parts, shard, half = plan
    vec_ref[SHARED_ROWS:, :] = jnp.zeros((vec_ref.shape[0] - SHARED_ROWS, LANES), F32)
    for slot, row in enumerate((ROW_GAIN_ONE, ROW_SHIFT_ONE, ROW_GAIN_TWO, ROW_SHIFT_TWO)):
        vec_ref[row : row + 1, :] = lane_total_row(g_vec_ref[slot])
    vec_ref[ROW_QUERY : ROW_QUERY + D, :] = g_query_ref[...]
    vec_ref[ROW_OUT : ROW_OUT + D + 1, :] = g_out_ref[: D + 1, :]
    for expert in range(E):
        for part in range(2):
            columns = slice(part * D, (part + 1) * D)
            vec_ref[pl.ds(ROW_UP + expert * 2 * D + part, D, stride=2), :] = g_up_ref[
                expert, :D, columns
            ]
            row = ROW_UP_B + 2 * expert + part
            vec_ref[row : row + 1, :] = g_up_ref[expert, D : D + 1, columns]
        row = ROW_DOWN + expert * FF
        vec_ref[row : row + FF, :] = g_down_ref[expert, :FF, :]
        row = ROW_DOWN_B + expert
        vec_ref[row : row + 1, :] = g_down_ref[expert, FF : FF + 1, :]
    core = scal_ref[0]
    own_at = pl.multiple_of(core * half, 8)
    other_at = pl.multiple_of((1 - core) * half, 8)
    for number in range(parts):
        tmp_ref[...] = take_shard(vec_ref, number, shard, 2 * half)
        own_ref[number] = tmp_ref[pl.ds(own_at, half), :]
        other_ref[number] = tmp_ref[pl.ds(other_at, half), :].astype(BF16)


def sample_backward_kernel(
    plan,
    scal_ref,
    count_ref,
    msg_ref,
    func_ref,
    keys_ref,
    vals_ref,
    first_ref,
    second_ref,
    slope_one_ref,
    slope_two_ref,
    hid_ref,
    pair_ref,
    own_ref,
    other_ref,
    out_own_ref,
    out_other_ref,
    grad_own_ref,
    grad_other_ref,
    send_ref,
    out_ref,
    grad_ref,
    vec_ref,
    left_keys_ref,
    left_vals_ref,
    shift_ref,
    keys_acc_ref,
    vals_acc_ref,
    g_pair_ref,
    g_hid_ref,
    g_in_ref,
    starts,
):
    tile, items, parts, shard, height, slots, steps = plan
    step = pl.program_id(0)
    core = scal_ref[0]
    out_ref[core] = out_own_ref[...]
    out_ref[1 - core] = out_other_ref[...]
    grad_ref[core] = grad_own_ref[...]
    grad_ref[1 - core] = grad_other_ref[...]

    @pl.when(step == 0)
    def _():
        store_starts(lambda item: count_ref[0, item], starts, items)
        g_pair_ref[...] = jnp.zeros(g_pair_ref.shape, F32)
        g_hid_ref[...] = jnp.zeros(g_hid_ref.shape, F32)
        g_in_ref[...] = jnp.zeros(g_in_ref.shape, F32)
        mask = head_mask()
        low, high = item_span(
            starts, items, scal_ref[1] * slots, scal_ref[1] * slots + tile * steps
        )

        def build(item, carry):
            at = pl.multiple_of(item * HD, HD)
            block = spread_heads(msg_ref[pl.ds(at, HD), :], mask)
            left_vals_ref[item] = block.astype(BF16)
            left_keys_ref[item] = jnp.transpose(block).astype(BF16)
            row = msg_ref[pl.ds(items * HD + item, 1), :]
            shift_ref[item] = jnp.transpose(jnp.broadcast_to(row, (D, D)))
            return carry

        @pl.when(high <= low)
        def _():
            last = items - 1
            left_vals_ref[last] = jnp.zeros((D, D), BF16)
            left_keys_ref[last] = jnp.zeros((D, D), BF16)
            shift_ref[last] = jnp.zeros((D, D), F32)

        lax.fori_loop(low, high, build, 0)

    keys = keys_ref[...]
    vals = vals_ref[...]
    begin = scal_ref[1] * slots + step * tile

    def visit(item, opening):
        row = item_row(starts, item, begin, tile)
        fresh_keys = row * (dot_nn(left_keys_ref[item], vals) + wide(shift_ref[item], tile))
        fresh_vals = row * dot_nn(left_vals_ref[item], keys)
        keys_acc_ref[...] = fresh_keys if opening else keys_acc_ref[...] + fresh_keys
        vals_acc_ref[...] = fresh_vals if opening else vals_acc_ref[...] + fresh_vals

    over_items(starts, items, begin, tile, visit)
    soft = keys.astype(F32)
    grad_keys = keys_acc_ref[...]
    grad_in = soft * (grad_keys - head_sum(grad_keys * soft))
    grad_pair = jnp.concatenate([grad_in, vals_acc_ref[...]], axis=0).astype(BF16)
    g_pair_ref[...] += dot_nt(second_ref[...], grad_pair)
    grad_second = (slope_two_ref[...].astype(F32) * dot_nn(pair_ref[...], grad_pair)).astype(BF16)
    first_ones = jnp.concatenate([first_ref[...], jnp.ones((16, tile), BF16)], axis=0)
    g_hid_ref[...] += dot_nt(first_ones, grad_second)
    grad_first = slope_one_ref[...].astype(F32) * dot_nn(hid_ref[...], grad_second)
    funcs = func_ref[0]
    for part in range(FIN):
        g_in_ref[part] += fold_lanes(grad_first * funcs[part : part + 1, :])
    g_in_ref[FIN] += fold_lanes(grad_first)

    @pl.when(step == steps - 1)
    def _():
        vec_ref[BRANCH_ROWS:, :] = jnp.zeros((vec_ref.shape[0] - BRANCH_ROWS, LANES), F32)
        for part in range(FIN + 1):
            vec_ref[part : part + 1, :] = lane_total_row(g_in_ref[part])
        vec_ref[ROW_HID : ROW_HID + D + 1, :] = g_hid_ref[: D + 1, :]
        for part in range(2):
            vec_ref[pl.ds(ROW_PAIR + part, D, stride=2), :] = g_pair_ref[
                :, part * D : (part + 1) * D
            ]
        for number in range(parts):
            send_ref[number, :height, :] = take_shard(vec_ref, number, shard, height).astype(BF16)
            send_ref[number, height:, :] = (
                own_ref[number] + other_ref[number].astype(F32)
            ).astype(BF16)


def sum_over_points(values, count):
    bit = 1
    while bit < count:
        masks = [bit] if 2 * bit >= count else [bit, 2 * bit, 3 * bit]
        pieces = [
            lax.ppermute(values, "pts", [(source, source ^ mask) for source in range(count)])
            for mask in masks
        ]
        values = functools.reduce(jnp.add, pieces, values)
        bit *= 4
    return values


def swap_cores(values):
    return lax.ppermute(values, "branch", [(0, 1), (1, 0)])


def whole(shape, kind=None):
    zeros = (0,) * len(shape)
    return pl.BlockSpec(shape, lambda *_: zeros)


def body(
    tokens,
    funcs,
    item_counts,
    func_counts,
    gate_ints,
    cotangent,
    shared_master,
    shared_m,
    shared_v,
    branch_master,
    branch_m,
    branch_v,
):
    count = lax.axis_size("pts")
    core = lax.axis_index("branch")
    scal = jnp.stack([core, lax.axis_index("pts")]).astype(jnp.int32)
    items = item_counts.shape[0]
    chip_rows = tokens.shape[0]
    rows = chip_rows // 2
    slots = funcs.shape[2]
    shared_len = shared_master.shape[0]
    branch_len = branch_master.shape[1]
    half = up_to(-(-shared_len // (2 * LANES)), 16)
    height = up_to(-(-branch_len // LANES), 16)
    msg_rows = items * HD + up_to(items, 8)
    params = pltpu.CompilerParams(vmem_limit_bytes=VMEM_LIMIT)
    shape = jax.ShapeDtypeStruct

    shared_pad = jnp.pad(shared_master.astype(BF16), (0, 2 * half * LANES - shared_len))
    shared_half = lax.dynamic_slice_in_dim(shared_pad, core * (half * LANES), half * LANES, 0)
    branch_pad = jnp.pad(
        branch_master.reshape(-1).astype(BF16), (0, height * LANES - branch_len)
    )
    send = jnp.concatenate([branch_pad, shared_half]).reshape(1, height + half, LANES)
    send = jnp.broadcast_to(send, (count, height + half, LANES))
    recv = lax.all_to_all(send, "pts", 0, 0)
    recv_other = swap_cores(recv)

    tile = min(SAMPLE_TILE, slots)
    steps = slots // tile
    stream = lambda height_: pl.BlockSpec((height_, tile), lambda i, *_: (0, i))
    vec_rows = up_to(BRANCH_ROWS + 2 * height + 8, 8)
    (
        msg,
        keys,
        vals,
        first,
        second,
        slope_one,
        slope_two,
        hid_w,
        pair_w,
    ) = pl.pallas_call(
        functools.partial(
            sample_forward_kernel, (tile, items, count, branch_len, height, slots)
        ),
        grid_spec=pltpu.PrefetchScalarGridSpec(
            num_scalar_prefetch=1,
            grid=(steps,),
            in_specs=[
                pl.BlockSpec(memory_space=pltpu.SMEM),
                pl.BlockSpec((count, height, LANES), lambda i, *_: (0, 0, 0)),
                pl.BlockSpec((1, FIN, tile), lambda i, *_: (0, 0, i)),
            ],
            out_specs=[
                whole((msg_rows, LANES)),
                stream(D),
                stream(D),
                stream(D),
                stream(D),
                stream(D),
                stream(D),
                whole((D, D)),
                whole((D, 2 * D)),
            ],
            scratch_shapes=[
                pltpu.VMEM((vec_rows, LANES), F32),
                pltpu.VMEM((8 + 2 * height, LANES), F32),
                pltpu.VMEM((5, D, D), F32),
                pltpu.VMEM((D, D), BF16),
                pltpu.VMEM((2 * D, D), BF16),
                pltpu.VMEM((items, D + 16, D), F32),
                pltpu.SMEM((items + 1,), jnp.int32),
            ],
        ),
        out_shape=[
            shape((msg_rows, LANES), F32),
            shape((D, slots), BF16),
            shape((D, slots), BF16),
            shape((D, slots), BF16),
            shape((D, slots), BF16),
            shape((D, slots), BF16),
            shape((D, slots), BF16),
            shape((D, D), BF16),
            shape((D, 2 * D), BF16),
        ],
        compiler_params=params,
        cost_estimate=pl.CostEstimate(
            flops=slots * D * D * 10, bytes_accessed=slots * D * 12, transcendentals=slots * D * 3
        ),
        name="sample_forward",
    )(scal, func_counts, recv, funcs)

    summary = sum_over_points(msg, count)
    summary_other = swap_cores(summary)

    shared_rows = up_to(SHARED_ROWS + 2 * half + 8, 8)
    (query_w, query_t, out_w, out_t, up_w, up_t, down_w, down_t, cols) = pl.pallas_call(
        functools.partial(weight_kernel, (count, shared_len, half, height)),
        in_specs=[
            pl.BlockSpec(memory_space=pltpu.SMEM),
            whole(recv.shape),
            whole(recv.shape),
        ],
        out_specs=[
            whole((D, D)),
            whole((D, D)),
            whole((D, D)),
            whole((D, D)),
            whole((E, D, FF)),
            whole((E, FF, D)),
            whole((E, FF, D)),
            whole((E, D, FF)),
            whole((D, D)),
        ],
        out_shape=[
            shape((D, D), BF16),
            shape((D, D), BF16),
            shape((D, D), BF16),
            shape((D, D), BF16),
            shape((E, D, FF), BF16),
            shape((E, FF, D), BF16),
            shape((E, FF, D), BF16),
            shape((E, D, FF), BF16),
            shape((D, D), F32),
        ],
        scratch_shapes=[
            pltpu.VMEM((shared_rows, LANES), F32),
            pltpu.VMEM((max(8 + 2 * half, D) + 8, LANES), F32),
        ],
        compiler_params=params,
        cost_estimate=pl.CostEstimate(flops=0, bytes_accessed=8 << 20, transcendentals=0),
        name="weights",
    )(scal, recv, recv_other)

    token_tile = min(TOKEN_TILE, rows)
    token_steps = rows // token_tile
    row_block = pl.BlockSpec(
        (token_tile, D), lambda i, scal_ref: (scal_ref[0] * token_steps + i, 0)
    )
    token_stream = lambda height_: pl.BlockSpec((height_, token_tile), lambda i, *_: (0, i))
    (token_t, cot_t, unit, scale, norm, soft) = pl.pallas_call(
        query_kernel,
        grid_spec=pltpu.PrefetchScalarGridSpec(
            num_scalar_prefetch=1,
            grid=(token_steps,),
            in_specs=[row_block, row_block, whole((D, D)), whole((D, D))],
            out_specs=[
                token_stream(D),
                token_stream(D),
                token_stream(D),
                token_stream(8),
                token_stream(D),
                token_stream(D),
            ],
        ),
        out_shape=[
            shape((D, rows), BF16),
            shape((D, rows), F32),
            shape((D, rows), F32),
            shape((8, rows), F32),
            shape((D, rows), BF16),
            shape((D, rows), F32),
        ],
        compiler_params=params,
        cost_estimate=pl.CostEstimate(
            flops=rows * D * D * 2, bytes_accessed=rows * D * 24, transcendentals=rows * D
        ),
        name="queries",
    )(scal, tokens, cotangent, query_t, cols)

    (
        output_own,
        grad_own,
        own_msg,
        other_msg,
        g_query,
        g_out,
        g_up,
        g_down,
        g_vec,
    ) = pl.pallas_call(
        functools.partial(token_kernel, (token_tile, items, chip_rows, token_steps)),
        grid_spec=pltpu.PrefetchScalarGridSpec(
            num_scalar_prefetch=1,
            grid=(token_steps,),
            in_specs=[
                pl.BlockSpec(memory_space=pltpu.SMEM),
                whole((msg_rows, LANES)),
                whole((msg_rows, LANES)),
                pl.BlockSpec((E, token_tile), lambda i, scal_ref: (0, scal_ref[0] * token_steps + i)),
                token_stream(D),
                token_stream(D),
                token_stream(D),
                token_stream(8),
                token_stream(D),
                token_stream(D),
                whole((D, D)),
                whole((D, D)),
                whole((D, D)),
                whole((E, D, FF)),
                whole((E, FF, D)),
                whole((E, FF, D)),
                whole((E, D, FF)),
                whole((D, D)),
            ],
            out_specs=[
                pl.BlockSpec((token_tile, D), lambda i, *_: (i, 0)),
                pl.BlockSpec((token_tile, D), lambda i, *_: (i, 0)),
                whole((msg_rows, LANES)),
                whole((msg_rows, LANES)),
                whole((D, D)),
                whole((D + 16, D)),
                whole((E, D + 16, FF)),
                whole((E, FF + 16, D)),
                whole((4, D, D)),
            ],
            scratch_shapes=[
                pltpu.VMEM((items, 4 * D, 2 * D), BF16),
                pltpu.VMEM((items, D, 4 * D), BF16),
                pltpu.VMEM((items, 4 * D, D), F32),
                pltpu.VMEM((4 * D, token_tile), F32),
                pltpu.VMEM((D, token_tile), F32),
                pltpu.SMEM((items + 1,), jnp.int32),
            ],
        ),
        out_shape=[
            shape((rows, D), BF16),
            shape((rows, D), F32),
            shape((msg_rows, LANES), F32),
            shape((msg_rows, LANES), F32),
            shape((D, D), F32),
            shape((D + 16, D), F32),
            shape((E, D + 16, FF), F32),
            shape((E, FF + 16, D), F32),
            shape((4, D, D), F32),
        ],
        compiler_params=params,
        cost_estimate=pl.CostEstimate(
            flops=rows * D * FF * 12 * E, bytes_accessed=rows * D * 24, transcendentals=rows * FF * E
        ),
        name="tokens",
    )(
        scal,
        item_counts,
        summary,
        summary_other,
        gate_ints.T,
        token_t,
        cot_t,
        unit,
        scale,
        norm,
        soft,
        query_w,
        out_w,
        out_t,
        up_w,
        up_t,
        down_w,
        down_t,
        cols,
    )

    summary_grad = sum_over_points(own_msg + swap_cores(other_msg), count)
    output_other = swap_cores(output_own)
    grad_other = swap_cores(grad_own)

    half_own, half_other = pl.pallas_call(
        functools.partial(pack_kernel, (count, shared_len, half)),
        in_specs=[pl.BlockSpec(memory_space=pltpu.SMEM)]
        + [whole(piece.shape) for piece in (g_query, g_out, g_up, g_down, g_vec)],
        out_specs=[whole((count, half, LANES)), whole((count, half, LANES))],
        out_shape=[shape((count, half, LANES), F32), shape((count, half, LANES), BF16)],
        scratch_shapes=[
            pltpu.VMEM((shared_rows, LANES), F32),
            pltpu.VMEM((2 * half, LANES), F32),
        ],
        compiler_params=params,
        cost_estimate=pl.CostEstimate(flops=0, bytes_accessed=4 << 20, transcendentals=0),
        name="pack",
    )(scal, g_query, g_out, g_up, g_down, g_vec)
    half_other = swap_cores(half_other)

    piece = pl.BlockSpec((rows // steps, D), lambda i, *_: (i, 0))
    both = pl.BlockSpec((2, rows // steps, D), lambda i, *_: (0, i, 0))
    grads_send, output, token_grad = pl.pallas_call(
        functools.partial(
            sample_backward_kernel,
            (tile, items, count, branch_len, height, slots, steps),
        ),
        grid_spec=pltpu.PrefetchScalarGridSpec(
            num_scalar_prefetch=1,
            grid=(steps,),
            in_specs=[
                pl.BlockSpec(memory_space=pltpu.SMEM),
                whole((msg_rows, LANES)),
                pl.BlockSpec((1, FIN, tile), lambda i, *_: (0, 0, i)),
                stream(D),
                stream(D),
                stream(D),
                stream(D),
                stream(D),
                stream(D),
                whole((D, D)),
                whole((D, 2 * D)),
                whole((count, half, LANES)),
                whole((count, half, LANES)),
                piece,
                piece,
                piece,
                piece,
            ],
            out_specs=[whole((count, height + half, LANES)), both, both],
            scratch_shapes=[
                pltpu.VMEM((vec_rows, LANES), F32),
                pltpu.VMEM((items, D, D), BF16),
                pltpu.VMEM((items, D, D), BF16),
                pltpu.VMEM((items, D, D), F32),
                pltpu.VMEM((D, tile), F32),
                pltpu.VMEM((D, tile), F32),
                pltpu.VMEM((D, 2 * D), F32),
                pltpu.VMEM((D + 16, D), F32),
                pltpu.VMEM((FIN + 1, D, D), F32),
                pltpu.SMEM((items + 1,), jnp.int32),
            ],
        ),
        out_shape=[
            shape((count, height + half, LANES), BF16),
            shape((2, rows, D), BF16),
            shape((2, rows, D), F32),
        ],
        compiler_params=params,
        cost_estimate=pl.CostEstimate(
            flops=slots * D * D * 16, bytes_accessed=slots * D * 12, transcendentals=0
        ),
        name="sample_backward",
    )(
        scal,
        func_counts,
        summary_grad,
        funcs,
        keys,
        vals,
        first,
        second,
        slope_one,
        slope_two,
        hid_w,
        pair_w,
        half_own,
        half_other,
        output_own,
        output_other,
        grad_own,
        grad_other,
    )

    grads = jnp.sum(lax.all_to_all(grads_send, "pts", 0, 0).astype(F32), axis=0)
    own_half = grads[height:].reshape(-1)
    other_half = swap_cores(own_half)
    shared_grad = jnp.where(
        core == 0,
        jnp.concatenate([own_half, other_half]),
        jnp.concatenate([other_half, own_half]),
    )[:shared_len]
    branch_grad = grads[:height].reshape(1, -1)[:, :branch_len]
    new_branch, new_branch_m, new_branch_v = adam_step(
        branch_master, branch_m, branch_v, branch_grad
    )
    new_shared, new_shared_m, new_shared_v = adam_step(
        shared_master, shared_m, shared_v, shared_grad
    )
    return (
        output.reshape(chip_rows, D),
        token_grad.reshape(chip_rows, D),
        new_shared,
        new_shared_m,
        new_shared_v,
        new_branch,
        new_branch_m,
        new_branch_v,
    )


def solution(mesh):
    in_specs = (
        P("pts", None),
        P("branch", None, "pts"),
        P(),
        P("branch", None),
        P("pts", None),
        P("pts", None),
        P("pts"),
        P("pts"),
        P("pts"),
        P("branch", "pts"),
        P("branch", "pts"),
        P("branch", "pts"),
    )
    out_specs = (
        P("pts", None),
        P("pts", None),
        P("pts"),
        P("pts"),
        P("pts"),
        P("branch", "pts"),
        P("branch", "pts"),
        P("branch", "pts"),
    )
    return jax.shard_map(body, mesh=mesh, in_specs=in_specs, out_specs=out_specs, check_vma=False)
```

```python
import functools
import math

import jax
import jax.numpy as jnp
from jax import lax
from jax.experimental import pallas as pl
from jax.experimental.pallas import tpu as pltpu
from jax.sharding import PartitionSpec as P

D = 128
H = 8
HD = 16
FF = 256
E = 4
FIN = 3
STEP = 10

EPS_NORM = 1e-05
BETA_ONE = 0.9
BETA_TWO = 0.999
RATE_LEARN = 0.1
DECAY_RATE = 0.01
EPS_ADAM = 1e-08

LANES = 128
VMEM_BASE = 15 * 1024 * 1024
VMEM_ITEM = 768 * 1024
SAMPLE_TILE = 1024
TOKEN_TILE = 1024

F32 = jnp.float32
BF16 = jnp.bfloat16

ROW_GAIN_ONE = 0
ROW_SHIFT_ONE = 1
ROW_QUERY = 2
ROW_OUT = ROW_QUERY + D
ROW_OUT_B = ROW_OUT + D
ROW_GAIN_TWO = ROW_OUT_B + 1
ROW_SHIFT_TWO = ROW_GAIN_TWO + 1
ROW_UP = ROW_SHIFT_TWO + 1
ROW_UP_B = ROW_UP + E * D * 2
ROW_DOWN = ROW_UP_B + E * 2
ROW_DOWN_B = ROW_DOWN + E * FF
SHARED_ROWS = ROW_DOWN_B + E

ROW_IN = 0
ROW_IN_B = ROW_IN + FIN
ROW_HID = ROW_IN_B + 1
ROW_HID_B = ROW_HID + D
ROW_PAIR = ROW_HID_B + 1
BRANCH_ROWS = ROW_PAIR + 2 * D

COL_GAIN_ONE = 0
COL_SHIFT_ONE = 1
COL_OUT_B = 2
COL_GAIN_TWO = 3
COL_SHIFT_TWO = 4
COL_UP_B = 5
COL_DOWN_B = COL_UP_B + 2 * E

TANH_C = math.sqrt(2.0 / math.pi)
TANH_CUBE = 0.044715


def up_to(amount, unit):
    return -(-amount // unit) * unit


def adam_step(master, moment_one, moment_two, grad):
    first = BETA_ONE * moment_one + (1.0 - BETA_ONE) * grad
    second = BETA_TWO * moment_two + (1.0 - BETA_TWO) * grad * grad
    first_hat = first / (1.0 - BETA_ONE**STEP)
    second_hat = second / (1.0 - BETA_TWO**STEP)
    fresh = master - RATE_LEARN * (
        first_hat / (jnp.sqrt(second_hat) + EPS_ADAM) + DECAY_RATE * master
    )
    return (fresh, first, second)


def dot_nn(left, right):
    return jnp.dot(left, right, preferred_element_type=F32)


def dot_nt(left, right):
    return lax.dot_general(left, right, (((1,), (1,)), ((), ())), preferred_element_type=F32)


def head_sum(values):
    split = values.reshape(H, HD, values.shape[1])
    total = jnp.sum(split, axis=1, keepdims=True)
    return jnp.broadcast_to(total, split.shape).reshape(values.shape)


def head_softmax(values):
    split = values.reshape(H, HD, values.shape[1])
    top = jnp.max(split, axis=1, keepdims=True)
    raised = jnp.exp(split - top)
    total = jnp.sum(raised, axis=1, keepdims=True)
    return (raised * (1.0 / total)).reshape(values.shape)


def gelu_parts(inner):
    square = inner * inner
    bend = TANH_C + (TANH_C * TANH_CUBE) * square
    curve = jnp.tanh(inner * bend)
    gate = 0.5 + 0.5 * curve
    slope = (TANH_C) + (3.0 * TANH_C * TANH_CUBE) * square
    grad = gate + inner * (0.5 - 0.5 * curve * curve) * slope
    return inner * gate, grad


def wide(tile, length):
    if length == tile.shape[1]:
        return tile
    return jnp.concatenate([tile] * (length // tile.shape[1]), axis=1)


def column(matrix, index, length):
    return jnp.broadcast_to(matrix[:, index : index + 1], (matrix.shape[0], length))


def fold_lanes(values):
    total = values[:, :LANES]
    for start in range(LANES, values.shape[1], LANES):
        total = total + values[:, start : start + LANES]
    return total


def lane_total_row(values):
    return jnp.sum(jnp.transpose(values), axis=0, keepdims=True)


def head_mask():
    row = lax.broadcasted_iota(jnp.int32, (D, D), 0) // HD
    col = lax.broadcasted_iota(jnp.int32, (D, D), 1) // HD
    return (row == col).astype(F32)


def fold_heads(values, mask):
    return jnp.sum((values * mask).reshape(H, HD, D), axis=0)


def spread_heads(compact, mask):
    return jnp.concatenate([compact] * H, axis=0) * mask


def store_starts(counts, starts, items):
    if items <= 8:
        total = jnp.int32(0)
        for item in range(items):
            starts[item] = total
            total = total + counts(item)
        starts[items] = total
    else:
        def step(item, total):
            starts[item] = total
            return total + counts(item)

        starts[items] = lax.fori_loop(0, items, step, jnp.int32(0))


def item_span(starts, items, begin, end):
    def step(item, span):
        low, high = span
        return (
            low + (starts[item + 1] <= begin).astype(jnp.int32),
            high + (starts[item] < end).astype(jnp.int32),
        )

    span = (jnp.int32(0), jnp.int32(0))
    if items <= 8:
        for item in range(items):
            span = step(item, span)
        return span
    return lax.fori_loop(0, items, step, span)


def item_row(starts, item, begin, length):
    position = begin + lax.broadcasted_iota(jnp.int32, (1, length), 1)
    return ((position >= starts[item]) & (position < starts[item + 1])).astype(F32)


def over_items(starts, items, begin, length, visit):
    low, high = item_span(starts, items, begin, begin + length)
    visit(jnp.minimum(low, items - 1), True)

    def step(item, carry):
        visit(item, False)
        return carry

    lax.fori_loop(low + 1, high, step, 0)


def put_shard(vec_ref, tmp_ref, number, shard, height):
    row, shift = divmod(number * shard, LANES)
    touched = (shift + shard - 1) // LANES + 1
    if shift == 0:
        vec_ref[row : row + touched, :] = tmp_ref[8 : 8 + touched, :]
        return
    if number == 0:
        tmp_ref[7:8, :] = jnp.zeros((1, LANES), F32)
    else:
        tmp_ref[7:8, :] = vec_ref[row : row + 1, :]
    lane = lax.broadcasted_iota(jnp.int32, (touched, LANES), 1)
    vec_ref[row : row + touched, :] = jnp.where(
        lane >= shift, tmp_ref[8 : 8 + touched, :], tmp_ref[7 : 7 + touched, :]
    )


def turned(block, amount):
    amount = amount % LANES
    return block if amount == 0 else pltpu.roll(block, amount, 1)


def take_shard(vec_ref, number, shard, height):
    row, shift = divmod(number * shard, LANES)
    here = vec_ref[row : row + height, :]
    if shift == 0:
        return here
    after = vec_ref[row + 1 : row + 1 + height, :]
    lane = lax.broadcasted_iota(jnp.int32, (height, LANES), 1)
    return turned(jnp.where(lane >= shift, here, after), LANES - shift)


def sample_forward_kernel(
    plan,
    scal_ref,
    count_ref,
    recv_ref,
    func_ref,
    msg_ref,
    keys_ref,
    vals_ref,
    first_ref,
    second_ref,
    slope_one_ref,
    slope_two_ref,
    hid_ref,
    pair_ref,
    vec_ref,
    tmp_ref,
    col_ref,
    hid_t_ref,
    pair_t_ref,
    acc_ref,
    starts,
):
    tile, items, parts, shard, height, slots = plan
    step = pl.program_id(0)

    @pl.when(step == 0)
    def _():
        store_starts(lambda item: count_ref[0, item], starts, items)
        acc_ref[...] = jnp.zeros(acc_ref.shape, F32)
        for number in range(parts):
            shift = (number * shard) % LANES
            tmp_ref[8 : 8 + height, :] = turned(recv_ref[number].astype(F32), shift)
            put_shard(vec_ref, tmp_ref, number, shard, height)
        for slot, row in enumerate((0, 1, 2, ROW_IN_B, ROW_HID_B)):
            col_ref[slot] = jnp.transpose(
                jnp.broadcast_to(vec_ref[row : row + 1, :], (D, D))
            )
        hid = vec_ref[ROW_HID : ROW_HID + D, :]
        hid_ref[...] = hid.astype(BF16)
        hid_t_ref[...] = jnp.transpose(hid).astype(BF16)
        for part in range(2):
            piece = vec_ref[pl.ds(ROW_PAIR + part, D, stride=2), :]
            pair_ref[:, part * D : (part + 1) * D] = piece.astype(BF16)
            pair_t_ref[part * D : (part + 1) * D, :] = jnp.transpose(piece).astype(BF16)

    funcs = func_ref[0]
    first_in = wide(col_ref[3], tile)
    for part in range(FIN):
        first_in = first_in + wide(col_ref[part], tile) * funcs[part : part + 1, :]
    first, slope_one = gelu_parts(first_in)
    first = first.astype(BF16)
    first_ref[...] = first
    slope_one_ref[...] = slope_one.astype(slope_one_ref.dtype)
    second_in = dot_nn(hid_t_ref[...], first) + wide(col_ref[4], tile)
    second, slope_two = gelu_parts(second_in)
    second = second.astype(BF16)
    second_ref[...] = second
    slope_two_ref[...] = slope_two.astype(slope_two_ref.dtype)
    pair = dot_nn(pair_t_ref[...], second)
    keys = head_softmax(pair[:D])
    keys_ref[...] = keys.astype(BF16)
    vals = pair[D:].astype(BF16)
    vals_ref[...] = vals
    vals_ones = jnp.concatenate([vals, jnp.ones((16, tile), BF16)], axis=0)
    begin = scal_ref[1] * slots + step * tile

    def visit(item, _):
        masked = (keys * item_row(starts, item, begin, tile)).astype(BF16)
        acc_ref[item] += dot_nt(vals_ones, masked)

    over_items(starts, items, begin, tile, visit)

    @pl.when(step == pl.num_programs(0) - 1)
    def _():
        mask = head_mask()
        msg_ref[items * HD :, :] = jnp.zeros((msg_ref.shape[0] - items * HD, LANES), F32)
        for item in range(items):
            msg_ref[item * HD : (item + 1) * HD, :] = fold_heads(acc_ref[item, :D, :], mask)
            msg_ref[items * HD + item : items * HD + item + 1, :] = acc_ref[item, D : D + 1, :]


def weight_kernel(
    plan,
    scal_ref,
    own_ref,
    other_ref,
    query_ref,
    query_t_ref,
    out_ref,
    out_t_ref,
    up_ref,
    up_t_ref,
    down_ref,
    down_t_ref,
    cols_ref,
    vec_ref,
    tmp_ref,
):
    parts, shard, half = plan
    core = scal_ref[0]
    own_at = pl.multiple_of(8 + core * half, 8)
    other_at = pl.multiple_of(8 + (1 - core) * half, 8)
    for number in range(parts):
        shift = (number * shard) % LANES
        tmp_ref[pl.ds(own_at, half), :] = turned(
            own_ref[number].astype(F32), shift
        )
        tmp_ref[pl.ds(other_at, half), :] = turned(
            other_ref[number].astype(F32), shift
        )
        put_shard(vec_ref, tmp_ref, number, shard, 2 * half)
    query = vec_ref[ROW_QUERY : ROW_QUERY + D, :]
    query_ref[...] = query.astype(BF16)
    query_t_ref[...] = jnp.transpose(query).astype(BF16)
    out = vec_ref[ROW_OUT : ROW_OUT + D, :]
    out_ref[...] = out.astype(BF16)
    out_t_ref[...] = jnp.transpose(out).astype(BF16)
    for expert in range(E):
        for part in range(2):
            up = vec_ref[pl.ds(ROW_UP + expert * 2 * D + part, D, stride=2), :]
            up_ref[expert, :, part * D : (part + 1) * D] = up.astype(BF16)
            up_t_ref[expert, part * D : (part + 1) * D, :] = jnp.transpose(up).astype(BF16)
            row = ROW_DOWN + expert * FF + part * D
            down = vec_ref[row : row + D, :]
            down_ref[expert, part * D : (part + 1) * D, :] = down.astype(BF16)
            down_t_ref[expert, :, part * D : (part + 1) * D] = jnp.transpose(down).astype(BF16)
    tmp_ref[0:D, :] = jnp.zeros((D, LANES), F32)
    rows = [ROW_GAIN_ONE, ROW_SHIFT_ONE, ROW_OUT_B, ROW_GAIN_TWO, ROW_SHIFT_TWO]
    rows += [ROW_UP_B + number for number in range(2 * E)]
    rows += [ROW_DOWN_B + number for number in range(E)]
    for slot, row in enumerate(rows):
        tmp_ref[slot : slot + 1, :] = vec_ref[row : row + 1, :]
    cols_ref[...] = jnp.transpose(tmp_ref[0:D, :])


def norm_unit(values):
    centre = values - jnp.sum(values, axis=0, keepdims=True) * (1.0 / D)
    spread = jnp.sum(centre * centre, axis=0, keepdims=True) * (1.0 / D)
    scale = lax.rsqrt(spread + EPS_NORM)
    return centre * scale, scale


def norm_back(grad_unit, unit, scale):
    mean_one = jnp.sum(grad_unit, axis=0, keepdims=True) * (1.0 / D)
    mean_two = jnp.sum(grad_unit * unit, axis=0, keepdims=True) * (1.0 / D)
    return scale * (grad_unit - mean_one - unit * mean_two)


def query_kernel(
    scal_ref,
    token_ref,
    cot_ref,
    query_t_ref,
    cols_ref,
    token_t_ref,
    cot_t_ref,
    unit_ref,
    scale_ref,
    norm_ref,
    soft_ref,
):
    tokens = jnp.transpose(token_ref[...].astype(F32))
    length = tokens.shape[1]
    token_t_ref[...] = tokens.astype(BF16)
    cot_t_ref[...] = jnp.transpose(cot_ref[...])
    unit, scale = norm_unit(tokens)
    unit_ref[...] = unit
    scale_ref[...] = jnp.broadcast_to(scale, scale_ref.shape)
    cols = cols_ref[...]
    norm = (unit * column(cols, COL_GAIN_ONE, length) + column(cols, COL_SHIFT_ONE, length)).astype(
        BF16
    )
    norm_ref[...] = norm
    soft_ref[...] = head_softmax(dot_nn(query_t_ref[...], norm))


def token_kernel(
    plan,
    scal_ref,
    count_ref,
    own_ref,
    other_ref,
    gate_ref,
    token_t_ref,
    cot_t_ref,
    unit_ref,
    scale_ref,
    norm_ref,
    soft_ref,
    query_ref,
    out_w_ref,
    out_t_ref,
    up_ref,
    up_t_ref,
    down_ref,
    down_t_ref,
    cols_ref,
    output_ref,
    grad_ref,
    own_msg_ref,
    other_msg_ref,
    g_query_ref,
    g_out_ref,
    g_up_ref,
    g_down_ref,
    g_vec_ref,
    left_ref,
    back_ref,
    acc_ref,
    mix_ref,
    pull_ref,
    starts,
):
    tile, items, slots, steps = plan
    step = pl.program_id(0)
    first_row = scal_ref[1] * slots + scal_ref[0] * (tile * steps)

    @pl.when(step == 0)
    def _():
        store_starts(lambda item: count_ref[item], starts, items)
        acc_ref[...] = jnp.zeros(acc_ref.shape, F32)
        g_query_ref[...] = jnp.zeros(g_query_ref.shape, F32)
        g_out_ref[...] = jnp.zeros(g_out_ref.shape, F32)
        g_up_ref[...] = jnp.zeros(g_up_ref.shape, F32)
        g_down_ref[...] = jnp.zeros(g_down_ref.shape, F32)
        g_vec_ref[...] = jnp.zeros(g_vec_ref.shape, F32)
        mask = head_mask()
        low, high = item_span(starts, items, first_row, first_row + tile * steps)

        def build(item, carry):
            at = pl.multiple_of(item * HD, HD)
            for slot, source in enumerate((own_ref, other_ref)):
                block = spread_heads(source[pl.ds(at, HD), :], mask)
                total = source[pl.ds(items * HD + item, 1), :] * mask
                for kind, piece in enumerate((block, total)):
                    row = (2 * kind + slot) * D
                    high_part = piece.astype(BF16)
                    left_ref[item, row : row + D, :D] = high_part
                    left_ref[item, row : row + D, D:] = (piece - high_part.astype(F32)).astype(BF16)
                    turned_piece = jnp.transpose(piece)
                    if kind == 1:
                        turned_piece = turned_piece * (1.0 / HD)
                    back_ref[item, :, row : row + D] = turned_piece.astype(BF16)
            return carry

        lax.fori_loop(low, high, build, 0)

    cols = cols_ref[...]
    begin = first_row + step * tile
    soft = soft_ref[...]
    soft_low = soft.astype(BF16)
    soft_vals = soft_low.astype(F32)

    def forward(item, opening):
        masked = (soft_vals * item_row(starts, item, begin, tile)).astype(BF16)
        fresh = dot_nn(left_ref[item], jnp.concatenate([masked, masked], axis=0))
        mix_ref[...] = fresh if opening else mix_ref[...] + fresh

    over_items(starts, items, begin, tile, forward)
    numer_one, numer_two = mix_ref[:D, :], mix_ref[D : 2 * D, :]
    inv_one, inv_two = 1.0 / mix_ref[2 * D : 3 * D, :], 1.0 / mix_ref[3 * D :, :]
    own_one, own_two = numer_one * inv_one, numer_two * inv_two
    attended = (0.5 * (own_one + own_two)).astype(BF16)
    cot = cot_t_ref[...]
    residual = (
        token_t_ref[...].astype(F32)
        + dot_nn(out_t_ref[...], attended)
        + column(cols, COL_OUT_B, tile)
    )
    unit, scale = norm_unit(residual)
    gain_two = column(cols, COL_GAIN_TWO, tile)
    norm = (unit * gain_two + column(cols, COL_SHIFT_TWO, tile)).astype(BF16)
    ones = jnp.ones((16, tile), BF16)
    norm_ones = jnp.concatenate([norm, ones], axis=0)
    gates = gate_ref[...].astype(F32)
    gates = gates / jnp.sum(gates, axis=0, keepdims=True)
    mixture = residual
    grad_norm = jnp.zeros((D, tile), F32)
    for expert in range(E):
        bias = jnp.concatenate(
            [column(cols, COL_UP_B + 2 * expert + part, tile) for part in range(2)], axis=0
        )
        inner = dot_nn(up_t_ref[expert], norm) + bias
        active, slope = gelu_parts(inner)
        active = active.astype(BF16)
        result = dot_nn(down_t_ref[expert], active) + column(cols, COL_DOWN_B + expert, tile)
        gate = gates[expert : expert + 1, :]
        mixture = mixture + gate * result
        grad_result = (gate * cot).astype(BF16)
        g_down_ref[expert] += dot_nt(jnp.concatenate([active, ones], axis=0), grad_result)
        grad_inner = (slope * dot_nn(down_ref[expert], grad_result)).astype(BF16)
        g_up_ref[expert] += dot_nt(norm_ones, grad_inner)
        grad_norm = grad_norm + dot_nn(up_ref[expert], grad_inner)
    output_ref[...] = jnp.transpose(mixture).astype(BF16)
    g_vec_ref[2] += fold_lanes(grad_norm * unit)
    g_vec_ref[3] += fold_lanes(grad_norm)
    grad_residual = cot + norm_back(grad_norm * gain_two, unit, scale)
    grad_proj = grad_residual.astype(BF16)
    g_out_ref[...] += dot_nt(jnp.concatenate([attended, ones], axis=0), grad_proj)
    grad_own = 0.5 * dot_nn(out_w_ref[...], grad_proj)
    grad_one, grad_two = grad_own * inv_one, grad_own * inv_two
    sum_one = -head_sum(grad_one * own_one)
    sum_two = -head_sum(grad_two * own_two)
    grads = jnp.concatenate([grad_one, grad_two, sum_one, sum_two], axis=0).astype(BF16)

    def backward(item, opening):
        row = item_row(starts, item, begin, tile)
        masked = (soft_vals * row).astype(BF16)
        acc_ref[item] += dot_nt(grads, masked)
        fresh = row * dot_nn(back_ref[item], grads)
        pull_ref[...] = fresh if opening else pull_ref[...] + fresh

    over_items(starts, items, begin, tile, backward)
    pull = pull_ref[...]
    grad_query = (soft * (pull - head_sum(pull * soft))).astype(BF16)
    g_query_ref[...] += dot_nt(norm_ref[...], grad_query)
    grad_norm_one = dot_nn(query_ref[...], grad_query)
    unit_one = unit_ref[...]
    g_vec_ref[0] += fold_lanes(grad_norm_one * unit_one)
    g_vec_ref[1] += fold_lanes(grad_norm_one)
    grad_token = grad_residual + norm_back(
        grad_norm_one * column(cols, COL_GAIN_ONE, tile), unit_one, scale_ref[0:1, :]
    )
    grad_ref[...] = jnp.transpose(grad_token)

    @pl.when(step == steps - 1)
    def _():
        mask = head_mask()
        for slot, target in enumerate((own_msg_ref, other_msg_ref)):
            target[items * HD :, :] = jnp.zeros((target.shape[0] - items * HD, LANES), F32)
            for item in range(items):
                full = acc_ref[item, slot * D : (slot + 1) * D, :]
                target[item * HD : (item + 1) * HD, :] = fold_heads(full, mask)
                sums = acc_ref[item, (2 + slot) * D : (3 + slot) * D, :]
                target[items * HD + item : items * HD + item + 1, :] = fold_heads(sums, mask)[0:1]


def pack_kernel(
    plan,
    scal_ref,
    g_query_ref,
    g_out_ref,
    g_up_ref,
    g_down_ref,
    g_vec_ref,
    own_ref,
    other_ref,
    vec_ref,
    tmp_ref,
):
    parts, shard, half = plan
    vec_ref[SHARED_ROWS:, :] = jnp.zeros((vec_ref.shape[0] - SHARED_ROWS, LANES), F32)
    for slot, row in enumerate((ROW_GAIN_ONE, ROW_SHIFT_ONE, ROW_GAIN_TWO, ROW_SHIFT_TWO)):
        vec_ref[row : row + 1, :] = lane_total_row(g_vec_ref[slot])
    vec_ref[ROW_QUERY : ROW_QUERY + D, :] = g_query_ref[...]
    vec_ref[ROW_OUT : ROW_OUT + D + 1, :] = g_out_ref[: D + 1, :]
    for expert in range(E):
        for part in range(2):
            columns = slice(part * D, (part + 1) * D)
            vec_ref[pl.ds(ROW_UP + expert * 2 * D + part, D, stride=2), :] = g_up_ref[
                expert, :D, columns
            ]
            row = ROW_UP_B + 2 * expert + part
            vec_ref[row : row + 1, :] = g_up_ref[expert, D : D + 1, columns]
        row = ROW_DOWN + expert * FF
        vec_ref[row : row + FF, :] = g_down_ref[expert, :FF, :]
        row = ROW_DOWN_B + expert
        vec_ref[row : row + 1, :] = g_down_ref[expert, FF : FF + 1, :]
    core = scal_ref[0]
    own_at = pl.multiple_of(core * half, 8)
    other_at = pl.multiple_of((1 - core) * half, 8)
    for number in range(parts):
        tmp_ref[...] = take_shard(vec_ref, number, shard, 2 * half)
        own_ref[number] = tmp_ref[pl.ds(own_at, half), :]
        other_ref[number] = tmp_ref[pl.ds(other_at, half), :].astype(BF16)


def sample_backward_kernel(
    plan,
    scal_ref,
    count_ref,
    msg_ref,
    func_ref,
    keys_ref,
    vals_ref,
    first_ref,
    second_ref,
    slope_one_ref,
    slope_two_ref,
    hid_ref,
    pair_ref,
    out_own_ref,
    out_other_ref,
    grad_own_ref,
    grad_other_ref,
    send_ref,
    out_ref,
    grad_ref,
    vec_ref,
    left_keys_ref,
    left_vals_ref,
    shift_ref,
    keys_acc_ref,
    vals_acc_ref,
    g_pair_ref,
    g_hid_ref,
    g_in_ref,
    starts,
):
    tile, items, parts, shard, height, slots, steps = plan
    step = pl.program_id(0)
    core = scal_ref[0]
    out_ref[core] = out_own_ref[...]
    out_ref[1 - core] = out_other_ref[...]
    grad_ref[core] = grad_own_ref[...]
    grad_ref[1 - core] = grad_other_ref[...]

    @pl.when(step == 0)
    def _():
        store_starts(lambda item: count_ref[0, item], starts, items)
        g_pair_ref[...] = jnp.zeros(g_pair_ref.shape, F32)
        g_hid_ref[...] = jnp.zeros(g_hid_ref.shape, F32)
        g_in_ref[...] = jnp.zeros(g_in_ref.shape, F32)
        mask = head_mask()
        low, high = item_span(
            starts, items, scal_ref[1] * slots, scal_ref[1] * slots + tile * steps
        )

        def build(item, carry):
            at = pl.multiple_of(item * HD, HD)
            block = spread_heads(msg_ref[pl.ds(at, HD), :], mask)
            left_vals_ref[item] = block.astype(BF16)
            left_keys_ref[item] = jnp.transpose(block).astype(BF16)
            row = msg_ref[pl.ds(items * HD + item, 1), :]
            shift_ref[item] = jnp.transpose(jnp.broadcast_to(row, (D, D)))
            return carry

        @pl.when(high <= low)
        def _():
            last = items - 1
            left_vals_ref[last] = jnp.zeros((D, D), BF16)
            left_keys_ref[last] = jnp.zeros((D, D), BF16)
            shift_ref[last] = jnp.zeros((D, D), F32)

        lax.fori_loop(low, high, build, 0)

    keys = keys_ref[...]
    vals = vals_ref[...]
    begin = scal_ref[1] * slots + step * tile

    def visit(item, opening):
        row = item_row(starts, item, begin, tile)
        fresh_keys = row * (dot_nn(left_keys_ref[item], vals) + wide(shift_ref[item], tile))
        fresh_vals = row * dot_nn(left_vals_ref[item], keys)
        keys_acc_ref[...] = fresh_keys if opening else keys_acc_ref[...] + fresh_keys
        vals_acc_ref[...] = fresh_vals if opening else vals_acc_ref[...] + fresh_vals

    over_items(starts, items, begin, tile, visit)
    soft = keys.astype(F32)
    grad_keys = keys_acc_ref[...]
    grad_in = soft * (grad_keys - head_sum(grad_keys * soft))
    grad_pair = jnp.concatenate([grad_in, vals_acc_ref[...]], axis=0).astype(BF16)
    g_pair_ref[...] += dot_nt(second_ref[...], grad_pair)
    grad_second = (slope_two_ref[...].astype(F32) * dot_nn(pair_ref[...], grad_pair)).astype(BF16)
    first_ones = jnp.concatenate([first_ref[...], jnp.ones((16, tile), BF16)], axis=0)
    g_hid_ref[...] += dot_nt(first_ones, grad_second)
    grad_first = slope_one_ref[...].astype(F32) * dot_nn(hid_ref[...], grad_second)
    funcs = func_ref[0]
    for part in range(FIN):
        g_in_ref[part] += fold_lanes(grad_first * funcs[part : part + 1, :])
    g_in_ref[FIN] += fold_lanes(grad_first)

    @pl.when(step == steps - 1)
    def _():
        vec_ref[BRANCH_ROWS:, :] = jnp.zeros((vec_ref.shape[0] - BRANCH_ROWS, LANES), F32)
        for part in range(FIN + 1):
            vec_ref[part : part + 1, :] = lane_total_row(g_in_ref[part])
        vec_ref[ROW_HID : ROW_HID + D + 1, :] = g_hid_ref[: D + 1, :]
        for part in range(2):
            vec_ref[pl.ds(ROW_PAIR + part, D, stride=2), :] = g_pair_ref[
                :, part * D : (part + 1) * D
            ]
        for number in range(parts):
            send_ref[number] = take_shard(vec_ref, number, shard, height).astype(BF16)


def sum_over_points(values, count, besides):
    bit = 1
    number = 0
    while bit < count:
        masks = [bit] if 2 * bit >= count else [bit, 2 * bit, 3 * bit]
        pieces = [
            lax.ppermute(values, "pts", [(source, source ^ mask) for source in range(count)])
            for mask in masks
        ]
        if number < len(besides):
            before = besides[number - 1] if number else None
            pieces, besides[number] = lax.optimization_barrier((pieces, besides[number](before)))
        values = functools.reduce(jnp.add, pieces, values)
        bit *= 4
        number += 1
    return values, besides


def gather_blocks(block, count):
    return lax.all_to_all(jnp.broadcast_to(block, (count,) + block.shape), "pts", 0, 0)


def swap_cores(values):
    return lax.ppermute(values, "branch", [(0, 1), (1, 0)])


def whole(shape, kind=None):
    zeros = (0,) * len(shape)
    return pl.BlockSpec(shape, lambda *_: zeros)


def body(
    tokens,
    funcs,
    item_counts,
    func_counts,
    gate_ints,
    cotangent,
    shared_master,
    shared_m,
    shared_v,
    branch_master,
    branch_m,
    branch_v,
):
    count = lax.axis_size("pts")
    core = lax.axis_index("branch")
    scal = jnp.stack([core, lax.axis_index("pts")]).astype(jnp.int32)
    items = item_counts.shape[0]
    chip_rows = tokens.shape[0]
    rows = chip_rows // 2
    slots = funcs.shape[2]
    shared_len = shared_master.shape[0]
    branch_len = branch_master.shape[1]
    half = up_to(-(-shared_len // (2 * LANES)), 16)
    height = up_to(-(-branch_len // LANES), 16)
    msg_rows = items * HD + up_to(items, 8)
    params = pltpu.CompilerParams(vmem_limit_bytes=VMEM_BASE + items * VMEM_ITEM)
    shape = jax.ShapeDtypeStruct

    shared_pad = jnp.pad(shared_master.astype(BF16), (0, 2 * half * LANES - shared_len))
    shared_half = lax.dynamic_slice_in_dim(shared_pad, core * (half * LANES), half * LANES, 0)
    branch_pad = jnp.pad(
        branch_master.reshape(-1).astype(BF16), (0, height * LANES - branch_len)
    )
    recv_branch = gather_blocks(branch_pad.reshape(height, LANES), count)
    recv_branch, shared_half = lax.optimization_barrier((recv_branch, shared_half))
    recv_shared = gather_blocks(shared_half.reshape(half, LANES), count)

    tile = min(SAMPLE_TILE, slots)
    steps = slots // tile
    stream = lambda height_: pl.BlockSpec((height_, tile), lambda i, *_: (0, i))
    vec_rows = up_to(BRANCH_ROWS + 2 * height + 8, 8)
    (
        msg,
        keys,
        vals,
        first,
        second,
        slope_one,
        slope_two,
        hid_w,
        pair_w,
    ) = pl.pallas_call(
        functools.partial(
            sample_forward_kernel, (tile, items, count, branch_len, height, slots)
        ),
        grid_spec=pltpu.PrefetchScalarGridSpec(
            num_scalar_prefetch=1,
            grid=(steps,),
            in_specs=[
                pl.BlockSpec(memory_space=pltpu.SMEM),
                pl.BlockSpec((count, height, LANES), lambda i, *_: (0, 0, 0)),
                pl.BlockSpec((1, FIN, tile), lambda i, *_: (0, 0, i)),
            ],
            out_specs=[
                whole((msg_rows, LANES)),
                stream(D),
                stream(D),
                stream(D),
                stream(D),
                stream(D),
                stream(D),
                whole((D, D)),
                whole((D, 2 * D)),
            ],
            scratch_shapes=[
                pltpu.VMEM((vec_rows, LANES), F32),
                pltpu.VMEM((8 + 2 * height, LANES), F32),
                pltpu.VMEM((5, D, D), F32),
                pltpu.VMEM((D, D), BF16),
                pltpu.VMEM((2 * D, D), BF16),
                pltpu.VMEM((items, D + 16, D), F32),
                pltpu.SMEM((items + 1,), jnp.int32),
            ],
        ),
        out_shape=[
            shape((msg_rows, LANES), F32),
            pltpu.HBM((D, slots), BF16),
            pltpu.HBM((D, slots), BF16),
            pltpu.HBM((D, slots), BF16),
            pltpu.HBM((D, slots), BF16),
            pltpu.HBM((D, slots), BF16),
            pltpu.HBM((D, slots), BF16),
            shape((D, D), BF16),
            shape((D, 2 * D), BF16),
        ],
        compiler_params=params,
        cost_estimate=pl.CostEstimate(
            flops=slots * D * D * 10, bytes_accessed=slots * D * 12, transcendentals=slots * D * 3
        ),
        name="sample_forward",
    )(scal, func_counts, recv_branch, funcs)

    shared_rows = up_to(SHARED_ROWS + 2 * half + 8, 8)

    def make_weights():
        return pl.pallas_call(
            functools.partial(weight_kernel, (count, shared_len, half)),
            in_specs=[
                pl.BlockSpec(memory_space=pltpu.SMEM),
                whole(recv_shared.shape),
                whole(recv_shared.shape),
            ],
            out_specs=[
                whole((D, D)),
                whole((D, D)),
                whole((D, D)),
                whole((D, D)),
                whole((E, D, FF)),
                whole((E, FF, D)),
                whole((E, FF, D)),
                whole((E, D, FF)),
                whole((D, D)),
            ],
            out_shape=[
                shape((D, D), BF16),
                shape((D, D), BF16),
                shape((D, D), BF16),
                shape((D, D), BF16),
                shape((E, D, FF), BF16),
                shape((E, FF, D), BF16),
                shape((E, FF, D), BF16),
                shape((E, D, FF), BF16),
                shape((D, D), F32),
            ],
            scratch_shapes=[
                pltpu.VMEM((shared_rows, LANES), F32),
                pltpu.VMEM((max(8 + 2 * half, D) + 8, LANES), F32),
            ],
            compiler_params=params,
            cost_estimate=pl.CostEstimate(flops=0, bytes_accessed=8 << 20, transcendentals=0),
            name="weights",
        )(scal, recv_shared, recv_other)

    token_tile = min(TOKEN_TILE, rows)
    token_steps = rows // token_tile
    row_block = pl.BlockSpec(
        (token_tile, D), lambda i, scal_ref: (scal_ref[0] * token_steps + i, 0)
    )
    token_stream = lambda height_: pl.BlockSpec((height_, token_tile), lambda i, *_: (0, i))

    def make_queries(weights):
        return pl.pallas_call(
            query_kernel,
            grid_spec=pltpu.PrefetchScalarGridSpec(
                num_scalar_prefetch=1,
                grid=(token_steps,),
                in_specs=[row_block, row_block, whole((D, D)), whole((D, D))],
                out_specs=[
                    token_stream(D),
                    token_stream(D),
                    token_stream(D),
                    token_stream(8),
                    token_stream(D),
                    token_stream(D),
                ],
            ),
            out_shape=[
                shape((D, rows), BF16),
                shape((D, rows), F32),
                shape((D, rows), F32),
                shape((8, rows), F32),
                shape((D, rows), BF16),
                shape((D, rows), F32),
            ],
            compiler_params=params,
            cost_estimate=pl.CostEstimate(
                flops=rows * D * D * 2, bytes_accessed=rows * D * 24, transcendentals=rows * D
            ),
            name="queries",
        )(scal, tokens, cotangent, weights[1], weights[8])

    msg, recv_shared = lax.optimization_barrier((msg, recv_shared))
    recv_other = swap_cores(recv_shared)
    weights = make_weights()
    summary, (weights, queries) = sum_over_points(
        msg, count, [lambda _: weights, make_queries]
    )
    query_w, query_t, out_w, out_t, up_w, up_t, down_w, down_t, cols = weights
    token_t, cot_t, unit, scale, norm, soft = queries
    summary_other = swap_cores(summary)

    (
        output_own,
        grad_own,
        own_msg,
        other_msg,
        g_query,
        g_out,
        g_up,
        g_down,
        g_vec,
    ) = pl.pallas_call(
        functools.partial(token_kernel, (token_tile, items, chip_rows, token_steps)),
        grid_spec=pltpu.PrefetchScalarGridSpec(
            num_scalar_prefetch=1,
            grid=(token_steps,),
            in_specs=[
                pl.BlockSpec(memory_space=pltpu.SMEM),
                whole((msg_rows, LANES)),
                whole((msg_rows, LANES)),
                pl.BlockSpec((E, token_tile), lambda i, scal_ref: (0, scal_ref[0] * token_steps + i)),
                token_stream(D),
                token_stream(D),
                token_stream(D),
                token_stream(8),
                token_stream(D),
                token_stream(D),
                whole((D, D)),
                whole((D, D)),
                whole((D, D)),
                whole((E, D, FF)),
                whole((E, FF, D)),
                whole((E, FF, D)),
                whole((E, D, FF)),
                whole((D, D)),
            ],
            out_specs=[
                pl.BlockSpec((token_tile, D), lambda i, *_: (i, 0)),
                pl.BlockSpec((token_tile, D), lambda i, *_: (i, 0)),
                whole((msg_rows, LANES)),
                whole((msg_rows, LANES)),
                whole((D, D)),
                whole((D + 16, D)),
                whole((E, D + 16, FF)),
                whole((E, FF + 16, D)),
                whole((4, D, D)),
            ],
            scratch_shapes=[
                pltpu.VMEM((items, 4 * D, 2 * D), BF16),
                pltpu.VMEM((items, D, 4 * D), BF16),
                pltpu.VMEM((items, 4 * D, D), F32),
                pltpu.VMEM((4 * D, token_tile), F32),
                pltpu.VMEM((D, token_tile), F32),
                pltpu.SMEM((items + 1,), jnp.int32),
            ],
        ),
        out_shape=[
            shape((rows, D), BF16),
            shape((rows, D), F32),
            shape((msg_rows, LANES), F32),
            shape((msg_rows, LANES), F32),
            shape((D, D), F32),
            shape((D + 16, D), F32),
            shape((E, D + 16, FF), F32),
            shape((E, FF + 16, D), F32),
            shape((4, D, D), F32),
        ],
        compiler_params=params,
        cost_estimate=pl.CostEstimate(
            flops=rows * D * FF * 12 * E, bytes_accessed=rows * D * 24, transcendentals=rows * FF * E
        ),
        name="tokens",
    )(
        scal,
        item_counts,
        summary,
        summary_other,
        gate_ints.T,
        token_t,
        cot_t,
        unit,
        scale,
        norm,
        soft,
        query_w,
        out_w,
        out_t,
        up_w,
        up_t,
        down_w,
        down_t,
        cols,
    )

    both_msg, parts = lax.optimization_barrier(
        (own_msg + swap_cores(other_msg), (g_query, g_out, g_up, g_down, g_vec))
    )
    half_own, half_other = pl.pallas_call(
        functools.partial(pack_kernel, (count, shared_len, half)),
        in_specs=[pl.BlockSpec(memory_space=pltpu.SMEM)]
        + [whole(piece.shape) for piece in parts],
        out_specs=[whole((count, half, LANES)), whole((count, half, LANES))],
        out_shape=[shape((count, half, LANES), F32), shape((count, half, LANES), BF16)],
        scratch_shapes=[
            pltpu.VMEM((shared_rows, LANES), F32),
            pltpu.VMEM((2 * half, LANES), F32),
        ],
        compiler_params=params,
        cost_estimate=pl.CostEstimate(flops=2 << 30, bytes_accessed=4 << 20, transcendentals=0),
        name="pack",
    )(scal, *parts)

    def add_halves(packed):
        return (packed[0] + swap_cores(packed[1]).astype(F32)).astype(BF16)

    output_other = swap_cores(output_own)
    grad_other = swap_cores(grad_own)
    packed = [half_own, half_other]
    summary_grad, (_, half_sum) = sum_over_points(
        both_msg,
        count,
        [lambda _: packed, lambda ready: (add_halves(ready), output_other, grad_other)],
    )
    half_sum, output_other, grad_other = half_sum
    summary_grad, half_sum = lax.optimization_barrier((summary_grad, half_sum))
    keys, vals, first, second, slope_one, slope_two = (
        pltpu.with_memory_space_constraint(kept, pltpu.HBM)
        for kept in (keys, vals, first, second, slope_one, slope_two)
    )
    piece = pl.BlockSpec((rows // steps, D), lambda i, *_: (i, 0))
    both = pl.BlockSpec((2, rows // steps, D), lambda i, *_: (0, i, 0))
    shared_recv = lax.all_to_all(half_sum, "pts", 0, 0)
    grads_send, output, token_grad = pl.pallas_call(
        functools.partial(
            sample_backward_kernel,
            (tile, items, count, branch_len, height, slots, steps),
        ),
        grid_spec=pltpu.PrefetchScalarGridSpec(
            num_scalar_prefetch=1,
            grid=(steps,),
            in_specs=[
                pl.BlockSpec(memory_space=pltpu.SMEM),
                whole((msg_rows, LANES)),
                pl.BlockSpec((1, FIN, tile), lambda i, *_: (0, 0, i)),
                stream(D),
                stream(D),
                stream(D),
                stream(D),
                stream(D),
                stream(D),
                whole((D, D)),
                whole((D, 2 * D)),
                piece,
                piece,
                piece,
                piece,
            ],
            out_specs=[whole((count, height, LANES)), both, both],
            scratch_shapes=[
                pltpu.VMEM((vec_rows, LANES), F32),
                pltpu.VMEM((items, D, D), BF16),
                pltpu.VMEM((items, D, D), BF16),
                pltpu.VMEM((items, D, D), F32),
                pltpu.VMEM((D, tile), F32),
                pltpu.VMEM((D, tile), F32),
                pltpu.VMEM((D, 2 * D), F32),
                pltpu.VMEM((D + 16, D), F32),
                pltpu.VMEM((FIN + 1, D, D), F32),
                pltpu.SMEM((items + 1,), jnp.int32),
            ],
        ),
        out_shape=[
            shape((count, height, LANES), BF16),
            shape((2, rows, D), BF16),
            shape((2, rows, D), F32),
        ],
        compiler_params=params,
        cost_estimate=pl.CostEstimate(
            flops=slots * D * D * 300, bytes_accessed=slots * D * 12, transcendentals=0
        ),
        name="sample_backward",
    )(
        scal,
        func_counts,
        summary_grad,
        funcs,
        keys,
        vals,
        first,
        second,
        slope_one,
        slope_two,
        hid_w,
        pair_w,
        output_own,
        output_other,
        grad_own,
        grad_other,
    )

    grads_send, shared_recv = lax.optimization_barrier((grads_send, shared_recv))
    own_half = jnp.sum(shared_recv.astype(F32), axis=0).reshape(-1)
    other_half = swap_cores(own_half)
    shared_grad = jnp.where(
        core == 0,
        jnp.concatenate([own_half, other_half]),
        jnp.concatenate([other_half, own_half]),
    )[:shared_len]
    branch_recv = lax.all_to_all(grads_send, "pts", 0, 0)
    branch_grad = jnp.sum(branch_recv.astype(F32), axis=0).reshape(1, -1)[:, :branch_len]
    new_branch, new_branch_m, new_branch_v = adam_step(
        branch_master, branch_m, branch_v, branch_grad
    )
    new_shared, new_shared_m, new_shared_v = adam_step(
        shared_master, shared_m, shared_v, shared_grad
    )
    return (
        output.reshape(chip_rows, D),
        token_grad.reshape(chip_rows, D),
        new_shared,
        new_shared_m,
        new_shared_v,
        new_branch,
        new_branch_m,
        new_branch_v,
    )


def solution(mesh):
    in_specs = (
        P("pts", None),
        P("branch", None, "pts"),
        P(),
        P("branch", None),
        P("pts", None),
        P("pts", None),
        P("pts"),
        P("pts"),
        P("pts"),
        P("branch", "pts"),
        P("branch", "pts"),
        P("branch", "pts"),
    )
    out_specs = (
        P("pts", None),
        P("pts", None),
        P("pts"),
        P("pts"),
        P("pts"),
        P("branch", "pts"),
        P("branch", "pts"),
        P("branch", "pts"),
    )
    return jax.shard_map(body, mesh=mesh, in_specs=in_specs, out_specs=out_specs, check_vma=False)
```

```python
import functools
import math

import jax
import jax.numpy as jnp
from jax import lax
from jax.experimental import pallas as pl
from jax.experimental.pallas import tpu as pltpu
from jax.sharding import PartitionSpec as P

D = 128
H = 8
HD = 16
FF = 256
E = 4
FIN = 3
STEP = 10

EPS_NORM = 1e-05
BETA_ONE = 0.9
BETA_TWO = 0.999
RATE_LEARN = 0.1
DECAY_RATE = 0.01
EPS_ADAM = 1e-08

LANES = 128
VMEM_BASE = 16 * 1024 * 1024
VMEM_ITEM = 768 * 1024
SAMPLE_TILE = 2048
BACK_TILE = 2048
TOKEN_TILE = 1024
CHUNK = 256

F32 = jnp.float32
BF16 = jnp.bfloat16

ROW_GAIN_ONE = 0
ROW_SHIFT_ONE = 1
ROW_QUERY = 2
ROW_OUT = ROW_QUERY + D
ROW_OUT_B = ROW_OUT + D
ROW_GAIN_TWO = ROW_OUT_B + 1
ROW_SHIFT_TWO = ROW_GAIN_TWO + 1
ROW_UP = ROW_SHIFT_TWO + 1
ROW_UP_B = ROW_UP + E * D * 2
ROW_DOWN = ROW_UP_B + E * 2
ROW_DOWN_B = ROW_DOWN + E * FF
SHARED_ROWS = ROW_DOWN_B + E

ROW_IN = 0
ROW_IN_B = ROW_IN + FIN
ROW_HID = ROW_IN_B + 1
ROW_HID_B = ROW_HID + D
ROW_PAIR = ROW_HID_B + 1
BRANCH_ROWS = ROW_PAIR + 2 * D

COL_GAIN_ONE = 0
COL_SHIFT_ONE = 1
COL_OUT_B = 2
COL_GAIN_TWO = 3
COL_SHIFT_TWO = 4
COL_UP_B = 5
COL_DOWN_B = COL_UP_B + 2 * E

TANH_C = math.sqrt(2.0 / math.pi)
TANH_CUBE = 0.044715


def up_to(amount, unit):
    return -(-amount // unit) * unit


def adam_step(master, moment_one, moment_two, grad):
    first = BETA_ONE * moment_one + (1.0 - BETA_ONE) * grad
    second = BETA_TWO * moment_two + (1.0 - BETA_TWO) * grad * grad
    first_hat = first / (1.0 - BETA_ONE**STEP)
    second_hat = second / (1.0 - BETA_TWO**STEP)
    fresh = master - RATE_LEARN * (
        first_hat / (jnp.sqrt(second_hat) + EPS_ADAM) + DECAY_RATE * master
    )
    return (fresh, first, second)


def dot_nn(left, right):
    return jnp.dot(left, right, preferred_element_type=F32)


def dot_nt(left, right):
    return lax.dot_general(left, right, (((1,), (1,)), ((), ())), preferred_element_type=F32)


def head_sum(values):
    split = values.reshape(H, HD, values.shape[1])
    total = jnp.sum(split, axis=1, keepdims=True)
    return jnp.broadcast_to(total, split.shape).reshape(values.shape)


def head_softmax(values):
    split = values.reshape(H, HD, values.shape[1])
    top = jnp.max(split, axis=1, keepdims=True)
    raised = jnp.exp(split - top)
    total = jnp.sum(raised, axis=1, keepdims=True)
    return (raised * (1.0 / total)).reshape(values.shape)


def gelu_value(inner):
    square = inner * inner
    bend = inner * (TANH_C + (TANH_C * TANH_CUBE) * square)
    return inner * (0.5 + 0.5 * jnp.tanh(bend))


def gelu_parts(inner):
    square = inner * inner
    bend = inner * (TANH_C + (TANH_C * TANH_CUBE) * square)
    gate = 0.5 + 0.5 * jnp.tanh(bend)
    rise = inner * (2.0 * TANH_C + (6.0 * TANH_C * TANH_CUBE) * square)
    return inner * gate, gate + (gate - gate * gate) * rise


def split_samples(funcs, parts_ref):
    high = funcs.astype(BF16).astype(F32)
    middle = (funcs - high).astype(BF16).astype(F32)
    parts_ref[0:FIN, :] = high
    parts_ref[FIN : 2 * FIN, :] = middle
    parts_ref[2 * FIN : 3 * FIN, :] = funcs - high - middle
    parts_ref[3 * FIN : 3 * FIN + 1, :] = jnp.ones((1, funcs.shape[1]), F32)
    parts_ref[3 * FIN + 1 :, :] = jnp.zeros((15 - 3 * FIN, funcs.shape[1]), F32)
    return parts_ref[...].astype(BF16)


def staggered(programs):
    waiting = list(programs)
    running = []
    while waiting or running:
        if waiting:
            running.append(waiting.pop(0))
        still = []
        for program in running:
            try:
                next(program)
                still.append(program)
            except StopIteration:
                pass
        running = still


def wide(tile, length):
    if length == tile.shape[1]:
        return tile
    return jnp.concatenate([tile] * (length // tile.shape[1]), axis=1)


def column(matrix, index, length):
    return jnp.broadcast_to(matrix[:, index : index + 1], (matrix.shape[0], length))


def fold_lanes(values):
    total = values[:, :LANES]
    for start in range(LANES, values.shape[1], LANES):
        total = total + values[:, start : start + LANES]
    return total


def lane_total_row(values):
    return jnp.sum(jnp.transpose(values), axis=0, keepdims=True)


def head_mask():
    row = lax.broadcasted_iota(jnp.int32, (D, D), 0) // HD
    col = lax.broadcasted_iota(jnp.int32, (D, D), 1) // HD
    return (row == col).astype(F32)


def fold_heads(values, mask):
    return jnp.sum((values * mask).reshape(H, HD, D), axis=0)


def spread_heads(compact, mask):
    return jnp.concatenate([compact] * H, axis=0) * mask


def store_starts(counts, starts, items):
    if items <= 8:
        total = jnp.int32(0)
        for item in range(items):
            starts[item] = total
            total = total + counts(item)
        starts[items] = total
    else:
        def step(item, total):
            starts[item] = total
            return total + counts(item)

        starts[items] = lax.fori_loop(0, items, step, jnp.int32(0))


def item_span(starts, items, begin, end):
    def step(item, span):
        low, high = span
        return (
            low + (starts[item + 1] <= begin).astype(jnp.int32),
            high + (starts[item] < end).astype(jnp.int32),
        )

    span = (jnp.int32(0), jnp.int32(0))
    if items <= 8:
        for item in range(items):
            span = step(item, span)
        return span
    return lax.fori_loop(0, items, step, span)


def item_row(starts, item, begin, length):
    position = begin + lax.broadcasted_iota(jnp.int32, (1, length), 1)
    return ((position >= starts[item]) & (position < starts[item + 1])).astype(F32)


def over_items(starts, items, begin, length, visit):
    low, high = item_span(starts, items, begin, begin + length)
    visit(jnp.minimum(low, items - 1), True)

    def step(item, carry):
        visit(item, False)
        return carry

    lax.fori_loop(low + 1, high, step, 0)


def over_parts(starts, item, begin, length, visit):
    width = min(256, length)
    for at in range(0, length, width):
        start = begin + at

        @pl.when((starts[item] < start + width) & (starts[item + 1] > start))
        def _(at=at, start=start):
            visit(slice(at, at + width), start)


def put_shard(vec_ref, tmp_ref, number, shard, height):
    row, shift = divmod(number * shard, LANES)
    touched = (shift + shard - 1) // LANES + 1
    if shift == 0:
        vec_ref[row : row + touched, :] = tmp_ref[8 : 8 + touched, :]
        return
    if number == 0:
        tmp_ref[7:8, :] = jnp.zeros((1, LANES), F32)
    else:
        tmp_ref[7:8, :] = vec_ref[row : row + 1, :]
    lane = lax.broadcasted_iota(jnp.int32, (touched, LANES), 1)
    vec_ref[row : row + touched, :] = jnp.where(
        lane >= shift, tmp_ref[8 : 8 + touched, :], tmp_ref[7 : 7 + touched, :]
    )


def turned(block, amount):
    amount = amount % LANES
    return block if amount == 0 else pltpu.roll(block, amount, 1)


def take_shard(vec_ref, number, shard, height):
    row, shift = divmod(number * shard, LANES)
    here = vec_ref[row : row + height, :]
    if shift == 0:
        return here
    after = vec_ref[row + 1 : row + 1 + height, :]
    lane = lax.broadcasted_iota(jnp.int32, (height, LANES), 1)
    return turned(jnp.where(lane >= shift, here, after), LANES - shift)


def sample_forward_kernel(
    plan,
    scal_ref,
    count_hbm,
    recv_ref,
    func_ref,
    msg_ref,
    keys_ref,
    vals_ref,
    hid_ref,
    pair_ref,
    in_t_ref,
    hid_t_ref,
    col_ref,
    vec_ref,
    tmp_ref,
    parts_ref,
    pair_t_ref,
    acc_ref,
    starts,
    count_ref,
    sem,
):
    tile, items, parts, shard, height, slots = plan
    step = pl.program_id(0)

    @pl.when(step == 0)
    def _():
        fetch = pltpu.make_async_copy(count_hbm, count_ref, sem)
        fetch.start()
        acc_ref[...] = jnp.zeros(acc_ref.shape, F32)
        for number in range(parts):
            shift = (number * shard) % LANES
            tmp_ref[8 : 8 + height, :] = turned(recv_ref[number].astype(F32), shift)
            put_shard(vec_ref, tmp_ref, number, shard, height)
        col_ref[...] = jnp.transpose(
            jnp.broadcast_to(vec_ref[ROW_HID_B : ROW_HID_B + 1, :], (D, D))
        )
        tmp_ref[0:16, :] = jnp.zeros((16, LANES), F32)
        for part in range(3):
            tmp_ref[part * FIN : (part + 1) * FIN, :] = vec_ref[ROW_IN : ROW_IN + FIN, :]
        tmp_ref[3 * FIN : 3 * FIN + 1, :] = vec_ref[ROW_IN_B : ROW_IN_B + 1, :]
        in_t_ref[...] = jnp.transpose(tmp_ref[0:16, :]).astype(BF16)
        hid = vec_ref[ROW_HID : ROW_HID + D, :]
        hid_ref[...] = hid.astype(BF16)
        hid_t_ref[...] = jnp.transpose(hid).astype(BF16)
        for part in range(2):
            piece = vec_ref[pl.ds(ROW_PAIR + part, D, stride=2), :]
            pair_ref[:, part * D : (part + 1) * D] = piece.astype(BF16)
            pair_t_ref[part * D : (part + 1) * D, :] = jnp.transpose(piece).astype(BF16)
        fetch.wait()
        store_starts(lambda item: count_ref[0, item], starts, items)

    samples = split_samples(func_ref[0], parts_ref)
    chunk = min(CHUNK, tile)

    def forward(start):
        at = slice(start, start + chunk)
        first_in = dot_nn(in_t_ref[...], samples[:, at])
        yield
        first = gelu_value(first_in).astype(BF16)
        yield
        second_in = dot_nn(hid_t_ref[...], first)
        yield
        second = gelu_value(second_in + wide(col_ref[...], chunk)).astype(BF16)
        yield
        pair = dot_nn(pair_t_ref[...], second)
        yield
        vals_ref[:, at] = pair[D:].astype(BF16)
        keys_ref[:, at] = head_softmax(pair[:D]).astype(BF16)

    staggered([forward(start) for start in range(0, tile, chunk)])
    keys = keys_ref[...]
    vals_ones = jnp.concatenate([vals_ref[...], jnp.ones((16, tile), BF16)], axis=0)
    begin = scal_ref[1] * slots + step * tile

    def visit(item, _):
        masked = keys * item_row(starts, item, begin, tile).astype(BF16)
        acc_ref[item] += dot_nt(vals_ones, masked)

    over_items(starts, items, begin, tile, visit)

    @pl.when(step == pl.num_programs(0) - 1)
    def _():
        mask = head_mask()
        msg_ref[items * HD :, :] = jnp.zeros((msg_ref.shape[0] - items * HD, LANES), F32)
        for item in range(items):
            msg_ref[item * HD : (item + 1) * HD, :] = fold_heads(acc_ref[item, :D, :], mask)
            msg_ref[items * HD + item : items * HD + item + 1, :] = acc_ref[item, D : D + 1, :]


def slope_kernel(func_ref, in_t_ref, hid_t_ref, col_ref, *refs):
    first_ref, second_ref, slope_one_ref, slope_two_ref, parts_ref = refs[-5:]
    samples = split_samples(func_ref[0], parts_ref)
    chunk = min(CHUNK, samples.shape[1])

    def slopes(start):
        at = slice(start, start + chunk)
        first_in = dot_nn(in_t_ref[...], samples[:, at])
        yield
        first, slope_one = gelu_parts(first_in)
        first = first.astype(BF16)
        first_ref[:, at] = first
        slope_one_ref[:, at] = slope_one.astype(BF16)
        yield
        second_in = dot_nn(hid_t_ref[...], first)
        yield
        second, slope_two = gelu_parts(second_in + wide(col_ref[...], chunk))
        second_ref[:, at] = second.astype(BF16)
        slope_two_ref[:, at] = slope_two.astype(BF16)

    staggered([slopes(start) for start in range(0, samples.shape[1], chunk)])


def weight_kernel(
    plan,
    scal_ref,
    own_ref,
    other_ref,
    query_ref,
    query_t_ref,
    out_ref,
    out_t_ref,
    up_ref,
    up_t_ref,
    down_ref,
    down_t_ref,
    cols_ref,
    vec_ref,
    tmp_ref,
):
    parts, shard, half = plan
    core = scal_ref[0]
    own_at = pl.multiple_of(8 + core * half, 8)
    other_at = pl.multiple_of(8 + (1 - core) * half, 8)
    for number in range(parts):
        shift = (number * shard) % LANES
        tmp_ref[pl.ds(own_at, half), :] = turned(
            own_ref[number].astype(F32), shift
        )
        tmp_ref[pl.ds(other_at, half), :] = turned(
            other_ref[number].astype(F32), shift
        )
        put_shard(vec_ref, tmp_ref, number, shard, 2 * half)
    query = vec_ref[ROW_QUERY : ROW_QUERY + D, :]
    query_ref[...] = query.astype(BF16)
    query_t_ref[...] = jnp.transpose(query).astype(BF16)
    out = vec_ref[ROW_OUT : ROW_OUT + D, :]
    out_ref[...] = out.astype(BF16)
    out_t_ref[...] = jnp.transpose(out).astype(BF16)
    for expert in range(E):
        for part in range(2):
            up = vec_ref[pl.ds(ROW_UP + expert * 2 * D + part, D, stride=2), :]
            up_ref[expert, :, part * D : (part + 1) * D] = up.astype(BF16)
            up_t_ref[expert, part * D : (part + 1) * D, :D] = jnp.transpose(up).astype(BF16)
            row = ROW_DOWN + expert * FF + part * D
            down = vec_ref[row : row + D, :]
            down_ref[expert, part * D : (part + 1) * D, :] = down.astype(BF16)
            down_t_ref[expert, :, part * D : (part + 1) * D] = jnp.transpose(down).astype(BF16)
    tmp_ref[0:D, :] = jnp.zeros((D, LANES), F32)
    rows = [ROW_GAIN_ONE, ROW_SHIFT_ONE, ROW_OUT_B, ROW_GAIN_TWO, ROW_SHIFT_TWO]
    rows += [ROW_UP_B + number for number in range(2 * E)]
    rows += [ROW_DOWN_B + number for number in range(E)]
    for slot, row in enumerate(rows):
        tmp_ref[slot : slot + 1, :] = vec_ref[row : row + 1, :]
    cols = jnp.transpose(tmp_ref[0:D, :])
    cols_ref[...] = cols
    lane = lax.broadcasted_iota(jnp.int32, (D, 16), 1)
    for expert in range(E):
        for part in range(2):
            bias = jnp.where(lane == COL_UP_B + 2 * expert + part, cols[:, :16], 0.0)
            up_t_ref[expert, part * D : (part + 1) * D, D:] = bias.astype(BF16)


def norm_unit(values):
    centre = values - jnp.sum(values, axis=0, keepdims=True) * (1.0 / D)
    spread = jnp.sum(centre * centre, axis=0, keepdims=True) * (1.0 / D)
    scale = lax.rsqrt(spread + EPS_NORM)
    return centre * scale, scale


def norm_back(grad_unit, unit, scale):
    mean_one = jnp.sum(grad_unit, axis=0, keepdims=True) * (1.0 / D)
    mean_two = jnp.sum(grad_unit * unit, axis=0, keepdims=True) * (1.0 / D)
    return scale * (grad_unit - mean_one - unit * mean_two)


def query_kernel(
    scal_ref,
    token_ref,
    cot_ref,
    query_t_ref,
    cols_ref,
    token_t_ref,
    cot_t_ref,
    unit_ref,
    scale_ref,
    norm_ref,
    soft_ref,
):
    tokens = jnp.transpose(token_ref[...].astype(F32))
    length = tokens.shape[1]
    token_t_ref[...] = tokens.astype(BF16)
    cot_t_ref[...] = jnp.transpose(cot_ref[...])
    unit, scale = norm_unit(tokens)
    unit_ref[...] = unit
    scale_ref[...] = jnp.broadcast_to(scale, scale_ref.shape)
    cols = cols_ref[...]
    norm = (unit * column(cols, COL_GAIN_ONE, length) + column(cols, COL_SHIFT_ONE, length)).astype(
        BF16
    )
    norm_ref[...] = norm
    soft_ref[...] = head_softmax(dot_nn(query_t_ref[...], norm))


def token_kernel(
    plan,
    scal_ref,
    own_ref,
    other_ref,
    gate_ref,
    token_t_ref,
    cot_t_ref,
    unit_ref,
    scale_ref,
    norm_ref,
    soft_ref,
    query_ref,
    out_w_ref,
    out_t_ref,
    up_ref,
    up_t_ref,
    down_ref,
    down_t_ref,
    cols_ref,
    output_ref,
    grad_ref,
    own_msg_ref,
    other_msg_ref,
    g_query_ref,
    g_out_ref,
    g_up_ref,
    g_down_ref,
    g_vec_ref,
    left_ref,
    back_ref,
    acc_ref,
    mix_ref,
    pull_ref,
    grads_ref,
    starts,
):
    tile, items, slots, steps = plan
    step = pl.program_id(0)
    first_row = scal_ref[1] * slots + scal_ref[0] * (tile * steps)

    @pl.when(step == 0)
    def _():
        store_starts(lambda item: scal_ref[2 + item], starts, items)
        acc_ref[...] = jnp.zeros(acc_ref.shape, F32)
        g_query_ref[...] = jnp.zeros(g_query_ref.shape, F32)
        g_out_ref[...] = jnp.zeros(g_out_ref.shape, F32)
        g_up_ref[...] = jnp.zeros(g_up_ref.shape, F32)
        g_down_ref[...] = jnp.zeros(g_down_ref.shape, F32)
        g_vec_ref[...] = jnp.zeros(g_vec_ref.shape, F32)
        mask = head_mask()
        low, high = item_span(starts, items, first_row, first_row + tile * steps)

        def build(item, carry):
            at = pl.multiple_of(item * HD, HD)
            for slot, source in enumerate((own_ref, other_ref)):
                block = spread_heads(source[pl.ds(at, HD), :], mask)
                total = source[pl.ds(items * HD + item, 1), :] * mask
                for kind, piece in enumerate((block, total)):
                    row = (2 * kind + slot) * D
                    high_part = piece.astype(BF16)
                    left_ref[item, row : row + D, :D] = high_part
                    left_ref[item, row : row + D, D:] = (piece - high_part.astype(F32)).astype(BF16)
                    turned_piece = jnp.transpose(piece)
                    if kind == 1:
                        turned_piece = turned_piece * (1.0 / HD)
                    back_ref[item, :, row : row + D] = turned_piece.astype(BF16)
            return carry

        lax.fori_loop(low, high, build, 0)

    cols = cols_ref[...]
    begin = first_row + step * tile
    soft = soft_ref[...]

    def attend(item, lanes, start):
        length = lanes.stop - lanes.start
        masked = soft_ref[:, lanes].astype(BF16) * item_row(starts, item, start, length).astype(BF16)
        return dot_nn(left_ref[item], jnp.concatenate([masked, masked], axis=0))

    def forward(item, opening):
        if opening:
            mix_ref[...] = attend(item, slice(0, tile), begin)
            return

        def add(lanes, start):
            mix_ref[:, lanes] += attend(item, lanes, start)

        over_parts(starts, item, begin, tile, add)

    over_items(starts, items, begin, tile, forward)
    numer_one, numer_two = mix_ref[:D, :], mix_ref[D : 2 * D, :]
    inv_one, inv_two = 1.0 / mix_ref[2 * D : 3 * D, :], 1.0 / mix_ref[3 * D :, :]
    own_one, own_two = numer_one * inv_one, numer_two * inv_two
    attended = (0.5 * (own_one + own_two)).astype(BF16)
    cot = cot_t_ref[...]
    residual = (
        token_t_ref[...].astype(F32)
        + dot_nn(out_t_ref[...], attended)
        + column(cols, COL_OUT_B, tile)
    )
    unit, scale = norm_unit(residual)
    gain_two = column(cols, COL_GAIN_TWO, tile)
    norm = (unit * gain_two + column(cols, COL_SHIFT_TWO, tile)).astype(BF16)
    ones = jnp.ones((16, tile), BF16)
    norm_ones = jnp.concatenate([norm, ones], axis=0)
    gates = gate_ref[...].astype(F32)
    gates = gates / jnp.sum(gates, axis=0, keepdims=True)
    mixture = residual
    grad_norm = jnp.zeros((D, tile), F32)
    for expert in range(E):
        inner = dot_nn(up_t_ref[expert], norm_ones)
        active, slope = gelu_parts(inner)
        active = active.astype(BF16)
        result = dot_nn(down_t_ref[expert], active) + column(cols, COL_DOWN_B + expert, tile)
        gate = gates[expert : expert + 1, :]
        mixture = mixture + gate * result
        grad_result = (gate * cot).astype(BF16)
        g_down_ref[expert] += dot_nt(jnp.concatenate([active, ones], axis=0), grad_result)
        grad_inner = (slope * dot_nn(down_ref[expert], grad_result)).astype(BF16)
        g_up_ref[expert] += dot_nt(norm_ones, grad_inner)
        grad_norm = grad_norm + dot_nn(up_ref[expert], grad_inner)
    output_ref[...] = jnp.transpose(mixture).astype(BF16)
    g_vec_ref[2] += fold_lanes(grad_norm * unit)
    g_vec_ref[3] += fold_lanes(grad_norm)
    grad_residual = cot + norm_back(grad_norm * gain_two, unit, scale)
    grad_proj = grad_residual.astype(BF16)
    g_out_ref[...] += dot_nt(jnp.concatenate([attended, ones], axis=0), grad_proj)
    grad_own = 0.5 * dot_nn(out_w_ref[...], grad_proj)
    grad_one, grad_two = grad_own * inv_one, grad_own * inv_two
    sum_one = -head_sum(grad_one * own_one)
    sum_two = -head_sum(grad_two * own_two)
    grads = jnp.concatenate([grad_one, grad_two, sum_one, sum_two], axis=0).astype(BF16)

    grads_ref[...] = grads

    def pull_back(item, lanes, start):
        length = lanes.stop - lanes.start
        row = item_row(starts, item, start, length)
        part = grads_ref[:, lanes]
        masked = soft_ref[:, lanes].astype(BF16) * row.astype(BF16)
        return dot_nt(part, masked), row * dot_nn(back_ref[item], part)

    def backward(item, opening):
        if opening:
            sums, pull_ref[...] = pull_back(item, slice(0, tile), begin)
            acc_ref[item] += sums
            return

        def add(lanes, start):
            sums, pull = pull_back(item, lanes, start)
            acc_ref[item] += sums
            pull_ref[:, lanes] += pull

        over_parts(starts, item, begin, tile, add)

    over_items(starts, items, begin, tile, backward)
    pull = pull_ref[...]
    grad_query = (soft * (pull - head_sum(pull * soft))).astype(BF16)
    g_query_ref[...] += dot_nt(norm_ref[...], grad_query)
    grad_norm_one = dot_nn(query_ref[...], grad_query)
    unit_one = unit_ref[...]
    g_vec_ref[0] += fold_lanes(grad_norm_one * unit_one)
    g_vec_ref[1] += fold_lanes(grad_norm_one)
    grad_token = grad_residual + norm_back(
        grad_norm_one * column(cols, COL_GAIN_ONE, tile), unit_one, scale_ref[0:1, :]
    )
    grad_ref[...] = jnp.transpose(grad_token)

    @pl.when(step == steps - 1)
    def _():
        mask = head_mask()
        for slot, target in enumerate((own_msg_ref, other_msg_ref)):
            target[items * HD :, :] = jnp.zeros((target.shape[0] - items * HD, LANES), F32)
            for item in range(items):
                full = acc_ref[item, slot * D : (slot + 1) * D, :]
                target[item * HD : (item + 1) * HD, :] = fold_heads(full, mask)
                sums = acc_ref[item, (2 + slot) * D : (3 + slot) * D, :]
                target[items * HD + item : items * HD + item + 1, :] = fold_heads(sums, mask)[0:1]


def pack_kernel(
    plan,
    scal_ref,
    g_query_ref,
    g_out_ref,
    g_up_ref,
    g_down_ref,
    g_vec_ref,
    own_ref,
    other_ref,
    vec_ref,
    tmp_ref,
):
    parts, shard, half = plan
    vec_ref[SHARED_ROWS:, :] = jnp.zeros((vec_ref.shape[0] - SHARED_ROWS, LANES), F32)
    for slot, row in enumerate((ROW_GAIN_ONE, ROW_SHIFT_ONE, ROW_GAIN_TWO, ROW_SHIFT_TWO)):
        vec_ref[row : row + 1, :] = lane_total_row(g_vec_ref[slot])
    vec_ref[ROW_QUERY : ROW_QUERY + D, :] = g_query_ref[...]
    vec_ref[ROW_OUT : ROW_OUT + D + 1, :] = g_out_ref[: D + 1, :]
    for expert in range(E):
        for part in range(2):
            columns = slice(part * D, (part + 1) * D)
            vec_ref[pl.ds(ROW_UP + expert * 2 * D + part, D, stride=2), :] = g_up_ref[
                expert, :D, columns
            ]
            row = ROW_UP_B + 2 * expert + part
            vec_ref[row : row + 1, :] = g_up_ref[expert, D : D + 1, columns]
        row = ROW_DOWN + expert * FF
        vec_ref[row : row + FF, :] = g_down_ref[expert, :FF, :]
        row = ROW_DOWN_B + expert
        vec_ref[row : row + 1, :] = g_down_ref[expert, FF : FF + 1, :]
    core = scal_ref[0]
    own_at = pl.multiple_of(core * half, 8)
    other_at = pl.multiple_of((1 - core) * half, 8)
    for number in range(parts):
        tmp_ref[...] = take_shard(vec_ref, number, shard, 2 * half)
        own_ref[number] = tmp_ref[pl.ds(own_at, half), :]
        other_ref[number] = tmp_ref[pl.ds(other_at, half), :].astype(BF16)


def sample_backward_kernel(
    plan,
    scal_ref,
    msg_ref,
    func_ref,
    keys_hbm,
    vals_hbm,
    first_hbm,
    second_hbm,
    slope_one_hbm,
    slope_two_hbm,
    hid_ref,
    pair_ref,
    send_ref,
    kept_ref,
    vec_ref,
    left_keys_ref,
    left_vals_ref,
    keys_acc_ref,
    vals_acc_ref,
    g_pair_ref,
    g_hid_ref,
    g_in_ref,
    parts_ref,
    pairs_ref,
    seconds_ref,
    firsts_ref,
    starts,
    sems,
):
    tile, items, parts, shard, height, slots, steps = plan
    sources = (keys_hbm, vals_hbm, second_hbm, slope_two_hbm, first_hbm, slope_one_hbm)
    fetches = [
        [
            pltpu.make_async_copy(
                source.at[:, step * tile : (step + 1) * tile],
                kept_ref.at[number, :, step * tile : (step + 1) * tile],
                sems.at[number, step],
            )
            for number, source in enumerate(sources)
        ]
        for step in range(steps)
    ]
    for group in fetches:
        for fetch in group:
            fetch.start()

    def prepare():
        store_starts(lambda item: scal_ref[2 + items + item], starts, items)
        g_pair_ref[...] = jnp.zeros(g_pair_ref.shape, F32)
        g_hid_ref[...] = jnp.zeros(g_hid_ref.shape, F32)
        g_in_ref[...] = jnp.zeros(g_in_ref.shape, F32)
        mask = head_mask()
        low, high = item_span(
            starts, items, scal_ref[1] * slots, scal_ref[1] * slots + tile * steps
        )

        def build(item, carry):
            at = pl.multiple_of(item * HD, HD)
            block = spread_heads(msg_ref[pl.ds(at, HD), :], mask)
            left_vals_ref[item] = block.astype(BF16)
            row = msg_ref[pl.ds(items * HD + item, 1), :]
            both = jnp.concatenate([block, row, jnp.zeros((D - 1, D), F32)], axis=0)
            left_keys_ref[item] = jnp.transpose(both)[:, : D + 16].astype(BF16)
            return carry

        @pl.when(high <= low)
        def _():
            last = items - 1
            left_vals_ref[last] = jnp.zeros((D, D), BF16)
            left_keys_ref[last] = jnp.zeros((D, D + 16), BF16)

        lax.fori_loop(low, high, build, 0)

    def work(step):
        def part(number):
            return kept_ref.at[number, :, step * tile : (step + 1) * tile]

        keys_ref, vals_ref, second_ref, slope_two_ref, first_ref, slope_one_ref = (
            part(number) for number in range(6)
        )
        fetches[step][0].wait()
        fetches[step][1].wait()
        keys = keys_ref[...]
        ones = jnp.ones((16, tile), BF16)
        vals_ones = jnp.concatenate([vals_ref[...], ones], axis=0)
        begin = scal_ref[1] * slots + step * tile

        def visit(item, opening):
            row = item_row(starts, item, begin, tile)
            fresh_keys = row * dot_nn(left_keys_ref[item], vals_ones)
            fresh_vals = row * dot_nn(left_vals_ref[item], keys)
            keys_acc_ref[...] = fresh_keys if opening else keys_acc_ref[...] + fresh_keys
            vals_acc_ref[...] = fresh_vals if opening else vals_acc_ref[...] + fresh_vals

        over_items(starts, items, begin, tile, visit)
        samples = split_samples(func_ref[0, :, step * tile : (step + 1) * tile], parts_ref)
        for number in range(2, 6):
            fetches[step][number].wait()
        chunk = min(CHUNK, tile)

        def backward(start):
            at = slice(start, start + chunk)
            soft = keys_ref[:, at].astype(F32)
            grad_keys = keys_acc_ref[:, at]
            grad_in = soft * (grad_keys - head_sum(grad_keys * soft))
            grad_pair = jnp.concatenate([grad_in, vals_acc_ref[:, at]], axis=0).astype(BF16)
            pairs_ref[:, at] = grad_pair
            yield
            grad_second = dot_nn(pair_ref[...], grad_pair)
            yield
            grad_second = (slope_two_ref[:, at].astype(F32) * grad_second).astype(BF16)
            seconds_ref[:, at] = grad_second
            yield
            grad_first = dot_nn(hid_ref[...], grad_second)
            yield
            firsts_ref[:, at] = (slope_one_ref[:, at].astype(F32) * grad_first).astype(BF16)

        staggered([backward(start) for start in range(0, tile, chunk)])
        g_pair_ref[...] += dot_nt(second_ref[...], pairs_ref[...])
        first_ones = jnp.concatenate([first_ref[...], ones], axis=0)
        g_hid_ref[...] += dot_nt(first_ones, seconds_ref[...])
        g_in_ref[...] += dot_nt(samples, firsts_ref[...])

    prepare()
    for step in range(steps):
        work(step)
    vec_ref[BRANCH_ROWS:, :] = jnp.zeros((vec_ref.shape[0] - BRANCH_ROWS, LANES), F32)
    vec_ref[ROW_IN : ROW_IN + FIN, :] = (
        g_in_ref[0:FIN, :] + g_in_ref[FIN : 2 * FIN, :] + g_in_ref[2 * FIN : 3 * FIN, :]
    )
    vec_ref[ROW_IN_B : ROW_IN_B + 1, :] = g_in_ref[3 * FIN : 3 * FIN + 1, :]
    vec_ref[ROW_HID : ROW_HID + D + 1, :] = g_hid_ref[: D + 1, :]
    for part in range(2):
        vec_ref[pl.ds(ROW_PAIR + part, D, stride=2), :] = g_pair_ref[
            :, part * D : (part + 1) * D
        ]
    for number in range(parts):
        send_ref[number] = take_shard(vec_ref, number, shard, height).astype(BF16)


def sum_over_points(values, count, besides, early=3):
    bit = 1
    number = 0
    while bit < count:
        masks = [bit] if 2 * bit >= count else [bit, 2 * bit, 3 * bit]
        pieces = [
            lax.ppermute(values, "pts", [(source, source ^ mask) for source in range(count)])
            for mask in masks
        ]
        if number < len(besides):
            before = besides[number - 1] if number else None
            some = early if number else len(masks)
            pieces[:some], besides[number] = lax.optimization_barrier(
                (pieces[:some], besides[number](before))
            )
        values = functools.reduce(jnp.add, pieces, values)
        bit *= 4
        number += 1
    return values, besides


def copies(block, count):
    return jnp.broadcast_to(block, (count,) + block.shape)


def swap_cores(values):
    return lax.ppermute(values, "branch", [(0, 1), (1, 0)])


def whole(shape, kind=None):
    zeros = (0,) * len(shape)
    return pl.BlockSpec(shape, lambda *_: zeros)


def body(
    tokens,
    funcs,
    item_counts,
    func_counts,
    gate_ints,
    cotangent,
    shared_master,
    shared_m,
    shared_v,
    branch_master,
    branch_m,
    branch_v,
):
    count = lax.axis_size("pts")
    core = lax.axis_index("branch")
    items = item_counts.shape[0]
    place = jnp.stack([core, lax.axis_index("pts")]).astype(jnp.int32)
    chip_rows = tokens.shape[0]
    rows = chip_rows // 2
    slots = funcs.shape[2]
    shared_len = shared_master.shape[0]
    branch_len = branch_master.shape[1]
    half = up_to(-(-shared_len // (2 * LANES)), 16)
    height = up_to(-(-branch_len // LANES), 16)
    msg_rows = items * HD + up_to(items, 8)
    params = pltpu.CompilerParams(vmem_limit_bytes=VMEM_BASE + items * VMEM_ITEM)
    shape = jax.ShapeDtypeStruct

    shared_pad = jnp.pad(shared_master.astype(BF16), (0, 2 * half * LANES - shared_len))
    shared_half = lax.dynamic_slice_in_dim(shared_pad, core * (half * LANES), half * LANES, 0)
    branch_pad = jnp.pad(
        branch_master.astype(BF16), ((0, 0), (0, height * LANES - branch_len))
    )
    recv_branch = lax.all_to_all(copies(branch_pad.reshape(height, LANES), count), "pts", 0, 0)
    shared_send = copies(shared_half.reshape(half, LANES), count)
    recv_branch, shared_send = lax.optimization_barrier((recv_branch, shared_send))
    recv_shared = lax.all_to_all(shared_send, "pts", 0, 0)

    tile = min(SAMPLE_TILE, slots)
    steps = slots // tile
    stream = lambda height_: pl.BlockSpec((height_, tile), lambda i, *_: (0, i))
    vec_rows = up_to(BRANCH_ROWS + 2 * height + 8, 8)
    (
        msg,
        keys,
        vals,
        hid_w,
        pair_w,
        in_t,
        hid_t,
        hid_col,
    ) = pl.pallas_call(
        functools.partial(
            sample_forward_kernel, (tile, items, count, branch_len, height, slots)
        ),
        grid_spec=pltpu.PrefetchScalarGridSpec(
            num_scalar_prefetch=1,
            grid=(steps,),
            in_specs=[
                pl.BlockSpec(memory_space=pl.ANY),
                pl.BlockSpec((count, height, LANES), lambda i, *_: (0, 0, 0)),
                pl.BlockSpec((1, FIN, tile), lambda i, *_: (0, 0, i)),
            ],
            out_specs=[
                whole((msg_rows, LANES)),
                stream(D),
                stream(D),
                whole((D, D)),
                whole((D, 2 * D)),
                whole((D, 16)),
                whole((D, D)),
                whole((D, D)),
            ],
            scratch_shapes=[
                pltpu.VMEM((vec_rows, LANES), F32),
                pltpu.VMEM((8 + 2 * height, LANES), F32),
                pltpu.VMEM((16, tile), F32),
                pltpu.VMEM((2 * D, D), BF16),
                pltpu.VMEM((items, D + 16, D), F32),
                pltpu.SMEM((items + 1,), jnp.int32),
                pltpu.SMEM((1, items), jnp.int32),
                pltpu.SemaphoreType.DMA,
            ],
        ),
        out_shape=[
            pltpu.VMEM((msg_rows, LANES), F32),
            pltpu.HBM((D, slots), BF16),
            pltpu.HBM((D, slots), BF16),
            shape((D, D), BF16),
            shape((D, 2 * D), BF16),
            shape((D, 16), BF16),
            shape((D, D), BF16),
            shape((D, D), F32),
        ],
        compiler_params=params,
        cost_estimate=pl.CostEstimate(
            flops=slots * D * D * 10, bytes_accessed=slots * D * 12, transcendentals=slots * D * 3
        ),
        name="sample_forward",
    )(
        place,
        pltpu.with_memory_space_constraint(func_counts, pltpu.HBM),
        recv_branch,
        funcs,
    )
    in_t, place, item_counts, func_counts = lax.optimization_barrier(
        (in_t, place, item_counts, func_counts)
    )
    scal = jnp.concatenate([place, item_counts, func_counts.reshape(-1)])


    def make_slopes(start, stop, sources, given):
        return pl.pallas_call(
            slope_kernel,
            grid=(stop - start,),
            in_specs=[
                pl.BlockSpec((1, FIN, tile), lambda i: (0, 0, i + start)),
                whole((D, 16)),
                whole((D, D)),
                whole((D, D)),
            ]
            + [pl.BlockSpec(memory_space=pl.ANY)] * len(given),
            out_specs=[pl.BlockSpec((D, tile), lambda i: (0, i + start))] * 4,
            out_shape=[pltpu.HBM((D, slots), BF16)] * 4,
            scratch_shapes=[pltpu.VMEM((16, tile), F32)],
            input_output_aliases={4 + number: number for number in range(len(given))},
            compiler_params=params,
            cost_estimate=pl.CostEstimate(
                flops=4 << 30, bytes_accessed=slots * D * 4, transcendentals=slots * D
            ),
            name="slopes",
        )(*sources, *given)

    shared_rows = up_to(SHARED_ROWS + 2 * half + 8, 8)

    def make_weights(recv_shared, recv_other):
        return pl.pallas_call(
            functools.partial(weight_kernel, (count, shared_len, half)),
            in_specs=[
                pl.BlockSpec(memory_space=pltpu.SMEM),
                whole(recv_shared.shape),
                whole(recv_shared.shape),
            ],
            out_specs=[
                whole((D, D)),
                whole((D, D)),
                whole((D, D)),
                whole((D, D)),
                whole((E, D, FF)),
                whole((E, FF, D + 16)),
                whole((E, FF, D)),
                whole((E, D, FF)),
                whole((D, D)),
            ],
            out_shape=[
                shape((D, D), BF16),
                shape((D, D), BF16),
                shape((D, D), BF16),
                shape((D, D), BF16),
                shape((E, D, FF), BF16),
                shape((E, FF, D + 16), BF16),
                shape((E, FF, D), BF16),
                shape((E, D, FF), BF16),
                shape((D, D), F32),
            ],
            scratch_shapes=[
                pltpu.VMEM((shared_rows, LANES), F32),
                pltpu.VMEM((max(8 + 2 * half, D) + 8, LANES), F32),
            ],
            compiler_params=params,
            cost_estimate=pl.CostEstimate(flops=0, bytes_accessed=8 << 20, transcendentals=0),
            name="weights",
        )(scal, recv_shared, recv_other)

    token_tile = min(TOKEN_TILE, rows)
    token_steps = rows // token_tile
    row_block = pl.BlockSpec(
        (token_tile, D), lambda i, scal_ref: (scal_ref[0] * token_steps + i, 0)
    )
    token_stream = lambda height_: pl.BlockSpec((height_, token_tile), lambda i, *_: (0, i))

    def make_queries(weights):
        return pl.pallas_call(
            query_kernel,
            grid_spec=pltpu.PrefetchScalarGridSpec(
                num_scalar_prefetch=1,
                grid=(token_steps,),
                in_specs=[row_block, row_block, whole((D, D)), whole((D, D))],
                out_specs=[
                    token_stream(D),
                    token_stream(D),
                    token_stream(D),
                    token_stream(8),
                    token_stream(D),
                    token_stream(D),
                ],
            ),
            out_shape=[
                shape((D, rows), BF16),
                shape((D, rows), F32),
                shape((D, rows), F32),
                shape((8, rows), F32),
                shape((D, rows), BF16),
                shape((D, rows), F32),
            ],
            compiler_params=params,
            cost_estimate=pl.CostEstimate(
                flops=rows * D * D * 2, bytes_accessed=rows * D * 24, transcendentals=rows * D
            ),
            name="queries",
        )(scal, tokens, cotangent, weights[1], weights[8])

    sources = (funcs, in_t, hid_t, hid_col)
    cut = (steps + 1) // 2

    def beside_one(_):
        return swap_cores(recv_shared), recv_shared, make_slopes(0, cut, sources, ())

    def beside_two(ready):
        weights = make_weights(ready[1], ready[0])
        rest = make_slopes(cut, steps, sources, ready[2]) if cut < steps else ready[2]
        return weights, make_queries(weights), rest

    summary, (_, (weights, queries, slopes)) = sum_over_points(
        msg, count, [beside_one, beside_two]
    )
    query_w, query_t, out_w, out_t, up_w, up_t, down_w, down_t, cols = weights
    token_t, cot_t, unit, scale, norm, soft = queries
    summary_other = swap_cores(summary)
    first, second, slope_one, slope_two = slopes

    (
        output_own,
        grad_own,
        own_msg,
        other_msg,
        g_query,
        g_out,
        g_up,
        g_down,
        g_vec,
    ) = pl.pallas_call(
        functools.partial(token_kernel, (token_tile, items, chip_rows, token_steps)),
        grid_spec=pltpu.PrefetchScalarGridSpec(
            num_scalar_prefetch=1,
            grid=(token_steps,),
            in_specs=[
                whole((msg_rows, LANES)),
                whole((msg_rows, LANES)),
                pl.BlockSpec((E, token_tile), lambda i, scal_ref: (0, scal_ref[0] * token_steps + i)),
                token_stream(D),
                token_stream(D),
                token_stream(D),
                token_stream(8),
                token_stream(D),
                token_stream(D),
                whole((D, D)),
                whole((D, D)),
                whole((D, D)),
                whole((E, D, FF)),
                whole((E, FF, D + 16)),
                whole((E, FF, D)),
                whole((E, D, FF)),
                whole((D, D)),
            ],
            out_specs=[
                pl.BlockSpec((token_tile, D), lambda i, *_: (i, 0)),
                pl.BlockSpec((token_tile, D), lambda i, *_: (i, 0)),
                whole((msg_rows, LANES)),
                whole((msg_rows, LANES)),
                whole((D, D)),
                whole((D + 16, D)),
                whole((E, D + 16, FF)),
                whole((E, FF + 16, D)),
                whole((4, D, D)),
            ],
            scratch_shapes=[
                pltpu.VMEM((items, 4 * D, 2 * D), BF16),
                pltpu.VMEM((items, D, 4 * D), BF16),
                pltpu.VMEM((items, 4 * D, D), F32),
                pltpu.VMEM((4 * D, token_tile), F32),
                pltpu.VMEM((D, token_tile), F32),
                pltpu.VMEM((4 * D, token_tile), BF16),
                pltpu.SMEM((items + 1,), jnp.int32),
            ],
        ),
        out_shape=[
            shape((rows, D), BF16),
            shape((rows, D), F32),
            pltpu.VMEM((msg_rows, LANES), F32),
            pltpu.VMEM((msg_rows, LANES), F32),
            shape((D, D), F32),
            shape((D + 16, D), F32),
            shape((E, D + 16, FF), F32),
            shape((E, FF + 16, D), F32),
            shape((4, D, D), F32),
        ],
        compiler_params=params,
        cost_estimate=pl.CostEstimate(
            flops=rows * D * FF * 12 * E, bytes_accessed=rows * D * 24, transcendentals=rows * FF * E
        ),
        name="tokens",
    )(
        scal,
        summary,
        summary_other,
        gate_ints.T,
        token_t,
        cot_t,
        unit,
        scale,
        norm,
        soft,
        query_w,
        out_w,
        out_t,
        up_w,
        up_t,
        down_w,
        down_t,
        cols,
    )

    both_msg, parts = lax.optimization_barrier(
        (own_msg + swap_cores(other_msg), (g_query, g_out, g_up, g_down, g_vec))
    )
    half_own, half_other = pl.pallas_call(
        functools.partial(pack_kernel, (count, shared_len, half)),
        in_specs=[pl.BlockSpec(memory_space=pltpu.SMEM)]
        + [whole(piece.shape) for piece in parts],
        out_specs=[whole((count, half, LANES)), whole((count, half, LANES))],
        out_shape=[shape((count, half, LANES), F32), shape((count, half, LANES), BF16)],
        scratch_shapes=[
            pltpu.VMEM((shared_rows, LANES), F32),
            pltpu.VMEM((2 * half, LANES), F32),
        ],
        compiler_params=params,
        cost_estimate=pl.CostEstimate(flops=2 << 30, bytes_accessed=4 << 20, transcendentals=0),
        name="pack",
    )(scal, *parts)

    output_other = swap_cores(output_own)
    grad_other = swap_cores(grad_own)

    def add_halves(packed):
        half_sum = (packed[0] + swap_cores(packed[1]).astype(F32)).astype(BF16)
        return half_sum, output_other, grad_other

    summary_grad, (_, tail) = sum_over_points(
        both_msg, count, [lambda _: [half_own, half_other], add_halves], 1
    )
    half_sum, output_other, grad_other = tail
    keys, vals, first, second, slope_one, slope_two = (
        pltpu.with_memory_space_constraint(kept, pltpu.HBM)
        for kept in (keys, vals, first, second, slope_one, slope_two)
    )
    back_tile = min(BACK_TILE, slots)
    back_steps = slots // back_tile
    shared_recv = lax.all_to_all(half_sum, "pts", 0, 0)
    grads_send = pl.pallas_call(
        functools.partial(
            sample_backward_kernel,
            (back_tile, items, count, branch_len, height, slots, back_steps),
        ),
        grid_spec=pltpu.PrefetchScalarGridSpec(
            num_scalar_prefetch=1,
            grid=(1,),
            in_specs=[
                whole((msg_rows, LANES)),
                whole((1, FIN, slots)),
                pl.BlockSpec(memory_space=pl.ANY),
                pl.BlockSpec(memory_space=pl.ANY),
                pl.BlockSpec(memory_space=pl.ANY),
                pl.BlockSpec(memory_space=pl.ANY),
                pl.BlockSpec(memory_space=pl.ANY),
                pl.BlockSpec(memory_space=pl.ANY),
                whole((D, D)),
                whole((D, 2 * D)),
            ],
            out_specs=whole((count, height, LANES)),
            scratch_shapes=[
                pltpu.VMEM((6, D, slots), BF16),
                pltpu.VMEM((vec_rows, LANES), F32),
                pltpu.VMEM((items, D, D + 16), BF16),
                pltpu.VMEM((items, D, D), BF16),
                pltpu.VMEM((D, back_tile), F32),
                pltpu.VMEM((D, back_tile), F32),
                pltpu.VMEM((D, 2 * D), F32),
                pltpu.VMEM((D + 16, D), F32),
                pltpu.VMEM((16, D), F32),
                pltpu.VMEM((16, back_tile), F32),
                pltpu.VMEM((2 * D, back_tile), BF16),
                pltpu.VMEM((D, back_tile), BF16),
                pltpu.VMEM((D, back_tile), BF16),
                pltpu.SMEM((items + 1,), jnp.int32),
                pltpu.SemaphoreType.DMA((6, back_steps)),
            ],
        ),
        out_shape=shape((count, height, LANES), BF16),
        compiler_params=params,
        cost_estimate=pl.CostEstimate(
            flops=slots * D * D * 300, bytes_accessed=slots * D * 12, transcendentals=0
        ),
        name="sample_backward",
    )(
        scal,
        summary_grad,
        funcs,
        keys,
        vals,
        first,
        second,
        slope_one,
        slope_two,
        hid_w,
        pair_w,
    )

    grads_send, shared_recv, halves = lax.optimization_barrier(
        (grads_send, shared_recv, (output_own, output_other, grad_own, grad_other))
    )
    output_own, output_other, grad_own, grad_other = halves
    output = jnp.where(
        core == 0,
        jnp.concatenate([output_own, output_other]),
        jnp.concatenate([output_other, output_own]),
    )
    token_grad = jnp.where(
        core == 0,
        jnp.concatenate([grad_own, grad_other]),
        jnp.concatenate([grad_other, grad_own]),
    )
    own_half = jnp.sum(shared_recv.astype(F32), axis=0).reshape(-1)
    other_half = swap_cores(own_half)
    shared_grad = jnp.where(
        core == 0,
        jnp.concatenate([own_half, other_half]),
        jnp.concatenate([other_half, own_half]),
    )[:shared_len]
    branch_recv = lax.all_to_all(grads_send, "pts", 0, 0)
    branch_grad = jnp.sum(branch_recv.astype(F32), axis=0).reshape(1, -1)[:, :branch_len]
    new_branch, new_branch_m, new_branch_v = adam_step(
        branch_master, branch_m, branch_v, branch_grad
    )
    new_shared, new_shared_m, new_shared_v = adam_step(
        shared_master, shared_m, shared_v, shared_grad
    )
    return (
        output,
        token_grad,
        new_shared,
        new_shared_m,
        new_shared_v,
        new_branch,
        new_branch_m,
        new_branch_v,
    )


def solution(mesh):
    in_specs = (
        P("pts", None),
        P("branch", None, "pts"),
        P(),
        P("branch", None),
        P("pts", None),
        P("pts", None),
        P("pts"),
        P("pts"),
        P("pts"),
        P("branch", "pts"),
        P("branch", "pts"),
        P("branch", "pts"),
    )
    out_specs = (
        P("pts", None),
        P("pts", None),
        P("pts"),
        P("pts"),
        P("pts"),
        P("branch", "pts"),
        P("branch", "pts"),
        P("branch", "pts"),
    )
    return jax.shard_map(body, mesh=mesh, in_specs=in_specs, out_specs=out_specs, check_vma=False)
```

```python
import functools
import math

import jax
import jax.numpy as jnp
from jax import lax
from jax.experimental import pallas as pl
from jax.experimental.pallas import tpu as pltpu
from jax.sharding import PartitionSpec as P

D = 128
H = 8
HD = 16
FF = 256
E = 4
FIN = 3
STEP = 10

EPS_NORM = 1e-05
BETA_ONE = 0.9
BETA_TWO = 0.999
RATE_LEARN = 0.1
DECAY_RATE = 0.01
EPS_ADAM = 1e-08

LANES = 128
VMEM_BASE = 16 * 1024 * 1024
VMEM_ITEM = 768 * 1024
SAMPLE_TILE = 2048
BACK_TILE = 4096
TOKEN_TILE = 1024
CHUNK = 256

F32 = jnp.float32
BF16 = jnp.bfloat16

ROW_GAIN_ONE = 0
ROW_SHIFT_ONE = 1
ROW_QUERY = 2
ROW_OUT = ROW_QUERY + D
ROW_OUT_B = ROW_OUT + D
ROW_GAIN_TWO = ROW_OUT_B + 1
ROW_SHIFT_TWO = ROW_GAIN_TWO + 1
ROW_UP = ROW_SHIFT_TWO + 1
ROW_UP_B = ROW_UP + E * D * 2
ROW_DOWN = ROW_UP_B + E * 2
ROW_DOWN_B = ROW_DOWN + E * FF
SHARED_ROWS = ROW_DOWN_B + E

ROW_IN = 0
ROW_IN_B = ROW_IN + FIN
ROW_HID = ROW_IN_B + 1
ROW_HID_B = ROW_HID + D
ROW_PAIR = ROW_HID_B + 1
BRANCH_ROWS = ROW_PAIR + 2 * D

COL_GAIN_ONE = 0
COL_SHIFT_ONE = 1
COL_OUT_B = 2
COL_GAIN_TWO = 3
COL_SHIFT_TWO = 4
COL_UP_B = 5
COL_DOWN_B = COL_UP_B + 2 * E

TANH_C = math.sqrt(2.0 / math.pi)
TANH_CUBE = 0.044715


def up_to(amount, unit):
    return -(-amount // unit) * unit


def adam_step(master, moment_one, moment_two, grad):
    first = BETA_ONE * moment_one + (1.0 - BETA_ONE) * grad
    second = BETA_TWO * moment_two + (1.0 - BETA_TWO) * grad * grad
    first_hat = first / (1.0 - BETA_ONE**STEP)
    second_hat = second / (1.0 - BETA_TWO**STEP)
    fresh = master - RATE_LEARN * (
        first_hat / (jnp.sqrt(second_hat) + EPS_ADAM) + DECAY_RATE * master
    )
    return (fresh, first, second)


def dot_nn(left, right):
    return jnp.dot(left, right, preferred_element_type=F32)


def dot_nt(left, right):
    return lax.dot_general(left, right, (((1,), (1,)), ((), ())), preferred_element_type=F32)


def head_sum(values):
    split = values.reshape(H, HD, values.shape[1])
    total = jnp.sum(split, axis=1, keepdims=True)
    return jnp.broadcast_to(total, split.shape).reshape(values.shape)


def head_softmax(values):
    split = values.reshape(H, HD, values.shape[1])
    top = jnp.max(split, axis=1, keepdims=True)
    raised = jnp.exp(split - top)
    total = jnp.sum(raised, axis=1, keepdims=True)
    return (raised * (1.0 / total)).reshape(values.shape)


def gelu_value(inner):
    square = inner * inner
    bend = inner * (TANH_C + (TANH_C * TANH_CUBE) * square)
    return inner * (0.5 + 0.5 * jnp.tanh(bend))


def gelu_parts(inner):
    square = inner * inner
    bend = inner * (TANH_C + (TANH_C * TANH_CUBE) * square)
    gate = 0.5 + 0.5 * jnp.tanh(bend)
    rise = inner * (2.0 * TANH_C + (6.0 * TANH_C * TANH_CUBE) * square)
    return inner * gate, gate + (gate - gate * gate) * rise


def split_samples(funcs, parts_ref):
    high = funcs.astype(BF16).astype(F32)
    middle = (funcs - high).astype(BF16).astype(F32)
    parts_ref[0:FIN, :] = high
    parts_ref[FIN : 2 * FIN, :] = middle
    parts_ref[2 * FIN : 3 * FIN, :] = funcs - high - middle
    parts_ref[3 * FIN : 3 * FIN + 1, :] = jnp.ones((1, funcs.shape[1]), F32)
    parts_ref[3 * FIN + 1 :, :] = jnp.zeros((15 - 3 * FIN, funcs.shape[1]), F32)
    return parts_ref[...].astype(BF16)


def staggered(programs):
    waiting = list(programs)
    running = []
    while waiting or running:
        if waiting:
            running.append(waiting.pop(0))
        still = []
        for program in running:
            try:
                next(program)
                still.append(program)
            except StopIteration:
                pass
        running = still


def wide(tile, length):
    if length == tile.shape[1]:
        return tile
    return jnp.concatenate([tile] * (length // tile.shape[1]), axis=1)


def column(matrix, index, length):
    return jnp.broadcast_to(matrix[:, index : index + 1], (matrix.shape[0], length))


def fold_lanes(values):
    total = values[:, :LANES]
    for start in range(LANES, values.shape[1], LANES):
        total = total + values[:, start : start + LANES]
    return total


def lane_total_row(values):
    return jnp.sum(jnp.transpose(values), axis=0, keepdims=True)


def head_mask():
    row = lax.broadcasted_iota(jnp.int32, (D, D), 0) // HD
    col = lax.broadcasted_iota(jnp.int32, (D, D), 1) // HD
    return (row == col).astype(F32)


def fold_heads(values, mask):
    return jnp.sum((values * mask).reshape(H, HD, D), axis=0)


def spread_heads(compact, mask):
    return jnp.concatenate([compact] * H, axis=0) * mask


def store_starts(counts, starts, items):
    if items <= 8:
        total = jnp.int32(0)
        for item in range(items):
            starts[item] = total
            total = total + counts(item)
        starts[items] = total
    else:
        def step(item, total):
            starts[item] = total
            return total + counts(item)

        starts[items] = lax.fori_loop(0, items, step, jnp.int32(0))


def item_span(starts, items, begin, end):
    def step(item, span):
        low, high = span
        return (
            low + (starts[item + 1] <= begin).astype(jnp.int32),
            high + (starts[item] < end).astype(jnp.int32),
        )

    span = (jnp.int32(0), jnp.int32(0))
    if items <= 8:
        for item in range(items):
            span = step(item, span)
        return span
    return lax.fori_loop(0, items, step, span)


def item_row(starts, item, begin, length):
    position = begin + lax.broadcasted_iota(jnp.int32, (1, length), 1)
    return ((position >= starts[item]) & (position < starts[item + 1])).astype(F32)


def over_items(starts, items, begin, length, visit):
    low, high = item_span(starts, items, begin, begin + length)
    visit(jnp.minimum(low, items - 1), True)

    def step(item, carry):
        visit(item, False)
        return carry

    lax.fori_loop(low + 1, high, step, 0)


def over_parts(starts, item, begin, length, visit):
    width = min(256, length)
    for at in range(0, length, width):
        start = begin + at

        @pl.when((starts[item] < start + width) & (starts[item + 1] > start))
        def _(at=at, start=start):
            visit(slice(at, at + width), start)


def put_shard(vec_ref, tmp_ref, number, shard, height):
    row, shift = divmod(number * shard, LANES)
    touched = (shift + shard - 1) // LANES + 1
    if shift == 0:
        vec_ref[row : row + touched, :] = tmp_ref[8 : 8 + touched, :]
        return
    if number == 0:
        tmp_ref[7:8, :] = jnp.zeros((1, LANES), F32)
    else:
        tmp_ref[7:8, :] = vec_ref[row : row + 1, :]
    lane = lax.broadcasted_iota(jnp.int32, (touched, LANES), 1)
    vec_ref[row : row + touched, :] = jnp.where(
        lane >= shift, tmp_ref[8 : 8 + touched, :], tmp_ref[7 : 7 + touched, :]
    )


def turned(block, amount):
    amount = amount % LANES
    return block if amount == 0 else pltpu.roll(block, amount, 1)


def take_shard(vec_ref, number, shard, height):
    row, shift = divmod(number * shard, LANES)
    here = vec_ref[row : row + height, :]
    if shift == 0:
        return here
    after = vec_ref[row + 1 : row + 1 + height, :]
    lane = lax.broadcasted_iota(jnp.int32, (height, LANES), 1)
    return turned(jnp.where(lane >= shift, here, after), LANES - shift)


def sample_forward_kernel(
    plan,
    scal_ref,
    count_hbm,
    recv_ref,
    func_ref,
    msg_ref,
    keys_ref,
    vals_ref,
    hid_ref,
    pair_ref,
    in_t_ref,
    hid_t_ref,
    col_ref,
    vec_ref,
    tmp_ref,
    parts_ref,
    pair_t_ref,
    acc_ref,
    starts,
    count_ref,
    sem,
):
    tile, items, parts, shard, height, slots = plan
    step = pl.program_id(0)

    @pl.when(step == 0)
    def _():
        fetch = pltpu.make_async_copy(count_hbm, count_ref, sem)
        fetch.start()
        acc_ref[...] = jnp.zeros(acc_ref.shape, F32)
        for number in range(parts):
            shift = (number * shard) % LANES
            tmp_ref[8 : 8 + height, :] = turned(recv_ref[number].astype(F32), shift)
            put_shard(vec_ref, tmp_ref, number, shard, height)
        col_ref[...] = jnp.transpose(
            jnp.broadcast_to(vec_ref[ROW_HID_B : ROW_HID_B + 1, :], (D, D))
        )
        tmp_ref[0:16, :] = jnp.zeros((16, LANES), F32)
        for part in range(3):
            tmp_ref[part * FIN : (part + 1) * FIN, :] = vec_ref[ROW_IN : ROW_IN + FIN, :]
        tmp_ref[3 * FIN : 3 * FIN + 1, :] = vec_ref[ROW_IN_B : ROW_IN_B + 1, :]
        in_t_ref[...] = jnp.transpose(tmp_ref[0:16, :]).astype(BF16)
        hid = vec_ref[ROW_HID : ROW_HID + D, :]
        hid_ref[...] = hid.astype(BF16)
        hid_t_ref[...] = jnp.transpose(hid).astype(BF16)
        for part in range(2):
            piece = vec_ref[pl.ds(ROW_PAIR + part, D, stride=2), :]
            pair_ref[:, part * D : (part + 1) * D] = piece.astype(BF16)
            pair_t_ref[part * D : (part + 1) * D, :] = jnp.transpose(piece).astype(BF16)
        fetch.wait()
        store_starts(lambda item: count_ref[0, item], starts, items)

    samples = split_samples(func_ref[0], parts_ref)
    chunk = min(CHUNK, tile)

    def forward(start):
        at = slice(start, start + chunk)
        first_in = dot_nn(in_t_ref[...], samples[:, at])
        yield
        first = gelu_value(first_in).astype(BF16)
        yield
        second_in = dot_nn(hid_t_ref[...], first)
        yield
        second = gelu_value(second_in + wide(col_ref[...], chunk)).astype(BF16)
        yield
        pair = dot_nn(pair_t_ref[...], second)
        yield
        vals_ref[:, at] = pair[D:].astype(BF16)
        keys_ref[:, at] = head_softmax(pair[:D]).astype(BF16)

    staggered([forward(start) for start in range(0, tile, chunk)])
    keys = keys_ref[...]
    vals_ones = jnp.concatenate([vals_ref[...], jnp.ones((16, tile), BF16)], axis=0)
    begin = scal_ref[1] * slots + step * tile

    def visit(item, _):
        masked = keys * item_row(starts, item, begin, tile).astype(BF16)
        acc_ref[item] += dot_nt(vals_ones, masked)

    over_items(starts, items, begin, tile, visit)

    @pl.when(step == pl.num_programs(0) - 1)
    def _():
        mask = head_mask()
        msg_ref[items * HD :, :] = jnp.zeros((msg_ref.shape[0] - items * HD, LANES), F32)
        for item in range(items):
            msg_ref[item * HD : (item + 1) * HD, :] = fold_heads(acc_ref[item, :D, :], mask)
            msg_ref[items * HD + item : items * HD + item + 1, :] = acc_ref[item, D : D + 1, :]


def weight_kernel(
    plan,
    scal_ref,
    own_ref,
    other_ref,
    query_ref,
    query_t_ref,
    out_ref,
    out_t_ref,
    up_ref,
    up_t_ref,
    down_ref,
    down_t_ref,
    cols_ref,
    vec_ref,
    tmp_ref,
):
    parts, shard, half = plan
    core = scal_ref[0]
    own_at = pl.multiple_of(8 + core * half, 8)
    other_at = pl.multiple_of(8 + (1 - core) * half, 8)
    for number in range(parts):
        shift = (number * shard) % LANES
        tmp_ref[pl.ds(own_at, half), :] = turned(
            own_ref[number].astype(F32), shift
        )
        tmp_ref[pl.ds(other_at, half), :] = turned(
            other_ref[number].astype(F32), shift
        )
        put_shard(vec_ref, tmp_ref, number, shard, 2 * half)
    query = vec_ref[ROW_QUERY : ROW_QUERY + D, :]
    query_ref[...] = query.astype(BF16)
    query_t_ref[...] = jnp.transpose(query).astype(BF16)
    out = vec_ref[ROW_OUT : ROW_OUT + D, :]
    out_ref[...] = out.astype(BF16)
    out_t_ref[...] = jnp.transpose(out).astype(BF16)
    for expert in range(E):
        for part in range(2):
            up = vec_ref[pl.ds(ROW_UP + expert * 2 * D + part, D, stride=2), :]
            up_ref[expert, :, part * D : (part + 1) * D] = up.astype(BF16)
            up_t_ref[expert, part * D : (part + 1) * D, :D] = jnp.transpose(up).astype(BF16)
            row = ROW_DOWN + expert * FF + part * D
            down = vec_ref[row : row + D, :]
            down_ref[expert, part * D : (part + 1) * D, :] = down.astype(BF16)
            down_t_ref[expert, :, part * D : (part + 1) * D] = jnp.transpose(down).astype(BF16)
    tmp_ref[0:D, :] = jnp.zeros((D, LANES), F32)
    rows = [ROW_GAIN_ONE, ROW_SHIFT_ONE, ROW_OUT_B, ROW_GAIN_TWO, ROW_SHIFT_TWO]
    rows += [ROW_UP_B + number for number in range(2 * E)]
    rows += [ROW_DOWN_B + number for number in range(E)]
    for slot, row in enumerate(rows):
        tmp_ref[slot : slot + 1, :] = vec_ref[row : row + 1, :]
    cols = jnp.transpose(tmp_ref[0:D, :])
    cols_ref[...] = cols
    lane = lax.broadcasted_iota(jnp.int32, (D, 16), 1)
    for expert in range(E):
        for part in range(2):
            bias = jnp.where(lane == COL_UP_B + 2 * expert + part, cols[:, :16], 0.0)
            up_t_ref[expert, part * D : (part + 1) * D, D:] = bias.astype(BF16)


def norm_unit(values):
    centre = values - jnp.sum(values, axis=0, keepdims=True) * (1.0 / D)
    spread = jnp.sum(centre * centre, axis=0, keepdims=True) * (1.0 / D)
    scale = lax.rsqrt(spread + EPS_NORM)
    return centre * scale, scale


def norm_back(grad_unit, unit, scale):
    mean_one = jnp.sum(grad_unit, axis=0, keepdims=True) * (1.0 / D)
    mean_two = jnp.sum(grad_unit * unit, axis=0, keepdims=True) * (1.0 / D)
    return scale * (grad_unit - mean_one - unit * mean_two)


def query_kernel(
    scal_ref,
    token_ref,
    cot_ref,
    query_t_ref,
    cols_ref,
    token_t_ref,
    cot_t_ref,
    unit_ref,
    scale_ref,
    norm_ref,
    soft_ref,
):
    tokens = jnp.transpose(token_ref[...].astype(F32))
    length = tokens.shape[1]
    token_t_ref[...] = tokens.astype(BF16)
    cot_t_ref[...] = jnp.transpose(cot_ref[...])
    unit, scale = norm_unit(tokens)
    unit_ref[...] = unit
    scale_ref[...] = jnp.broadcast_to(scale, scale_ref.shape)
    cols = cols_ref[...]
    norm = (unit * column(cols, COL_GAIN_ONE, length) + column(cols, COL_SHIFT_ONE, length)).astype(
        BF16
    )
    norm_ref[...] = norm
    soft_ref[...] = head_softmax(dot_nn(query_t_ref[...], norm))


def token_kernel(
    plan,
    scal_ref,
    own_ref,
    other_ref,
    gate_ref,
    token_t_ref,
    cot_t_ref,
    unit_ref,
    scale_ref,
    norm_ref,
    soft_ref,
    query_ref,
    out_w_ref,
    out_t_ref,
    up_ref,
    up_t_ref,
    down_ref,
    down_t_ref,
    cols_ref,
    output_ref,
    grad_ref,
    own_msg_ref,
    other_msg_ref,
    g_query_ref,
    g_out_ref,
    g_up_ref,
    g_down_ref,
    g_vec_ref,
    left_ref,
    back_ref,
    acc_ref,
    mix_ref,
    pull_ref,
    grads_ref,
    starts,
):
    tile, items, slots, steps = plan
    step = pl.program_id(0)
    first_row = scal_ref[1] * slots + scal_ref[0] * (tile * steps)

    @pl.when(step == 0)
    def _():
        store_starts(lambda item: scal_ref[2 + item], starts, items)
        acc_ref[...] = jnp.zeros(acc_ref.shape, F32)
        g_query_ref[...] = jnp.zeros(g_query_ref.shape, F32)
        g_out_ref[...] = jnp.zeros(g_out_ref.shape, F32)
        g_up_ref[...] = jnp.zeros(g_up_ref.shape, F32)
        g_down_ref[...] = jnp.zeros(g_down_ref.shape, F32)
        g_vec_ref[...] = jnp.zeros(g_vec_ref.shape, F32)
        mask = head_mask()
        low, high = item_span(starts, items, first_row, first_row + tile * steps)

        def build(item, carry):
            at = pl.multiple_of(item * HD, HD)
            for slot, source in enumerate((own_ref, other_ref)):
                block = spread_heads(source[pl.ds(at, HD), :], mask)
                total = source[pl.ds(items * HD + item, 1), :] * mask
                for kind, piece in enumerate((block, total)):
                    row = (2 * kind + slot) * D
                    high_part = piece.astype(BF16)
                    left_ref[item, row : row + D, :D] = high_part
                    left_ref[item, row : row + D, D:] = (piece - high_part.astype(F32)).astype(BF16)
                    turned_piece = jnp.transpose(piece)
                    if kind == 1:
                        turned_piece = turned_piece * (1.0 / HD)
                    back_ref[item, :, row : row + D] = turned_piece.astype(BF16)
            return carry

        lax.fori_loop(low, high, build, 0)

    cols = cols_ref[...]
    begin = first_row + step * tile
    soft = soft_ref[...]

    def attend(item, lanes, start):
        length = lanes.stop - lanes.start
        masked = soft_ref[:, lanes].astype(BF16) * item_row(starts, item, start, length).astype(BF16)
        return dot_nn(left_ref[item], jnp.concatenate([masked, masked], axis=0))

    def forward(item, opening):
        if opening:
            mix_ref[...] = attend(item, slice(0, tile), begin)
            return

        def add(lanes, start):
            mix_ref[:, lanes] += attend(item, lanes, start)

        over_parts(starts, item, begin, tile, add)

    over_items(starts, items, begin, tile, forward)
    numer_one, numer_two = mix_ref[:D, :], mix_ref[D : 2 * D, :]
    inv_one, inv_two = 1.0 / mix_ref[2 * D : 3 * D, :], 1.0 / mix_ref[3 * D :, :]
    own_one, own_two = numer_one * inv_one, numer_two * inv_two
    attended = (0.5 * (own_one + own_two)).astype(BF16)
    cot = cot_t_ref[...]
    residual = (
        token_t_ref[...].astype(F32)
        + dot_nn(out_t_ref[...], attended)
        + column(cols, COL_OUT_B, tile)
    )
    unit, scale = norm_unit(residual)
    gain_two = column(cols, COL_GAIN_TWO, tile)
    norm = (unit * gain_two + column(cols, COL_SHIFT_TWO, tile)).astype(BF16)
    ones = jnp.ones((16, tile), BF16)
    norm_ones = jnp.concatenate([norm, ones], axis=0)
    gates = gate_ref[...].astype(F32)
    gates = gates / jnp.sum(gates, axis=0, keepdims=True)
    mixture = residual
    grad_norm = jnp.zeros((D, tile), F32)
    for expert in range(E):
        inner = dot_nn(up_t_ref[expert], norm_ones)
        active, slope = gelu_parts(inner)
        active = active.astype(BF16)
        result = dot_nn(down_t_ref[expert], active) + column(cols, COL_DOWN_B + expert, tile)
        gate = gates[expert : expert + 1, :]
        mixture = mixture + gate * result
        grad_result = (gate * cot).astype(BF16)
        g_down_ref[expert] += dot_nt(jnp.concatenate([active, ones], axis=0), grad_result)
        grad_inner = (slope * dot_nn(down_ref[expert], grad_result)).astype(BF16)
        g_up_ref[expert] += dot_nt(norm_ones, grad_inner)
        grad_norm = grad_norm + dot_nn(up_ref[expert], grad_inner)
    output_ref[...] = jnp.transpose(mixture).astype(BF16)
    g_vec_ref[2] += fold_lanes(grad_norm * unit)
    g_vec_ref[3] += fold_lanes(grad_norm)
    grad_residual = cot + norm_back(grad_norm * gain_two, unit, scale)
    grad_proj = grad_residual.astype(BF16)
    g_out_ref[...] += dot_nt(jnp.concatenate([attended, ones], axis=0), grad_proj)
    grad_own = 0.5 * dot_nn(out_w_ref[...], grad_proj)
    grad_one, grad_two = grad_own * inv_one, grad_own * inv_two
    sum_one = -head_sum(grad_one * own_one)
    sum_two = -head_sum(grad_two * own_two)
    grads = jnp.concatenate([grad_one, grad_two, sum_one, sum_two], axis=0).astype(BF16)

    grads_ref[...] = grads

    def pull_back(item, lanes, start):
        length = lanes.stop - lanes.start
        row = item_row(starts, item, start, length)
        part = grads_ref[:, lanes]
        masked = soft_ref[:, lanes].astype(BF16) * row.astype(BF16)
        return dot_nt(part, masked), row * dot_nn(back_ref[item], part)

    def backward(item, opening):
        if opening:
            sums, pull_ref[...] = pull_back(item, slice(0, tile), begin)
            acc_ref[item] += sums
            return

        def add(lanes, start):
            sums, pull = pull_back(item, lanes, start)
            acc_ref[item] += sums
            pull_ref[:, lanes] += pull

        over_parts(starts, item, begin, tile, add)

    over_items(starts, items, begin, tile, backward)
    pull = pull_ref[...]
    grad_query = (soft * (pull - head_sum(pull * soft))).astype(BF16)
    g_query_ref[...] += dot_nt(norm_ref[...], grad_query)
    grad_norm_one = dot_nn(query_ref[...], grad_query)
    unit_one = unit_ref[...]
    g_vec_ref[0] += fold_lanes(grad_norm_one * unit_one)
    g_vec_ref[1] += fold_lanes(grad_norm_one)
    grad_token = grad_residual + norm_back(
        grad_norm_one * column(cols, COL_GAIN_ONE, tile), unit_one, scale_ref[0:1, :]
    )
    grad_ref[...] = jnp.transpose(grad_token)

    @pl.when(step == steps - 1)
    def _():
        mask = head_mask()
        for slot, target in enumerate((own_msg_ref, other_msg_ref)):
            target[items * HD :, :] = jnp.zeros((target.shape[0] - items * HD, LANES), F32)
            for item in range(items):
                full = acc_ref[item, slot * D : (slot + 1) * D, :]
                target[item * HD : (item + 1) * HD, :] = fold_heads(full, mask)
                sums = acc_ref[item, (2 + slot) * D : (3 + slot) * D, :]
                target[items * HD + item : items * HD + item + 1, :] = fold_heads(sums, mask)[0:1]


def pack_kernel(
    plan,
    scal_ref,
    g_query_ref,
    g_out_ref,
    g_up_ref,
    g_down_ref,
    g_vec_ref,
    own_ref,
    other_ref,
    vec_ref,
    tmp_ref,
):
    parts, shard, half = plan
    vec_ref[SHARED_ROWS:, :] = jnp.zeros((vec_ref.shape[0] - SHARED_ROWS, LANES), F32)
    for slot, row in enumerate((ROW_GAIN_ONE, ROW_SHIFT_ONE, ROW_GAIN_TWO, ROW_SHIFT_TWO)):
        vec_ref[row : row + 1, :] = lane_total_row(g_vec_ref[slot])
    vec_ref[ROW_QUERY : ROW_QUERY + D, :] = g_query_ref[...]
    vec_ref[ROW_OUT : ROW_OUT + D + 1, :] = g_out_ref[: D + 1, :]
    for expert in range(E):
        for part in range(2):
            columns = slice(part * D, (part + 1) * D)
            vec_ref[pl.ds(ROW_UP + expert * 2 * D + part, D, stride=2), :] = g_up_ref[
                expert, :D, columns
            ]
            row = ROW_UP_B + 2 * expert + part
            vec_ref[row : row + 1, :] = g_up_ref[expert, D : D + 1, columns]
        row = ROW_DOWN + expert * FF
        vec_ref[row : row + FF, :] = g_down_ref[expert, :FF, :]
        row = ROW_DOWN_B + expert
        vec_ref[row : row + 1, :] = g_down_ref[expert, FF : FF + 1, :]
    core = scal_ref[0]
    own_at = pl.multiple_of(core * half, 8)
    other_at = pl.multiple_of((1 - core) * half, 8)
    for number in range(parts):
        tmp_ref[...] = take_shard(vec_ref, number, shard, 2 * half)
        own_ref[number] = tmp_ref[pl.ds(own_at, half), :]
        other_ref[number] = tmp_ref[pl.ds(other_at, half), :].astype(BF16)


def sample_backward_kernel(
    plan,
    scal_ref,
    msg_ref,
    func_ref,
    keys_hbm,
    vals_hbm,
    in_t_ref,
    hid_t_ref,
    col_ref,
    hid_ref,
    pair_ref,
    send_ref,
    kept_ref,
    vec_ref,
    left_keys_ref,
    left_vals_ref,
    keys_acc_ref,
    vals_acc_ref,
    g_pair_ref,
    g_hid_ref,
    g_in_ref,
    parts_ref,
    pairs_ref,
    seconds_ref,
    firsts_ref,
    first_ref,
    second_ref,
    starts,
    sems,
):
    tile, items, parts, shard, height, slots, steps = plan
    sources = (keys_hbm, vals_hbm)
    fetches = [
        [
            pltpu.make_async_copy(
                source.at[:, step * tile : (step + 1) * tile],
                kept_ref.at[number, :, step * tile : (step + 1) * tile],
                sems.at[number, step],
            )
            for number, source in enumerate(sources)
        ]
        for step in range(steps)
    ]
    for group in fetches:
        for fetch in group:
            fetch.start()

    def prepare():
        store_starts(lambda item: scal_ref[2 + items + item], starts, items)
        g_pair_ref[...] = jnp.zeros(g_pair_ref.shape, F32)
        g_hid_ref[...] = jnp.zeros(g_hid_ref.shape, F32)
        g_in_ref[...] = jnp.zeros(g_in_ref.shape, F32)
        mask = head_mask()
        low, high = item_span(
            starts, items, scal_ref[1] * slots, scal_ref[1] * slots + tile * steps
        )

        def build(item, carry):
            at = pl.multiple_of(item * HD, HD)
            block = spread_heads(msg_ref[pl.ds(at, HD), :], mask)
            left_vals_ref[item] = block.astype(BF16)
            row = msg_ref[pl.ds(items * HD + item, 1), :]
            both = jnp.concatenate([block, row, jnp.zeros((D - 1, D), F32)], axis=0)
            left_keys_ref[item] = jnp.transpose(both)[:, : D + 16].astype(BF16)
            return carry

        @pl.when(high <= low)
        def _():
            last = items - 1
            left_vals_ref[last] = jnp.zeros((D, D), BF16)
            left_keys_ref[last] = jnp.zeros((D, D + 16), BF16)

        lax.fori_loop(low, high, build, 0)

    def work(step):
        def part(number):
            return kept_ref.at[number, :, step * tile : (step + 1) * tile]

        keys_ref, vals_ref = part(0), part(1)
        fetches[step][0].wait()
        fetches[step][1].wait()
        keys = keys_ref[...]
        ones = jnp.ones((16, tile), BF16)
        vals_ones = jnp.concatenate([vals_ref[...], ones], axis=0)
        begin = scal_ref[1] * slots + step * tile

        def visit(item, opening):
            row = item_row(starts, item, begin, tile)
            fresh_keys = row * dot_nn(left_keys_ref[item], vals_ones)
            fresh_vals = row * dot_nn(left_vals_ref[item], keys)
            keys_acc_ref[...] = fresh_keys if opening else keys_acc_ref[...] + fresh_keys
            vals_acc_ref[...] = fresh_vals if opening else vals_acc_ref[...] + fresh_vals

        over_items(starts, items, begin, tile, visit)
        samples = split_samples(func_ref[0, :, step * tile : (step + 1) * tile], parts_ref)
        chunk = min(CHUNK, tile)

        def backward(start):
            at = slice(start, start + chunk)
            first_in = dot_nn(in_t_ref[...], samples[:, at])
            yield
            first, slope_one = gelu_parts(first_in)
            first = first.astype(BF16)
            first_ref[:, at] = first
            yield
            second_in = dot_nn(hid_t_ref[...], first)
            yield
            second, slope_two = gelu_parts(second_in + wide(col_ref[...], chunk))
            second_ref[:, at] = second.astype(BF16)
            soft = keys_ref[:, at].astype(F32)
            grad_keys = keys_acc_ref[:, at]
            grad_in = soft * (grad_keys - head_sum(grad_keys * soft))
            grad_pair = jnp.concatenate([grad_in, vals_acc_ref[:, at]], axis=0).astype(BF16)
            pairs_ref[:, at] = grad_pair
            yield
            grad_second = dot_nn(pair_ref[...], grad_pair)
            yield
            grad_second = (slope_two * grad_second).astype(BF16)
            seconds_ref[:, at] = grad_second
            yield
            grad_first = dot_nn(hid_ref[...], grad_second)
            yield
            firsts_ref[:, at] = (slope_one * grad_first).astype(BF16)

        staggered([backward(start) for start in range(0, tile, chunk)])
        g_pair_ref[...] += dot_nt(second_ref[...], pairs_ref[...])
        first_ones = jnp.concatenate([first_ref[...], ones], axis=0)
        g_hid_ref[...] += dot_nt(first_ones, seconds_ref[...])
        g_in_ref[...] += dot_nt(samples, firsts_ref[...])

    prepare()
    for step in range(steps):
        work(step)
    vec_ref[BRANCH_ROWS:, :] = jnp.zeros((vec_ref.shape[0] - BRANCH_ROWS, LANES), F32)
    vec_ref[ROW_IN : ROW_IN + FIN, :] = (
        g_in_ref[0:FIN, :] + g_in_ref[FIN : 2 * FIN, :] + g_in_ref[2 * FIN : 3 * FIN, :]
    )
    vec_ref[ROW_IN_B : ROW_IN_B + 1, :] = g_in_ref[3 * FIN : 3 * FIN + 1, :]
    vec_ref[ROW_HID : ROW_HID + D + 1, :] = g_hid_ref[: D + 1, :]
    for part in range(2):
        vec_ref[pl.ds(ROW_PAIR + part, D, stride=2), :] = g_pair_ref[
            :, part * D : (part + 1) * D
        ]
    for number in range(parts):
        send_ref[number] = take_shard(vec_ref, number, shard, height).astype(BF16)


def sum_over_points(values, count, besides, early):
    bit = 1
    number = 0
    while bit < count:
        masks = [bit] if 2 * bit >= count else [bit, 2 * bit, 3 * bit]
        pieces = [
            lax.ppermute(values, "pts", [(source, source ^ mask) for source in range(count)])
            for mask in masks
        ]
        if number < len(besides):
            some = early[number]
            before = besides[number - 1] if number else None
            pieces[some], besides[number] = lax.optimization_barrier(
                (pieces[some], besides[number](before))
            )
        values = functools.reduce(jnp.add, pieces, values)
        bit *= 4
        number += 1
    return values, besides


def copies(block, count):
    return jnp.broadcast_to(block, (count,) + block.shape)


def swap_cores(values):
    return lax.ppermute(values, "branch", [(0, 1), (1, 0)])


def whole(shape, kind=None):
    zeros = (0,) * len(shape)
    return pl.BlockSpec(shape, lambda *_: zeros)


def body(
    tokens,
    funcs,
    item_counts,
    func_counts,
    gate_ints,
    cotangent,
    shared_master,
    shared_m,
    shared_v,
    branch_master,
    branch_m,
    branch_v,
):
    count = lax.axis_size("pts")
    core = lax.axis_index("branch")
    items = item_counts.shape[0]
    place = jnp.stack([core, lax.axis_index("pts")]).astype(jnp.int32)
    chip_rows = tokens.shape[0]
    rows = chip_rows // 2
    slots = funcs.shape[2]
    shared_len = shared_master.shape[0]
    branch_len = branch_master.shape[1]
    half = up_to(-(-shared_len // (2 * LANES)), 16)
    height = up_to(-(-branch_len // LANES), 16)
    msg_rows = items * HD + up_to(items, 8)
    params = pltpu.CompilerParams(vmem_limit_bytes=VMEM_BASE + items * VMEM_ITEM)
    shape = jax.ShapeDtypeStruct

    shared_pad = jnp.pad(shared_master.astype(BF16), (0, 2 * half * LANES - shared_len))
    shared_half = lax.dynamic_slice_in_dim(shared_pad, core * (half * LANES), half * LANES, 0)
    branch_pad = jnp.pad(
        branch_master.astype(BF16), ((0, 0), (0, height * LANES - branch_len))
    )
    recv_branch = lax.all_to_all(copies(branch_pad.reshape(height, LANES), count), "pts", 0, 0)
    shared_send = copies(shared_half.reshape(half, LANES), count)
    recv_branch, shared_send = lax.optimization_barrier((recv_branch, shared_send))
    recv_shared = lax.all_to_all(shared_send, "pts", 0, 0)

    tile = min(SAMPLE_TILE, slots)
    steps = slots // tile
    stream = lambda height_: pl.BlockSpec((height_, tile), lambda i, *_: (0, i))
    vec_rows = up_to(BRANCH_ROWS + 2 * height + 8, 8)
    (
        msg,
        keys,
        vals,
        hid_w,
        pair_w,
        in_t,
        hid_t,
        hid_col,
    ) = pl.pallas_call(
        functools.partial(
            sample_forward_kernel, (tile, items, count, branch_len, height, slots)
        ),
        grid_spec=pltpu.PrefetchScalarGridSpec(
            num_scalar_prefetch=1,
            grid=(steps,),
            in_specs=[
                pl.BlockSpec(memory_space=pl.ANY),
                pl.BlockSpec((count, height, LANES), lambda i, *_: (0, 0, 0)),
                pl.BlockSpec((1, FIN, tile), lambda i, *_: (0, 0, i)),
            ],
            out_specs=[
                whole((msg_rows, LANES)),
                stream(D),
                stream(D),
                whole((D, D)),
                whole((D, 2 * D)),
                whole((D, 16)),
                whole((D, D)),
                whole((D, D)),
            ],
            scratch_shapes=[
                pltpu.VMEM((vec_rows, LANES), F32),
                pltpu.VMEM((8 + 2 * height, LANES), F32),
                pltpu.VMEM((16, tile), F32),
                pltpu.VMEM((2 * D, D), BF16),
                pltpu.VMEM((items, D + 16, D), F32),
                pltpu.SMEM((items + 1,), jnp.int32),
                pltpu.SMEM((1, items), jnp.int32),
                pltpu.SemaphoreType.DMA,
            ],
        ),
        out_shape=[
            pltpu.VMEM((msg_rows, LANES), F32),
            pltpu.HBM((D, slots), BF16),
            pltpu.HBM((D, slots), BF16),
            shape((D, D), BF16),
            shape((D, 2 * D), BF16),
            shape((D, 16), BF16),
            shape((D, D), BF16),
            shape((D, D), F32),
        ],
        compiler_params=params,
        cost_estimate=pl.CostEstimate(
            flops=slots * D * D * 10, bytes_accessed=slots * D * 12, transcendentals=slots * D * 3
        ),
        name="sample_forward",
    )(
        place,
        pltpu.with_memory_space_constraint(func_counts, pltpu.HBM),
        recv_branch,
        funcs,
    )
    in_t, place, item_counts, func_counts = lax.optimization_barrier(
        (in_t, place, item_counts, func_counts)
    )
    scal = jnp.concatenate([place, item_counts, func_counts.reshape(-1)])


    shared_rows = up_to(SHARED_ROWS + 2 * half + 8, 8)

    def make_weights(recv_shared, recv_other):
        return pl.pallas_call(
            functools.partial(weight_kernel, (count, shared_len, half)),
            in_specs=[
                pl.BlockSpec(memory_space=pltpu.SMEM),
                whole(recv_shared.shape),
                whole(recv_shared.shape),
            ],
            out_specs=[
                whole((D, D)),
                whole((D, D)),
                whole((D, D)),
                whole((D, D)),
                whole((E, D, FF)),
                whole((E, FF, D + 16)),
                whole((E, FF, D)),
                whole((E, D, FF)),
                whole((D, D)),
            ],
            out_shape=[
                shape((D, D), BF16),
                shape((D, D), BF16),
                shape((D, D), BF16),
                shape((D, D), BF16),
                shape((E, D, FF), BF16),
                shape((E, FF, D + 16), BF16),
                shape((E, FF, D), BF16),
                shape((E, D, FF), BF16),
                shape((D, D), F32),
            ],
            scratch_shapes=[
                pltpu.VMEM((shared_rows, LANES), F32),
                pltpu.VMEM((max(8 + 2 * half, D) + 8, LANES), F32),
            ],
            compiler_params=params,
            cost_estimate=pl.CostEstimate(flops=0, bytes_accessed=8 << 20, transcendentals=0),
            name="weights",
        )(scal, recv_shared, recv_other)

    token_tile = min(TOKEN_TILE, rows)
    token_steps = rows // token_tile
    row_block = pl.BlockSpec(
        (token_tile, D), lambda i, scal_ref: (scal_ref[0] * token_steps + i, 0)
    )
    token_stream = lambda height_: pl.BlockSpec((height_, token_tile), lambda i, *_: (0, i))

    def make_queries(weights):
        return pl.pallas_call(
            query_kernel,
            grid_spec=pltpu.PrefetchScalarGridSpec(
                num_scalar_prefetch=1,
                grid=(token_steps,),
                in_specs=[row_block, row_block, whole((D, D)), whole((D, D))],
                out_specs=[
                    token_stream(D),
                    token_stream(D),
                    token_stream(D),
                    token_stream(8),
                    token_stream(D),
                    token_stream(D),
                ],
            ),
            out_shape=[
                shape((D, rows), BF16),
                shape((D, rows), F32),
                shape((D, rows), F32),
                shape((8, rows), F32),
                shape((D, rows), BF16),
                shape((D, rows), F32),
            ],
            compiler_params=params,
            cost_estimate=pl.CostEstimate(
                flops=rows * D * D * 2, bytes_accessed=rows * D * 24, transcendentals=rows * D
            ),
            name="queries",
        )(scal, tokens, cotangent, weights[1], weights[8])

    def beside_two(received):
        weights = make_weights(received, swap_cores(received))
        return weights, make_queries(weights)

    summary, (_, (weights, queries)) = sum_over_points(
        msg, count, [lambda _: recv_shared, beside_two], (slice(1), slice(3))
    )
    query_w, query_t, out_w, out_t, up_w, up_t, down_w, down_t, cols = weights
    token_t, cot_t, unit, scale, norm, soft = queries
    summary_other = swap_cores(summary)

    (
        output_own,
        grad_own,
        own_msg,
        other_msg,
        g_query,
        g_out,
        g_up,
        g_down,
        g_vec,
    ) = pl.pallas_call(
        functools.partial(token_kernel, (token_tile, items, chip_rows, token_steps)),
        grid_spec=pltpu.PrefetchScalarGridSpec(
            num_scalar_prefetch=1,
            grid=(token_steps,),
            in_specs=[
                whole((msg_rows, LANES)),
                whole((msg_rows, LANES)),
                pl.BlockSpec((E, token_tile), lambda i, scal_ref: (0, scal_ref[0] * token_steps + i)),
                token_stream(D),
                token_stream(D),
                token_stream(D),
                token_stream(8),
                token_stream(D),
                token_stream(D),
                whole((D, D)),
                whole((D, D)),
                whole((D, D)),
                whole((E, D, FF)),
                whole((E, FF, D + 16)),
                whole((E, FF, D)),
                whole((E, D, FF)),
                whole((D, D)),
            ],
            out_specs=[
                pl.BlockSpec((token_tile, D), lambda i, *_: (i, 0)),
                pl.BlockSpec((token_tile, D), lambda i, *_: (i, 0)),
                whole((msg_rows, LANES)),
                whole((msg_rows, LANES)),
                whole((D, D)),
                whole((D + 16, D)),
                whole((E, D + 16, FF)),
                whole((E, FF + 16, D)),
                whole((4, D, D)),
            ],
            scratch_shapes=[
                pltpu.VMEM((items, 4 * D, 2 * D), BF16),
                pltpu.VMEM((items, D, 4 * D), BF16),
                pltpu.VMEM((items, 4 * D, D), F32),
                pltpu.VMEM((4 * D, token_tile), F32),
                pltpu.VMEM((D, token_tile), F32),
                pltpu.VMEM((4 * D, token_tile), BF16),
                pltpu.SMEM((items + 1,), jnp.int32),
            ],
        ),
        out_shape=[
            shape((rows, D), BF16),
            shape((rows, D), F32),
            pltpu.VMEM((msg_rows, LANES), F32),
            pltpu.VMEM((msg_rows, LANES), F32),
            shape((D, D), F32),
            shape((D + 16, D), F32),
            shape((E, D + 16, FF), F32),
            shape((E, FF + 16, D), F32),
            shape((4, D, D), F32),
        ],
        compiler_params=params,
        cost_estimate=pl.CostEstimate(
            flops=rows * D * FF * 12 * E, bytes_accessed=rows * D * 24, transcendentals=rows * FF * E
        ),
        name="tokens",
    )(
        scal,
        summary,
        summary_other,
        gate_ints.T,
        token_t,
        cot_t,
        unit,
        scale,
        norm,
        soft,
        query_w,
        out_w,
        out_t,
        up_w,
        up_t,
        down_w,
        down_t,
        cols,
    )

    both_msg, parts = lax.optimization_barrier(
        (own_msg + swap_cores(other_msg), (g_query, g_out, g_up, g_down, g_vec))
    )
    half_own, half_other = pl.pallas_call(
        functools.partial(pack_kernel, (count, shared_len, half)),
        in_specs=[pl.BlockSpec(memory_space=pltpu.SMEM)]
        + [whole(piece.shape) for piece in parts],
        out_specs=[whole((count, half, LANES)), whole((count, half, LANES))],
        out_shape=[shape((count, half, LANES), F32), shape((count, half, LANES), BF16)],
        scratch_shapes=[
            pltpu.VMEM((shared_rows, LANES), F32),
            pltpu.VMEM((2 * half, LANES), F32),
        ],
        compiler_params=params,
        cost_estimate=pl.CostEstimate(flops=2 << 30, bytes_accessed=4 << 20, transcendentals=0),
        name="pack",
    )(scal, *parts)

    output_other = swap_cores(output_own)
    grad_other = swap_cores(grad_own)

    def add_halves(packed):
        half_sum = (packed[0] + swap_cores(packed[1]).astype(F32)).astype(BF16)
        return half_sum, output_other, grad_other

    summary_grad, (_, tail) = sum_over_points(
        both_msg, count, [lambda _: [half_own, half_other], add_halves], (slice(3), slice(2, 3))
    )
    half_sum, output_other, grad_other = tail
    keys, vals = (pltpu.with_memory_space_constraint(kept, pltpu.HBM) for kept in (keys, vals))
    back_tile = min(BACK_TILE, slots)
    back_steps = slots // back_tile
    shared_recv = lax.all_to_all(half_sum, "pts", 0, 0)
    grads_send = pl.pallas_call(
        functools.partial(
            sample_backward_kernel,
            (back_tile, items, count, branch_len, height, slots, back_steps),
        ),
        grid_spec=pltpu.PrefetchScalarGridSpec(
            num_scalar_prefetch=1,
            grid=(1,),
            in_specs=[
                whole((msg_rows, LANES)),
                whole((1, FIN, slots)),
                pl.BlockSpec(memory_space=pl.ANY),
                pl.BlockSpec(memory_space=pl.ANY),
                whole((D, 16)),
                whole((D, D)),
                whole((D, D)),
                whole((D, D)),
                whole((D, 2 * D)),
            ],
            out_specs=whole((count, height, LANES)),
            scratch_shapes=[
                pltpu.VMEM((2, D, slots), BF16),
                pltpu.VMEM((vec_rows, LANES), F32),
                pltpu.VMEM((items, D, D + 16), BF16),
                pltpu.VMEM((items, D, D), BF16),
                pltpu.VMEM((D, back_tile), F32),
                pltpu.VMEM((D, back_tile), F32),
                pltpu.VMEM((D, 2 * D), F32),
                pltpu.VMEM((D + 16, D), F32),
                pltpu.VMEM((16, D), F32),
                pltpu.VMEM((16, back_tile), F32),
                pltpu.VMEM((2 * D, back_tile), BF16),
                pltpu.VMEM((D, back_tile), BF16),
                pltpu.VMEM((D, back_tile), BF16),
                pltpu.VMEM((D, back_tile), BF16),
                pltpu.VMEM((D, back_tile), BF16),
                pltpu.SMEM((items + 1,), jnp.int32),
                pltpu.SemaphoreType.DMA((2, back_steps)),
            ],
        ),
        out_shape=shape((count, height, LANES), BF16),
        compiler_params=pltpu.CompilerParams(
            vmem_limit_bytes=2 * VMEM_BASE + items * VMEM_ITEM
        ),
        cost_estimate=pl.CostEstimate(
            flops=slots * D * D * 300, bytes_accessed=slots * D * 12, transcendentals=0
        ),
        name="sample_backward",
    )(
        scal,
        summary_grad,
        funcs,
        keys,
        vals,
        in_t,
        hid_t,
        hid_col,
        hid_w,
        pair_w,
    )

    grads_send, shared_recv, halves = lax.optimization_barrier(
        (grads_send, shared_recv, (output_own, output_other, grad_own, grad_other))
    )
    output_own, output_other, grad_own, grad_other = halves
    output = jnp.where(
        core == 0,
        jnp.concatenate([output_own, output_other]),
        jnp.concatenate([output_other, output_own]),
    )
    token_grad = jnp.where(
        core == 0,
        jnp.concatenate([grad_own, grad_other]),
        jnp.concatenate([grad_other, grad_own]),
    )
    own_half = jnp.sum(shared_recv.astype(F32), axis=0).reshape(-1)
    other_half = swap_cores(own_half)
    shared_grad = jnp.where(
        core == 0,
        jnp.concatenate([own_half, other_half]),
        jnp.concatenate([other_half, own_half]),
    )[:shared_len]
    branch_recv = lax.all_to_all(grads_send, "pts", 0, 0)
    branch_grad = jnp.sum(branch_recv.astype(F32), axis=0).reshape(1, -1)[:, :branch_len]
    new_branch, new_branch_m, new_branch_v = adam_step(
        branch_master, branch_m, branch_v, branch_grad
    )
    new_shared, new_shared_m, new_shared_v = adam_step(
        shared_master, shared_m, shared_v, shared_grad
    )
    return (
        output,
        token_grad,
        new_shared,
        new_shared_m,
        new_shared_v,
        new_branch,
        new_branch_m,
        new_branch_v,
    )


def solution(mesh):
    in_specs = (
        P("pts", None),
        P("branch", None, "pts"),
        P(),
        P("branch", None),
        P("pts", None),
        P("pts", None),
        P("pts"),
        P("pts"),
        P("pts"),
        P("branch", "pts"),
        P("branch", "pts"),
        P("branch", "pts"),
    )
    out_specs = (
        P("pts", None),
        P("pts", None),
        P("pts"),
        P("pts"),
        P("pts"),
        P("branch", "pts"),
        P("branch", "pts"),
        P("branch", "pts"),
    )
    return jax.shard_map(body, mesh=mesh, in_specs=in_specs, out_specs=out_specs, check_vma=False)
```

```python
import functools
import math

import jax
import jax.numpy as jnp
from jax import lax
from jax.experimental import pallas as pl
from jax.experimental.pallas import tpu as pltpu
from jax.sharding import PartitionSpec as P

D = 128
H = 8
HD = 16
FF = 256
E = 4
FIN = 3
STEP = 10

EPS_NORM = 1e-05
BETA_ONE = 0.9
BETA_TWO = 0.999
RATE_LEARN = 0.1
DECAY_RATE = 0.01
EPS_ADAM = 1e-08

LANES = 128
VMEM_BASE = 16 * 1024 * 1024
VMEM_ITEM = 768 * 1024
SAMPLE_TILE = 2048
BACK_TILE = 4096
TOKEN_TILE = 1024
CHUNK = 256

F32 = jnp.float32
BF16 = jnp.bfloat16

ROW_GAIN_ONE = 0
ROW_SHIFT_ONE = 1
ROW_QUERY = 2
ROW_OUT = ROW_QUERY + D
ROW_OUT_B = ROW_OUT + D
ROW_GAIN_TWO = ROW_OUT_B + 1
ROW_SHIFT_TWO = ROW_GAIN_TWO + 1
ROW_UP = ROW_SHIFT_TWO + 1
ROW_UP_B = ROW_UP + E * D * 2
ROW_DOWN = ROW_UP_B + E * 2
ROW_DOWN_B = ROW_DOWN + E * FF
SHARED_ROWS = ROW_DOWN_B + E

ROW_IN = 0
ROW_IN_B = ROW_IN + FIN
ROW_HID = ROW_IN_B + 1
ROW_HID_B = ROW_HID + D
ROW_PAIR = ROW_HID_B + 1
BRANCH_ROWS = ROW_PAIR + 2 * D

COL_GAIN_ONE = 0
COL_SHIFT_ONE = 1
COL_OUT_B = 2
COL_GAIN_TWO = 3
COL_SHIFT_TWO = 4
COL_UP_B = 5
COL_DOWN_B = COL_UP_B + 2 * E

TANH_C = math.sqrt(2.0 / math.pi)
TANH_CUBE = 0.044715


def up_to(amount, unit):
    return -(-amount // unit) * unit


def adam_step(master, moment_one, moment_two, grad):
    first = BETA_ONE * moment_one + (1.0 - BETA_ONE) * grad
    second = BETA_TWO * moment_two + (1.0 - BETA_TWO) * grad * grad
    first_hat = first / (1.0 - BETA_ONE**STEP)
    second_hat = second / (1.0 - BETA_TWO**STEP)
    fresh = master - RATE_LEARN * (
        first_hat / (jnp.sqrt(second_hat) + EPS_ADAM) + DECAY_RATE * master
    )
    return (fresh, first, second)


def dot_nn(left, right):
    return jnp.dot(left, right, preferred_element_type=F32)


def dot_nt(left, right):
    return lax.dot_general(left, right, (((1,), (1,)), ((), ())), preferred_element_type=F32)


def head_sum(values):
    split = values.reshape(H, HD, values.shape[1])
    total = jnp.sum(split, axis=1, keepdims=True)
    return jnp.broadcast_to(total, split.shape).reshape(values.shape)


def head_softmax(values):
    split = values.reshape(H, HD, values.shape[1])
    top = jnp.max(split, axis=1, keepdims=True)
    raised = jnp.exp(split - top)
    total = jnp.sum(raised, axis=1, keepdims=True)
    return (raised * (1.0 / total)).reshape(values.shape)


def gelu_value(inner):
    square = inner * inner
    bend = inner * (TANH_C + (TANH_C * TANH_CUBE) * square)
    return inner * (0.5 + 0.5 * jnp.tanh(bend))


def gelu_parts(inner):
    square = inner * inner
    bend = inner * (TANH_C + (TANH_C * TANH_CUBE) * square)
    gate = 0.5 + 0.5 * jnp.tanh(bend)
    rise = inner * (2.0 * TANH_C + (6.0 * TANH_C * TANH_CUBE) * square)
    return inner * gate, gate + (gate - gate * gate) * rise


def split_samples(funcs, parts_ref):
    high = funcs.astype(BF16).astype(F32)
    middle = (funcs - high).astype(BF16).astype(F32)
    parts_ref[0:FIN, :] = high
    parts_ref[FIN : 2 * FIN, :] = middle
    parts_ref[2 * FIN : 3 * FIN, :] = funcs - high - middle
    parts_ref[3 * FIN : 3 * FIN + 1, :] = jnp.ones((1, funcs.shape[1]), F32)
    parts_ref[3 * FIN + 1 :, :] = jnp.zeros((15 - 3 * FIN, funcs.shape[1]), F32)
    return parts_ref[...].astype(BF16)


def staggered(programs):
    waiting = list(programs)
    running = []
    while waiting or running:
        if waiting:
            running.append(waiting.pop(0))
        still = []
        for program in running:
            try:
                next(program)
                still.append(program)
            except StopIteration:
                pass
        running = still


def wide(tile, length):
    if length == tile.shape[1]:
        return tile
    return jnp.concatenate([tile] * (length // tile.shape[1]), axis=1)


def column(matrix, index, length):
    return jnp.broadcast_to(matrix[:, index : index + 1], (matrix.shape[0], length))


def fold_lanes(values):
    total = values[:, :LANES]
    for start in range(LANES, values.shape[1], LANES):
        total = total + values[:, start : start + LANES]
    return total


def lane_total_row(values):
    return jnp.sum(jnp.transpose(values), axis=0, keepdims=True)


def head_mask():
    row = lax.broadcasted_iota(jnp.int32, (D, D), 0) // HD
    col = lax.broadcasted_iota(jnp.int32, (D, D), 1) // HD
    return (row == col).astype(F32)


def fold_heads(values, mask):
    return jnp.sum((values * mask).reshape(H, HD, D), axis=0)


def spread_heads(compact, mask):
    return jnp.concatenate([compact] * H, axis=0) * mask


def store_starts(counts, starts, items):
    if items <= 8:
        total = jnp.int32(0)
        for item in range(items):
            starts[item] = total
            total = total + counts(item)
        starts[items] = total
    else:
        def step(item, total):
            starts[item] = total
            return total + counts(item)

        starts[items] = lax.fori_loop(0, items, step, jnp.int32(0))


def item_span(starts, items, begin, end):
    def step(item, span):
        low, high = span
        return (
            low + (starts[item + 1] <= begin).astype(jnp.int32),
            high + (starts[item] < end).astype(jnp.int32),
        )

    span = (jnp.int32(0), jnp.int32(0))
    if items <= 8:
        for item in range(items):
            span = step(item, span)
        return span
    return lax.fori_loop(0, items, step, span)


def item_row(starts, item, begin, length):
    position = begin + lax.broadcasted_iota(jnp.int32, (1, length), 1)
    return ((position >= starts[item]) & (position < starts[item + 1])).astype(F32)


def over_items(starts, items, begin, length, visit):
    low, high = item_span(starts, items, begin, begin + length)
    visit(jnp.minimum(low, items - 1), True)

    def step(item, carry):
        visit(item, False)
        return carry

    lax.fori_loop(low + 1, high, step, 0)


def over_parts(starts, item, begin, length, visit):
    width = min(256, length)
    for at in range(0, length, width):
        start = begin + at

        @pl.when((starts[item] < start + width) & (starts[item + 1] > start))
        def _(at=at, start=start):
            visit(slice(at, at + width), start)


def put_shard(vec_ref, tmp_ref, number, shard, height):
    row, shift = divmod(number * shard, LANES)
    touched = (shift + shard - 1) // LANES + 1
    if shift == 0:
        vec_ref[row : row + touched, :] = tmp_ref[8 : 8 + touched, :]
        return
    if number == 0:
        tmp_ref[7:8, :] = jnp.zeros((1, LANES), F32)
    else:
        tmp_ref[7:8, :] = vec_ref[row : row + 1, :]
    lane = lax.broadcasted_iota(jnp.int32, (touched, LANES), 1)
    vec_ref[row : row + touched, :] = jnp.where(
        lane >= shift, tmp_ref[8 : 8 + touched, :], tmp_ref[7 : 7 + touched, :]
    )


def turned(block, amount):
    amount = amount % LANES
    return block if amount == 0 else pltpu.roll(block, amount, 1)


def take_shard(vec_ref, number, shard, height):
    row, shift = divmod(number * shard, LANES)
    here = vec_ref[row : row + height, :]
    if shift == 0:
        return here
    after = vec_ref[row + 1 : row + 1 + height, :]
    lane = lax.broadcasted_iota(jnp.int32, (height, LANES), 1)
    return turned(jnp.where(lane >= shift, here, after), LANES - shift)


def sample_forward_kernel(
    plan,
    scal_ref,
    count_hbm,
    recv_ref,
    func_ref,
    msg_ref,
    keys_ref,
    vals_ref,
    hid_ref,
    pair_ref,
    in_t_ref,
    hid_t_ref,
    col_ref,
    vec_ref,
    tmp_ref,
    parts_ref,
    pair_t_ref,
    acc_ref,
    starts,
    count_ref,
    sem,
):
    tile, items, parts, shard, height, slots = plan
    step = pl.program_id(0)

    @pl.when(step == 0)
    def _():
        fetch = pltpu.make_async_copy(count_hbm, count_ref, sem)
        fetch.start()
        acc_ref[...] = jnp.zeros(acc_ref.shape, F32)
        for number in range(parts):
            shift = (number * shard) % LANES
            tmp_ref[8 : 8 + height, :] = turned(recv_ref[number].astype(F32), shift)
            put_shard(vec_ref, tmp_ref, number, shard, height)
        col_ref[...] = jnp.transpose(
            jnp.broadcast_to(vec_ref[ROW_HID_B : ROW_HID_B + 1, :], (D, D))
        )
        tmp_ref[0:16, :] = jnp.zeros((16, LANES), F32)
        for part in range(3):
            tmp_ref[part * FIN : (part + 1) * FIN, :] = vec_ref[ROW_IN : ROW_IN + FIN, :]
        tmp_ref[3 * FIN : 3 * FIN + 1, :] = vec_ref[ROW_IN_B : ROW_IN_B + 1, :]
        in_t_ref[...] = jnp.transpose(tmp_ref[0:16, :]).astype(BF16)
        hid = vec_ref[ROW_HID : ROW_HID + D, :]
        hid_ref[...] = hid.astype(BF16)
        hid_t_ref[...] = jnp.transpose(hid).astype(BF16)
        for part in range(2):
            piece = vec_ref[pl.ds(ROW_PAIR + part, D, stride=2), :]
            pair_ref[:, part * D : (part + 1) * D] = piece.astype(BF16)
            pair_t_ref[part * D : (part + 1) * D, :] = jnp.transpose(piece).astype(BF16)
        fetch.wait()
        store_starts(lambda item: count_ref[0, item], starts, items)

    samples = split_samples(func_ref[0], parts_ref)
    chunk = min(CHUNK, tile)

    def forward(start):
        at = slice(start, start + chunk)
        first_in = dot_nn(in_t_ref[...], samples[:, at])
        yield
        first = gelu_value(first_in).astype(BF16)
        yield
        second_in = dot_nn(hid_t_ref[...], first)
        yield
        second = gelu_value(second_in + wide(col_ref[...], chunk)).astype(BF16)
        yield
        pair = dot_nn(pair_t_ref[...], second)
        yield
        vals_ref[:, at] = pair[D:].astype(BF16)
        keys_ref[:, at] = head_softmax(pair[:D]).astype(BF16)

    staggered([forward(start) for start in range(0, tile, chunk)])
    keys = keys_ref[...]
    vals_ones = jnp.concatenate([vals_ref[...], jnp.ones((16, tile), BF16)], axis=0)
    begin = scal_ref[1] * slots + step * tile

    def visit(item, _):
        masked = keys * item_row(starts, item, begin, tile).astype(BF16)
        acc_ref[item] += dot_nt(vals_ones, masked)

    over_items(starts, items, begin, tile, visit)

    @pl.when(step == pl.num_programs(0) - 1)
    def _():
        mask = head_mask()
        msg_ref[items * HD :, :] = jnp.zeros((msg_ref.shape[0] - items * HD, LANES), F32)
        for item in range(items):
            msg_ref[item * HD : (item + 1) * HD, :] = fold_heads(acc_ref[item, :D, :], mask)
            msg_ref[items * HD + item : items * HD + item + 1, :] = acc_ref[item, D : D + 1, :]


def weight_kernel(
    plan,
    scal_ref,
    own_ref,
    other_ref,
    query_ref,
    query_t_ref,
    out_ref,
    out_t_ref,
    up_ref,
    up_t_ref,
    down_ref,
    down_t_ref,
    cols_ref,
    vec_ref,
    tmp_ref,
):
    parts, shard, half = plan
    core = scal_ref[0]
    own_at = pl.multiple_of(8 + core * half, 8)
    other_at = pl.multiple_of(8 + (1 - core) * half, 8)
    for number in range(parts):
        shift = (number * shard) % LANES
        tmp_ref[pl.ds(own_at, half), :] = turned(
            own_ref[number].astype(F32), shift
        )
        tmp_ref[pl.ds(other_at, half), :] = turned(
            other_ref[number].astype(F32), shift
        )
        put_shard(vec_ref, tmp_ref, number, shard, 2 * half)
    query = vec_ref[ROW_QUERY : ROW_QUERY + D, :]
    query_ref[...] = query.astype(BF16)
    query_t_ref[...] = jnp.transpose(query).astype(BF16)
    out = vec_ref[ROW_OUT : ROW_OUT + D, :]
    out_ref[...] = out.astype(BF16)
    out_t_ref[...] = jnp.transpose(out).astype(BF16)
    for expert in range(E):
        for part in range(2):
            up = vec_ref[pl.ds(ROW_UP + expert * 2 * D + part, D, stride=2), :]
            up_ref[expert, :, part * D : (part + 1) * D] = up.astype(BF16)
            up_t_ref[expert, part * D : (part + 1) * D, :D] = jnp.transpose(up).astype(BF16)
            row = ROW_DOWN + expert * FF + part * D
            down = vec_ref[row : row + D, :]
            down_ref[expert, part * D : (part + 1) * D, :] = down.astype(BF16)
            down_t_ref[expert, :, part * D : (part + 1) * D] = jnp.transpose(down).astype(BF16)
    tmp_ref[0:D, :] = jnp.zeros((D, LANES), F32)
    rows = [ROW_GAIN_ONE, ROW_SHIFT_ONE, ROW_OUT_B, ROW_GAIN_TWO, ROW_SHIFT_TWO]
    rows += [ROW_UP_B + number for number in range(2 * E)]
    rows += [ROW_DOWN_B + number for number in range(E)]
    for slot, row in enumerate(rows):
        tmp_ref[slot : slot + 1, :] = vec_ref[row : row + 1, :]
    cols = jnp.transpose(tmp_ref[0:D, :])
    cols_ref[...] = cols
    lane = lax.broadcasted_iota(jnp.int32, (D, 16), 1)
    for expert in range(E):
        for part in range(2):
            bias = jnp.where(lane == COL_UP_B + 2 * expert + part, cols[:, :16], 0.0)
            up_t_ref[expert, part * D : (part + 1) * D, D:] = bias.astype(BF16)


def norm_unit(values):
    centre = values - jnp.sum(values, axis=0, keepdims=True) * (1.0 / D)
    spread = jnp.sum(centre * centre, axis=0, keepdims=True) * (1.0 / D)
    scale = lax.rsqrt(spread + EPS_NORM)
    return centre * scale, scale


def norm_back(grad_unit, unit, scale):
    mean_one = jnp.sum(grad_unit, axis=0, keepdims=True) * (1.0 / D)
    mean_two = jnp.sum(grad_unit * unit, axis=0, keepdims=True) * (1.0 / D)
    return scale * (grad_unit - mean_one - unit * mean_two)


def query_kernel(
    scal_ref,
    token_ref,
    cot_ref,
    query_t_ref,
    cols_ref,
    token_t_ref,
    cot_t_ref,
    unit_ref,
    scale_ref,
    norm_ref,
    soft_ref,
):
    tokens = jnp.transpose(token_ref[...].astype(F32))
    length = tokens.shape[1]
    token_t_ref[...] = tokens.astype(BF16)
    cot_t_ref[...] = jnp.transpose(cot_ref[...])
    unit, scale = norm_unit(tokens)
    unit_ref[...] = unit
    scale_ref[...] = jnp.broadcast_to(scale, scale_ref.shape)
    cols = cols_ref[...]
    norm = (unit * column(cols, COL_GAIN_ONE, length) + column(cols, COL_SHIFT_ONE, length)).astype(
        BF16
    )
    norm_ref[...] = norm
    soft_ref[...] = head_softmax(dot_nn(query_t_ref[...], norm))


def token_kernel(
    plan,
    scal_ref,
    own_ref,
    other_ref,
    gate_ref,
    token_t_ref,
    cot_t_ref,
    unit_ref,
    scale_ref,
    norm_ref,
    soft_ref,
    query_ref,
    out_w_ref,
    out_t_ref,
    up_ref,
    up_t_ref,
    down_ref,
    down_t_ref,
    cols_ref,
    output_ref,
    grad_ref,
    own_msg_ref,
    other_msg_ref,
    g_query_ref,
    g_out_ref,
    g_up_ref,
    g_down_ref,
    g_vec_ref,
    left_ref,
    back_ref,
    acc_ref,
    mix_ref,
    pull_ref,
    grads_ref,
    starts,
):
    tile, items, slots, steps = plan
    step = pl.program_id(0)
    first_row = scal_ref[1] * slots + scal_ref[0] * (tile * steps)

    @pl.when(step == 0)
    def _():
        store_starts(lambda item: scal_ref[2 + item], starts, items)
        acc_ref[...] = jnp.zeros(acc_ref.shape, F32)
        g_query_ref[...] = jnp.zeros(g_query_ref.shape, F32)
        g_out_ref[...] = jnp.zeros(g_out_ref.shape, F32)
        g_up_ref[...] = jnp.zeros(g_up_ref.shape, F32)
        g_down_ref[...] = jnp.zeros(g_down_ref.shape, F32)
        g_vec_ref[...] = jnp.zeros(g_vec_ref.shape, F32)
        mask = head_mask()
        low, high = item_span(starts, items, first_row, first_row + tile * steps)

        def build(item, carry):
            at = pl.multiple_of(item * HD, HD)
            for slot, source in enumerate((own_ref, other_ref)):
                block = spread_heads(source[pl.ds(at, HD), :], mask)
                total = source[pl.ds(items * HD + item, 1), :] * mask
                for kind, piece in enumerate((block, total)):
                    row = (2 * kind + slot) * D
                    high_part = piece.astype(BF16)
                    left_ref[item, row : row + D, :D] = high_part
                    left_ref[item, row : row + D, D:] = (piece - high_part.astype(F32)).astype(BF16)
                    turned_piece = jnp.transpose(piece)
                    if kind == 1:
                        turned_piece = turned_piece * (1.0 / HD)
                    back_ref[item, :, row : row + D] = turned_piece.astype(BF16)
            return carry

        lax.fori_loop(low, high, build, 0)

    cols = cols_ref[...]
    begin = first_row + step * tile
    soft = soft_ref[...]

    def attend(item, lanes, start):
        length = lanes.stop - lanes.start
        masked = soft_ref[:, lanes].astype(BF16) * item_row(starts, item, start, length).astype(BF16)
        return dot_nn(left_ref[item], jnp.concatenate([masked, masked], axis=0))

    def forward(item, opening):
        if opening:
            mix_ref[...] = attend(item, slice(0, tile), begin)
            return

        def add(lanes, start):
            mix_ref[:, lanes] += attend(item, lanes, start)

        over_parts(starts, item, begin, tile, add)

    over_items(starts, items, begin, tile, forward)
    numer_one, numer_two = mix_ref[:D, :], mix_ref[D : 2 * D, :]
    inv_one, inv_two = 1.0 / mix_ref[2 * D : 3 * D, :], 1.0 / mix_ref[3 * D :, :]
    own_one, own_two = numer_one * inv_one, numer_two * inv_two
    attended = (0.5 * (own_one + own_two)).astype(BF16)
    cot = cot_t_ref[...]
    residual = (
        token_t_ref[...].astype(F32)
        + dot_nn(out_t_ref[...], attended)
        + column(cols, COL_OUT_B, tile)
    )
    unit, scale = norm_unit(residual)
    gain_two = column(cols, COL_GAIN_TWO, tile)
    norm = (unit * gain_two + column(cols, COL_SHIFT_TWO, tile)).astype(BF16)
    ones = jnp.ones((16, tile), BF16)
    norm_ones = jnp.concatenate([norm, ones], axis=0)
    gates = gate_ref[...].astype(F32)
    gates = gates / jnp.sum(gates, axis=0, keepdims=True)
    mixture = residual
    grad_norm = jnp.zeros((D, tile), F32)
    for expert in range(E):
        inner = dot_nn(up_t_ref[expert], norm_ones)
        active, slope = gelu_parts(inner)
        active = active.astype(BF16)
        result = dot_nn(down_t_ref[expert], active) + column(cols, COL_DOWN_B + expert, tile)
        gate = gates[expert : expert + 1, :]
        mixture = mixture + gate * result
        grad_result = (gate * cot).astype(BF16)
        g_down_ref[expert] += dot_nt(jnp.concatenate([active, ones], axis=0), grad_result)
        grad_inner = (slope * dot_nn(down_ref[expert], grad_result)).astype(BF16)
        g_up_ref[expert] += dot_nt(norm_ones, grad_inner)
        grad_norm = grad_norm + dot_nn(up_ref[expert], grad_inner)
    output_ref[...] = jnp.transpose(mixture).astype(BF16)
    g_vec_ref[2] += fold_lanes(grad_norm * unit)
    g_vec_ref[3] += fold_lanes(grad_norm)
    grad_residual = cot + norm_back(grad_norm * gain_two, unit, scale)
    grad_proj = grad_residual.astype(BF16)
    g_out_ref[...] += dot_nt(jnp.concatenate([attended, ones], axis=0), grad_proj)
    grad_own = 0.5 * dot_nn(out_w_ref[...], grad_proj)
    grad_one, grad_two = grad_own * inv_one, grad_own * inv_two
    sum_one = -head_sum(grad_one * own_one)
    sum_two = -head_sum(grad_two * own_two)
    grads = jnp.concatenate([grad_one, grad_two, sum_one, sum_two], axis=0).astype(BF16)

    grads_ref[...] = grads

    def pull_back(item, lanes, start):
        length = lanes.stop - lanes.start
        row = item_row(starts, item, start, length)
        part = grads_ref[:, lanes]
        masked = soft_ref[:, lanes].astype(BF16) * row.astype(BF16)
        return dot_nt(part, masked), row * dot_nn(back_ref[item], part)

    def backward(item, opening):
        if opening:
            sums, pull_ref[...] = pull_back(item, slice(0, tile), begin)
            acc_ref[item] += sums
            return

        def add(lanes, start):
            sums, pull = pull_back(item, lanes, start)
            acc_ref[item] += sums
            pull_ref[:, lanes] += pull

        over_parts(starts, item, begin, tile, add)

    over_items(starts, items, begin, tile, backward)
    pull = pull_ref[...]
    grad_query = (soft * (pull - head_sum(pull * soft))).astype(BF16)
    g_query_ref[...] += dot_nt(norm_ref[...], grad_query)
    grad_norm_one = dot_nn(query_ref[...], grad_query)
    unit_one = unit_ref[...]
    g_vec_ref[0] += fold_lanes(grad_norm_one * unit_one)
    g_vec_ref[1] += fold_lanes(grad_norm_one)
    grad_token = grad_residual + norm_back(
        grad_norm_one * column(cols, COL_GAIN_ONE, tile), unit_one, scale_ref[0:1, :]
    )
    grad_ref[...] = jnp.transpose(grad_token)

    @pl.when(step == steps - 1)
    def _():
        mask = head_mask()
        for slot, target in enumerate((own_msg_ref, other_msg_ref)):
            target[items * HD :, :] = jnp.zeros((target.shape[0] - items * HD, LANES), F32)
            for item in range(items):
                full = acc_ref[item, slot * D : (slot + 1) * D, :]
                target[item * HD : (item + 1) * HD, :] = fold_heads(full, mask)
                sums = acc_ref[item, (2 + slot) * D : (3 + slot) * D, :]
                target[items * HD + item : items * HD + item + 1, :] = fold_heads(sums, mask)[0:1]


def pack_kernel(
    plan,
    scal_ref,
    g_query_ref,
    g_out_ref,
    g_up_ref,
    g_down_ref,
    g_vec_ref,
    own_ref,
    other_ref,
    vec_ref,
    tmp_ref,
):
    parts, shard, half = plan
    vec_ref[SHARED_ROWS:, :] = jnp.zeros((vec_ref.shape[0] - SHARED_ROWS, LANES), F32)
    for slot, row in enumerate((ROW_GAIN_ONE, ROW_SHIFT_ONE, ROW_GAIN_TWO, ROW_SHIFT_TWO)):
        vec_ref[row : row + 1, :] = lane_total_row(g_vec_ref[slot])
    vec_ref[ROW_QUERY : ROW_QUERY + D, :] = g_query_ref[...]
    vec_ref[ROW_OUT : ROW_OUT + D + 1, :] = g_out_ref[: D + 1, :]
    for expert in range(E):
        for part in range(2):
            columns = slice(part * D, (part + 1) * D)
            vec_ref[pl.ds(ROW_UP + expert * 2 * D + part, D, stride=2), :] = g_up_ref[
                expert, :D, columns
            ]
            row = ROW_UP_B + 2 * expert + part
            vec_ref[row : row + 1, :] = g_up_ref[expert, D : D + 1, columns]
        row = ROW_DOWN + expert * FF
        vec_ref[row : row + FF, :] = g_down_ref[expert, :FF, :]
        row = ROW_DOWN_B + expert
        vec_ref[row : row + 1, :] = g_down_ref[expert, FF : FF + 1, :]
    core = scal_ref[0]
    own_at = pl.multiple_of(core * half, 8)
    other_at = pl.multiple_of((1 - core) * half, 8)
    for number in range(parts):
        tmp_ref[...] = take_shard(vec_ref, number, shard, 2 * half)
        own_ref[number] = tmp_ref[pl.ds(own_at, half), :]
        other_ref[number] = tmp_ref[pl.ds(other_at, half), :].astype(BF16)


def sample_backward_kernel(
    plan,
    scal_ref,
    msg_ref,
    func_ref,
    keys_hbm,
    vals_hbm,
    in_t_ref,
    hid_t_ref,
    col_ref,
    hid_ref,
    pair_ref,
    send_ref,
    kept_ref,
    vec_ref,
    left_keys_ref,
    left_vals_ref,
    keys_acc_ref,
    vals_acc_ref,
    g_pair_ref,
    g_hid_ref,
    g_in_ref,
    parts_ref,
    pairs_ref,
    seconds_ref,
    firsts_ref,
    first_ref,
    second_ref,
    starts,
    sems,
):
    tile, items, parts, shard, height, slots, steps = plan
    sources = (keys_hbm, vals_hbm)
    fetches = [
        [
            pltpu.make_async_copy(
                source.at[:, step * tile : (step + 1) * tile],
                kept_ref.at[number, :, step * tile : (step + 1) * tile],
                sems.at[number, step],
            )
            for number, source in enumerate(sources)
        ]
        for step in range(steps)
    ]
    for group in fetches:
        for fetch in group:
            fetch.start()

    def prepare():
        store_starts(lambda item: scal_ref[2 + items + item], starts, items)
        g_pair_ref[...] = jnp.zeros(g_pair_ref.shape, F32)
        g_hid_ref[...] = jnp.zeros(g_hid_ref.shape, F32)
        g_in_ref[...] = jnp.zeros(g_in_ref.shape, F32)
        mask = head_mask()
        low, high = item_span(
            starts, items, scal_ref[1] * slots, scal_ref[1] * slots + tile * steps
        )

        def build(item, carry):
            at = pl.multiple_of(item * HD, HD)
            block = spread_heads(msg_ref[pl.ds(at, HD), :], mask)
            high = block.astype(BF16)
            left_vals_ref[item, :, :D] = high
            left_vals_ref[item, :, D:] = (block - high.astype(F32)).astype(BF16)
            row = msg_ref[pl.ds(items * HD + item, 1), :]
            both = jnp.concatenate([block, row, jnp.zeros((D - 1, D), F32)], axis=0)
            both = jnp.transpose(both)[:, : D + 16]
            high = both.astype(BF16)
            left_keys_ref[item, 0] = high
            left_keys_ref[item, 1] = (both - high.astype(F32)).astype(BF16)
            return carry

        @pl.when(high <= low)
        def _():
            last = items - 1
            left_vals_ref[last] = jnp.zeros((D, 2 * D), BF16)
            left_keys_ref[last] = jnp.zeros((2, D, D + 16), BF16)

        lax.fori_loop(low, high, build, 0)

    def work(step):
        def part(number):
            return kept_ref.at[number, :, step * tile : (step + 1) * tile]

        keys_ref, vals_ref = part(0), part(1)
        fetches[step][0].wait()
        fetches[step][1].wait()
        keys = keys_ref[...]
        ones = jnp.ones((16, tile), BF16)
        vals_ones = jnp.concatenate([vals_ref[...], ones], axis=0)
        begin = scal_ref[1] * slots + step * tile

        def visit(item, opening):
            row = item_row(starts, item, begin, tile)
            fresh_keys = row * (
                dot_nn(left_keys_ref[item, 0], vals_ones) + dot_nn(left_keys_ref[item, 1], vals_ones)
            )
            fresh_vals = row * dot_nn(
                left_vals_ref[item], jnp.concatenate([keys, keys], axis=0)
            )
            keys_acc_ref[...] = fresh_keys if opening else keys_acc_ref[...] + fresh_keys
            vals_acc_ref[...] = fresh_vals if opening else vals_acc_ref[...] + fresh_vals

        over_items(starts, items, begin, tile, visit)
        samples = split_samples(func_ref[0, :, step * tile : (step + 1) * tile], parts_ref)
        chunk = min(CHUNK, tile)

        def backward(start):
            at = slice(start, start + chunk)
            first_in = dot_nn(in_t_ref[...], samples[:, at])
            yield
            first, slope_one = gelu_parts(first_in)
            first = first.astype(BF16)
            first_ref[:, at] = first
            yield
            second_in = dot_nn(hid_t_ref[...], first)
            yield
            second, slope_two = gelu_parts(second_in + wide(col_ref[...], chunk))
            second_ref[:, at] = second.astype(BF16)
            soft = keys_ref[:, at].astype(F32)
            grad_keys = keys_acc_ref[:, at]
            grad_in = soft * (grad_keys - head_sum(grad_keys * soft))
            grad_pair = jnp.concatenate([grad_in, vals_acc_ref[:, at]], axis=0).astype(BF16)
            pairs_ref[:, at] = grad_pair
            yield
            grad_second = dot_nn(pair_ref[...], grad_pair)
            yield
            grad_second = (slope_two * grad_second).astype(BF16)
            seconds_ref[:, at] = grad_second
            yield
            grad_first = dot_nn(hid_ref[...], grad_second)
            yield
            firsts_ref[:, at] = (slope_one * grad_first).astype(BF16)

        staggered([backward(start) for start in range(0, tile, chunk)])
        g_pair_ref[...] += dot_nt(second_ref[...], pairs_ref[...])
        first_ones = jnp.concatenate([first_ref[...], ones], axis=0)
        g_hid_ref[...] += dot_nt(first_ones, seconds_ref[...])
        g_in_ref[...] += dot_nt(samples, firsts_ref[...])

    prepare()
    for step in range(steps):
        work(step)
    vec_ref[BRANCH_ROWS:, :] = jnp.zeros((vec_ref.shape[0] - BRANCH_ROWS, LANES), F32)
    vec_ref[ROW_IN : ROW_IN + FIN, :] = (
        g_in_ref[0:FIN, :] + g_in_ref[FIN : 2 * FIN, :] + g_in_ref[2 * FIN : 3 * FIN, :]
    )
    vec_ref[ROW_IN_B : ROW_IN_B + 1, :] = g_in_ref[3 * FIN : 3 * FIN + 1, :]
    vec_ref[ROW_HID : ROW_HID + D + 1, :] = g_hid_ref[: D + 1, :]
    for part in range(2):
        vec_ref[pl.ds(ROW_PAIR + part, D, stride=2), :] = g_pair_ref[
            :, part * D : (part + 1) * D
        ]
    for number in range(parts):
        send_ref[number] = take_shard(vec_ref, number, shard, height).astype(BF16)


def sum_over_points(values, count, besides, early):
    bit = 1
    number = 0
    while bit < count:
        masks = [bit] if 2 * bit >= count else [bit, 2 * bit, 3 * bit]
        pieces = [
            lax.ppermute(values, "pts", [(source, source ^ mask) for source in range(count)])
            for mask in masks
        ]
        if number < len(besides):
            some = early[number]
            before = besides[number - 1] if number else None
            pieces[some], besides[number] = lax.optimization_barrier(
                (pieces[some], besides[number](before))
            )
        values = functools.reduce(jnp.add, pieces, values)
        bit *= 4
        number += 1
    return values, besides


def copies(block, count):
    return jnp.broadcast_to(block, (count,) + block.shape)


def swap_cores(values):
    return lax.ppermute(values, "branch", [(0, 1), (1, 0)])


def whole(shape, kind=None):
    zeros = (0,) * len(shape)
    return pl.BlockSpec(shape, lambda *_: zeros)


def body(
    tokens,
    funcs,
    item_counts,
    func_counts,
    gate_ints,
    cotangent,
    shared_master,
    shared_m,
    shared_v,
    branch_master,
    branch_m,
    branch_v,
):
    count = lax.axis_size("pts")
    core = lax.axis_index("branch")
    items = item_counts.shape[0]
    place = jnp.stack([core, lax.axis_index("pts")]).astype(jnp.int32)
    chip_rows = tokens.shape[0]
    rows = chip_rows // 2
    slots = funcs.shape[2]
    shared_len = shared_master.shape[0]
    branch_len = branch_master.shape[1]
    half = up_to(-(-shared_len // (2 * LANES)), 16)
    height = up_to(-(-branch_len // LANES), 16)
    msg_rows = items * HD + up_to(items, 8)
    params = pltpu.CompilerParams(vmem_limit_bytes=VMEM_BASE + items * VMEM_ITEM)
    shape = jax.ShapeDtypeStruct

    shared_pad = jnp.pad(shared_master.astype(BF16), (0, 2 * half * LANES - shared_len))
    shared_half = lax.dynamic_slice_in_dim(shared_pad, core * (half * LANES), half * LANES, 0)
    branch_pad = jnp.pad(
        branch_master.astype(BF16), ((0, 0), (0, height * LANES - branch_len))
    )
    recv_branch = lax.all_to_all(copies(branch_pad.reshape(height, LANES), count), "pts", 0, 0)
    shared_send = copies(shared_half.reshape(half, LANES), count)
    recv_branch, shared_send = lax.optimization_barrier((recv_branch, shared_send))
    recv_shared = lax.all_to_all(shared_send, "pts", 0, 0)

    tile = min(SAMPLE_TILE, slots)
    steps = slots // tile
    stream = lambda height_: pl.BlockSpec((height_, tile), lambda i, *_: (0, i))
    vec_rows = up_to(BRANCH_ROWS + 2 * height + 8, 8)
    (
        msg,
        keys,
        vals,
        hid_w,
        pair_w,
        in_t,
        hid_t,
        hid_col,
    ) = pl.pallas_call(
        functools.partial(
            sample_forward_kernel, (tile, items, count, branch_len, height, slots)
        ),
        grid_spec=pltpu.PrefetchScalarGridSpec(
            num_scalar_prefetch=1,
            grid=(steps,),
            in_specs=[
                pl.BlockSpec(memory_space=pl.ANY),
                pl.BlockSpec((count, height, LANES), lambda i, *_: (0, 0, 0)),
                pl.BlockSpec((1, FIN, tile), lambda i, *_: (0, 0, i)),
            ],
            out_specs=[
                whole((msg_rows, LANES)),
                stream(D),
                stream(D),
                whole((D, D)),
                whole((D, 2 * D)),
                whole((D, 16)),
                whole((D, D)),
                whole((D, D)),
            ],
            scratch_shapes=[
                pltpu.VMEM((vec_rows, LANES), F32),
                pltpu.VMEM((8 + 2 * height, LANES), F32),
                pltpu.VMEM((16, tile), F32),
                pltpu.VMEM((2 * D, D), BF16),
                pltpu.VMEM((items, D + 16, D), F32),
                pltpu.SMEM((items + 1,), jnp.int32),
                pltpu.SMEM((1, items), jnp.int32),
                pltpu.SemaphoreType.DMA,
            ],
        ),
        out_shape=[
            pltpu.VMEM((msg_rows, LANES), F32),
            pltpu.HBM((D, slots), BF16),
            pltpu.HBM((D, slots), BF16),
            shape((D, D), BF16),
            shape((D, 2 * D), BF16),
            shape((D, 16), BF16),
            shape((D, D), BF16),
            shape((D, D), F32),
        ],
        compiler_params=params,
        cost_estimate=pl.CostEstimate(
            flops=slots * D * D * 10, bytes_accessed=slots * D * 12, transcendentals=slots * D * 3
        ),
        name="sample_forward",
    )(
        place,
        pltpu.with_memory_space_constraint(func_counts, pltpu.HBM),
        recv_branch,
        funcs,
    )
    in_t, place, item_counts, func_counts = lax.optimization_barrier(
        (in_t, place, item_counts, func_counts)
    )
    scal = jnp.concatenate([place, item_counts, func_counts.reshape(-1)])


    shared_rows = up_to(SHARED_ROWS + 2 * half + 8, 8)

    def make_weights(recv_shared, recv_other):
        return pl.pallas_call(
            functools.partial(weight_kernel, (count, shared_len, half)),
            in_specs=[
                pl.BlockSpec(memory_space=pltpu.SMEM),
                whole(recv_shared.shape),
                whole(recv_shared.shape),
            ],
            out_specs=[
                whole((D, D)),
                whole((D, D)),
                whole((D, D)),
                whole((D, D)),
                whole((E, D, FF)),
                whole((E, FF, D + 16)),
                whole((E, FF, D)),
                whole((E, D, FF)),
                whole((D, D)),
            ],
            out_shape=[
                shape((D, D), BF16),
                shape((D, D), BF16),
                shape((D, D), BF16),
                shape((D, D), BF16),
                shape((E, D, FF), BF16),
                shape((E, FF, D + 16), BF16),
                shape((E, FF, D), BF16),
                shape((E, D, FF), BF16),
                shape((D, D), F32),
            ],
            scratch_shapes=[
                pltpu.VMEM((shared_rows, LANES), F32),
                pltpu.VMEM((max(8 + 2 * half, D) + 8, LANES), F32),
            ],
            compiler_params=params,
            cost_estimate=pl.CostEstimate(flops=0, bytes_accessed=8 << 20, transcendentals=0),
            name="weights",
        )(scal, recv_shared, recv_other)

    token_tile = min(TOKEN_TILE, rows)
    token_steps = rows // token_tile
    row_block = pl.BlockSpec(
        (token_tile, D), lambda i, scal_ref: (scal_ref[0] * token_steps + i, 0)
    )
    token_stream = lambda height_: pl.BlockSpec((height_, token_tile), lambda i, *_: (0, i))

    def make_queries(weights):
        return pl.pallas_call(
            query_kernel,
            grid_spec=pltpu.PrefetchScalarGridSpec(
                num_scalar_prefetch=1,
                grid=(token_steps,),
                in_specs=[row_block, row_block, whole((D, D)), whole((D, D))],
                out_specs=[
                    token_stream(D),
                    token_stream(D),
                    token_stream(D),
                    token_stream(8),
                    token_stream(D),
                    token_stream(D),
                ],
            ),
            out_shape=[
                shape((D, rows), BF16),
                shape((D, rows), F32),
                shape((D, rows), F32),
                shape((8, rows), F32),
                shape((D, rows), BF16),
                shape((D, rows), F32),
            ],
            compiler_params=params,
            cost_estimate=pl.CostEstimate(
                flops=rows * D * D * 2, bytes_accessed=rows * D * 24, transcendentals=rows * D
            ),
            name="queries",
        )(scal, tokens, cotangent, weights[1], weights[8])

    def beside_two(received):
        weights = make_weights(received, swap_cores(received))
        return weights, make_queries(weights)

    summary, (_, (weights, queries)) = sum_over_points(
        msg, count, [lambda _: recv_shared, beside_two], (slice(1), slice(3))
    )
    query_w, query_t, out_w, out_t, up_w, up_t, down_w, down_t, cols = weights
    token_t, cot_t, unit, scale, norm, soft = queries
    summary_other = swap_cores(summary)

    (
        output_own,
        grad_own,
        own_msg,
        other_msg,
        g_query,
        g_out,
        g_up,
        g_down,
        g_vec,
    ) = pl.pallas_call(
        functools.partial(token_kernel, (token_tile, items, chip_rows, token_steps)),
        grid_spec=pltpu.PrefetchScalarGridSpec(
            num_scalar_prefetch=1,
            grid=(token_steps,),
            in_specs=[
                whole((msg_rows, LANES)),
                whole((msg_rows, LANES)),
                pl.BlockSpec((E, token_tile), lambda i, scal_ref: (0, scal_ref[0] * token_steps + i)),
                token_stream(D),
                token_stream(D),
                token_stream(D),
                token_stream(8),
                token_stream(D),
                token_stream(D),
                whole((D, D)),
                whole((D, D)),
                whole((D, D)),
                whole((E, D, FF)),
                whole((E, FF, D + 16)),
                whole((E, FF, D)),
                whole((E, D, FF)),
                whole((D, D)),
            ],
            out_specs=[
                pl.BlockSpec((token_tile, D), lambda i, *_: (i, 0)),
                pl.BlockSpec((token_tile, D), lambda i, *_: (i, 0)),
                whole((msg_rows, LANES)),
                whole((msg_rows, LANES)),
                whole((D, D)),
                whole((D + 16, D)),
                whole((E, D + 16, FF)),
                whole((E, FF + 16, D)),
                whole((4, D, D)),
            ],
            scratch_shapes=[
                pltpu.VMEM((items, 4 * D, 2 * D), BF16),
                pltpu.VMEM((items, D, 4 * D), BF16),
                pltpu.VMEM((items, 4 * D, D), F32),
                pltpu.VMEM((4 * D, token_tile), F32),
                pltpu.VMEM((D, token_tile), F32),
                pltpu.VMEM((4 * D, token_tile), BF16),
                pltpu.SMEM((items + 1,), jnp.int32),
            ],
        ),
        out_shape=[
            shape((rows, D), BF16),
            shape((rows, D), F32),
            pltpu.VMEM((msg_rows, LANES), F32),
            pltpu.VMEM((msg_rows, LANES), F32),
            shape((D, D), F32),
            shape((D + 16, D), F32),
            shape((E, D + 16, FF), F32),
            shape((E, FF + 16, D), F32),
            shape((4, D, D), F32),
        ],
        compiler_params=params,
        cost_estimate=pl.CostEstimate(
            flops=rows * D * FF * 12 * E, bytes_accessed=rows * D * 24, transcendentals=rows * FF * E
        ),
        name="tokens",
    )(
        scal,
        summary,
        summary_other,
        gate_ints.T,
        token_t,
        cot_t,
        unit,
        scale,
        norm,
        soft,
        query_w,
        out_w,
        out_t,
        up_w,
        up_t,
        down_w,
        down_t,
        cols,
    )

    both_msg, parts = lax.optimization_barrier(
        (own_msg + swap_cores(other_msg), (g_query, g_out, g_up, g_down, g_vec))
    )
    half_own, half_other = pl.pallas_call(
        functools.partial(pack_kernel, (count, shared_len, half)),
        in_specs=[pl.BlockSpec(memory_space=pltpu.SMEM)]
        + [whole(piece.shape) for piece in parts],
        out_specs=[whole((count, half, LANES)), whole((count, half, LANES))],
        out_shape=[shape((count, half, LANES), F32), shape((count, half, LANES), BF16)],
        scratch_shapes=[
            pltpu.VMEM((shared_rows, LANES), F32),
            pltpu.VMEM((2 * half, LANES), F32),
        ],
        compiler_params=params,
        cost_estimate=pl.CostEstimate(flops=2 << 30, bytes_accessed=4 << 20, transcendentals=0),
        name="pack",
    )(scal, *parts)

    output_other = swap_cores(output_own)
    grad_other = swap_cores(grad_own)

    def add_halves(packed):
        half_sum = (packed[0] + swap_cores(packed[1]).astype(F32)).astype(BF16)
        return half_sum, output_other, grad_other

    summary_grad, (_, tail) = sum_over_points(
        both_msg, count, [lambda _: [half_own, half_other], add_halves], (slice(3), slice(2, 3))
    )
    half_sum, output_other, grad_other = tail
    keys, vals = (pltpu.with_memory_space_constraint(kept, pltpu.HBM) for kept in (keys, vals))
    back_tile = min(BACK_TILE, slots)
    back_steps = slots // back_tile
    shared_recv = lax.all_to_all(half_sum, "pts", 0, 0)
    grads_send = pl.pallas_call(
        functools.partial(
            sample_backward_kernel,
            (back_tile, items, count, branch_len, height, slots, back_steps),
        ),
        grid_spec=pltpu.PrefetchScalarGridSpec(
            num_scalar_prefetch=1,
            grid=(1,),
            in_specs=[
                whole((msg_rows, LANES)),
                whole((1, FIN, slots)),
                pl.BlockSpec(memory_space=pl.ANY),
                pl.BlockSpec(memory_space=pl.ANY),
                whole((D, 16)),
                whole((D, D)),
                whole((D, D)),
                whole((D, D)),
                whole((D, 2 * D)),
            ],
            out_specs=whole((count, height, LANES)),
            scratch_shapes=[
                pltpu.VMEM((2, D, slots), BF16),
                pltpu.VMEM((vec_rows, LANES), F32),
                pltpu.VMEM((items, 2, D, D + 16), BF16),
                pltpu.VMEM((items, D, 2 * D), BF16),
                pltpu.VMEM((D, back_tile), F32),
                pltpu.VMEM((D, back_tile), F32),
                pltpu.VMEM((D, 2 * D), F32),
                pltpu.VMEM((D + 16, D), F32),
                pltpu.VMEM((16, D), F32),
                pltpu.VMEM((16, back_tile), F32),
                pltpu.VMEM((2 * D, back_tile), BF16),
                pltpu.VMEM((D, back_tile), BF16),
                pltpu.VMEM((D, back_tile), BF16),
                pltpu.VMEM((D, back_tile), BF16),
                pltpu.VMEM((D, back_tile), BF16),
                pltpu.SMEM((items + 1,), jnp.int32),
                pltpu.SemaphoreType.DMA((2, back_steps)),
            ],
        ),
        out_shape=shape((count, height, LANES), BF16),
        compiler_params=pltpu.CompilerParams(
            vmem_limit_bytes=2 * VMEM_BASE + items * VMEM_ITEM
        ),
        cost_estimate=pl.CostEstimate(
            flops=slots * D * D * 300, bytes_accessed=slots * D * 12, transcendentals=0
        ),
        name="sample_backward",
    )(
        scal,
        summary_grad,
        funcs,
        keys,
        vals,
        in_t,
        hid_t,
        hid_col,
        hid_w,
        pair_w,
    )

    grads_send, shared_recv, halves = lax.optimization_barrier(
        (grads_send, shared_recv, (output_own, output_other, grad_own, grad_other))
    )
    output_own, output_other, grad_own, grad_other = halves
    output = jnp.where(
        core == 0,
        jnp.concatenate([output_own, output_other]),
        jnp.concatenate([output_other, output_own]),
    )
    token_grad = jnp.where(
        core == 0,
        jnp.concatenate([grad_own, grad_other]),
        jnp.concatenate([grad_other, grad_own]),
    )
    own_half = jnp.sum(shared_recv.astype(F32), axis=0).reshape(-1)
    other_half = swap_cores(own_half)
    shared_grad = jnp.where(
        core == 0,
        jnp.concatenate([own_half, other_half]),
        jnp.concatenate([other_half, own_half]),
    )[:shared_len]
    branch_recv = lax.all_to_all(grads_send, "pts", 0, 0)
    branch_grad = jnp.sum(branch_recv.astype(F32), axis=0).reshape(1, -1)[:, :branch_len]
    new_branch, new_branch_m, new_branch_v = adam_step(
        branch_master, branch_m, branch_v, branch_grad
    )
    new_shared, new_shared_m, new_shared_v = adam_step(
        shared_master, shared_m, shared_v, shared_grad
    )
    return (
        output,
        token_grad,
        new_shared,
        new_shared_m,
        new_shared_v,
        new_branch,
        new_branch_m,
        new_branch_v,
    )


def solution(mesh):
    in_specs = (
        P("pts", None),
        P("branch", None, "pts"),
        P(),
        P("branch", None),
        P("pts", None),
        P("pts", None),
        P("pts"),
        P("pts"),
        P("pts"),
        P("branch", "pts"),
        P("branch", "pts"),
        P("branch", "pts"),
    )
    out_specs = (
        P("pts", None),
        P("pts", None),
        P("pts"),
        P("pts"),
        P("pts"),
        P("branch", "pts"),
        P("branch", "pts"),
        P("branch", "pts"),
    )
    return jax.shard_map(body, mesh=mesh, in_specs=in_specs, out_specs=out_specs, check_vma=False)
```

```python
import functools
import math

import jax
import jax.numpy as jnp
from jax import lax
from jax.experimental import pallas as pl
from jax.experimental.pallas import tpu as pltpu
from jax.sharding import PartitionSpec as P

D = 128
H = 8
HD = 16
FF = 256
E = 4
FIN = 3
STEP = 10

EPS_NORM = 1e-05
BETA_ONE = 0.9
BETA_TWO = 0.999
RATE_LEARN = 0.1
DECAY_RATE = 0.01
EPS_ADAM = 1e-08

LANES = 128
VMEM_BASE = 16 * 1024 * 1024
VMEM_ITEM = 768 * 1024
SAMPLE_TILE = 2048
BACK_TILE = 4096
TOKEN_TILE = 1024
CHUNK = 256

F32 = jnp.float32
BF16 = jnp.bfloat16

ROW_GAIN_ONE = 0
ROW_SHIFT_ONE = 1
ROW_QUERY = 2
ROW_OUT = ROW_QUERY + D
ROW_OUT_B = ROW_OUT + D
ROW_GAIN_TWO = ROW_OUT_B + 1
ROW_SHIFT_TWO = ROW_GAIN_TWO + 1
ROW_UP = ROW_SHIFT_TWO + 1
ROW_UP_B = ROW_UP + E * D * 2
ROW_DOWN = ROW_UP_B + E * 2
ROW_DOWN_B = ROW_DOWN + E * FF
SHARED_ROWS = ROW_DOWN_B + E

ROW_IN = 0
ROW_IN_B = ROW_IN + FIN
ROW_HID = ROW_IN_B + 1
ROW_HID_B = ROW_HID + D
ROW_PAIR = ROW_HID_B + 1
BRANCH_ROWS = ROW_PAIR + 2 * D

COL_GAIN_ONE = 0
COL_SHIFT_ONE = 1
COL_OUT_B = 2
COL_GAIN_TWO = 3
COL_SHIFT_TWO = 4
COL_UP_B = 5
COL_DOWN_B = COL_UP_B + 2 * E

TANH_C = math.sqrt(2.0 / math.pi)
TANH_CUBE = 0.044715


def up_to(amount, unit):
    return -(-amount // unit) * unit


def adam_step(master, moment_one, moment_two, grad):
    first = BETA_ONE * moment_one + (1.0 - BETA_ONE) * grad
    second = BETA_TWO * moment_two + (1.0 - BETA_TWO) * grad * grad
    first_hat = first / (1.0 - BETA_ONE**STEP)
    second_hat = second / (1.0 - BETA_TWO**STEP)
    fresh = master - RATE_LEARN * (
        first_hat / (jnp.sqrt(second_hat) + EPS_ADAM) + DECAY_RATE * master
    )
    return (fresh, first, second)


def dot_nn(left, right):
    return jnp.dot(left, right, preferred_element_type=F32)


def dot_nt(left, right):
    return lax.dot_general(left, right, (((1,), (1,)), ((), ())), preferred_element_type=F32)


def head_sum(values):
    split = values.reshape(H, HD, values.shape[1])
    total = jnp.sum(split, axis=1, keepdims=True)
    return jnp.broadcast_to(total, split.shape).reshape(values.shape)


def head_softmax(values):
    split = values.reshape(H, HD, values.shape[1])
    top = jnp.max(split, axis=1, keepdims=True)
    raised = jnp.exp(split - top)
    total = jnp.sum(raised, axis=1, keepdims=True)
    return (raised * (1.0 / total)).reshape(values.shape)


def gelu_value(inner):
    square = inner * inner
    bend = inner * (TANH_C + (TANH_C * TANH_CUBE) * square)
    return inner * (0.5 + 0.5 * jnp.tanh(bend))


def gelu_parts(inner):
    square = inner * inner
    bend = inner * (TANH_C + (TANH_C * TANH_CUBE) * square)
    gate = 0.5 + 0.5 * jnp.tanh(bend)
    rise = inner * (2.0 * TANH_C + (6.0 * TANH_C * TANH_CUBE) * square)
    return inner * gate, gate + (gate - gate * gate) * rise


def split_samples(funcs, parts_ref):
    high = funcs.astype(BF16).astype(F32)
    middle = (funcs - high).astype(BF16).astype(F32)
    parts_ref[0:FIN, :] = high
    parts_ref[FIN : 2 * FIN, :] = middle
    parts_ref[2 * FIN : 3 * FIN, :] = funcs - high - middle
    parts_ref[3 * FIN : 3 * FIN + 1, :] = jnp.ones((1, funcs.shape[1]), F32)
    parts_ref[3 * FIN + 1 :, :] = jnp.zeros((15 - 3 * FIN, funcs.shape[1]), F32)
    return parts_ref[...].astype(BF16)


def staggered(programs):
    waiting = list(programs)
    running = []
    while waiting or running:
        if waiting:
            running.append(waiting.pop(0))
        still = []
        for program in running:
            try:
                next(program)
                still.append(program)
            except StopIteration:
                pass
        running = still


def wide(tile, length):
    if length == tile.shape[1]:
        return tile
    return jnp.concatenate([tile] * (length // tile.shape[1]), axis=1)


def column(matrix, index, length):
    return jnp.broadcast_to(matrix[:, index : index + 1], (matrix.shape[0], length))


def fold_lanes(values):
    total = values[:, :LANES]
    for start in range(LANES, values.shape[1], LANES):
        total = total + values[:, start : start + LANES]
    return total


def lane_total_row(values):
    return jnp.sum(jnp.transpose(values), axis=0, keepdims=True)


def head_mask():
    row = lax.broadcasted_iota(jnp.int32, (D, D), 0) // HD
    col = lax.broadcasted_iota(jnp.int32, (D, D), 1) // HD
    return (row == col).astype(F32)


def fold_heads(values, mask):
    return jnp.sum((values * mask).reshape(H, HD, D), axis=0)


def spread_heads(compact, mask):
    return jnp.concatenate([compact] * H, axis=0) * mask


def store_starts(counts, starts, items):
    if items <= 8:
        total = jnp.int32(0)
        for item in range(items):
            starts[item] = total
            total = total + counts(item)
        starts[items] = total
    else:
        def step(item, total):
            starts[item] = total
            return total + counts(item)

        starts[items] = lax.fori_loop(0, items, step, jnp.int32(0))


def item_span(starts, items, begin, end):
    def step(item, span):
        low, high = span
        return (
            low + (starts[item + 1] <= begin).astype(jnp.int32),
            high + (starts[item] < end).astype(jnp.int32),
        )

    span = (jnp.int32(0), jnp.int32(0))
    if items <= 8:
        for item in range(items):
            span = step(item, span)
        return span
    return lax.fori_loop(0, items, step, span)


def item_row(starts, item, begin, length):
    position = begin + lax.broadcasted_iota(jnp.int32, (1, length), 1)
    return ((position >= starts[item]) & (position < starts[item + 1])).astype(F32)


def over_items(starts, items, begin, length, visit):
    low, high = item_span(starts, items, begin, begin + length)
    visit(jnp.minimum(low, items - 1), True)

    def step(item, carry):
        visit(item, False)
        return carry

    lax.fori_loop(low + 1, high, step, 0)


def over_parts(starts, item, begin, length, visit):
    width = min(256, length)
    for at in range(0, length, width):
        start = begin + at

        @pl.when((starts[item] < start + width) & (starts[item + 1] > start))
        def _(at=at, start=start):
            visit(slice(at, at + width), start)


def put_shard(vec_ref, tmp_ref, number, shard, height):
    row, shift = divmod(number * shard, LANES)
    touched = (shift + shard - 1) // LANES + 1
    if shift == 0:
        vec_ref[row : row + touched, :] = tmp_ref[8 : 8 + touched, :]
        return
    if number == 0:
        tmp_ref[7:8, :] = jnp.zeros((1, LANES), F32)
    else:
        tmp_ref[7:8, :] = vec_ref[row : row + 1, :]
    lane = lax.broadcasted_iota(jnp.int32, (touched, LANES), 1)
    vec_ref[row : row + touched, :] = jnp.where(
        lane >= shift, tmp_ref[8 : 8 + touched, :], tmp_ref[7 : 7 + touched, :]
    )


def turned(block, amount):
    amount = amount % LANES
    return block if amount == 0 else pltpu.roll(block, amount, 1)


def take_shard(vec_ref, number, shard, height):
    row, shift = divmod(number * shard, LANES)
    here = vec_ref[row : row + height, :]
    if shift == 0:
        return here
    after = vec_ref[row + 1 : row + 1 + height, :]
    lane = lax.broadcasted_iota(jnp.int32, (height, LANES), 1)
    return turned(jnp.where(lane >= shift, here, after), LANES - shift)


def sample_forward_kernel(
    plan,
    scal_ref,
    count_hbm,
    recv_ref,
    func_ref,
    msg_ref,
    keys_ref,
    vals_ref,
    hid_ref,
    pair_ref,
    in_t_ref,
    hid_t_ref,
    col_ref,
    vec_ref,
    tmp_ref,
    parts_ref,
    pair_t_ref,
    acc_ref,
    starts,
    count_ref,
    sem,
):
    tile, items, parts, shard, height, slots = plan
    step = pl.program_id(0)

    @pl.when(step == 0)
    def _():
        fetch = pltpu.make_async_copy(count_hbm, count_ref, sem)
        fetch.start()
        acc_ref[...] = jnp.zeros(acc_ref.shape, F32)
        for number in range(parts):
            shift = (number * shard) % LANES
            tmp_ref[8 : 8 + height, :] = turned(recv_ref[number].astype(F32), shift)
            put_shard(vec_ref, tmp_ref, number, shard, height)
        col_ref[...] = jnp.transpose(
            jnp.broadcast_to(vec_ref[ROW_HID_B : ROW_HID_B + 1, :], (D, D))
        )
        tmp_ref[0:16, :] = jnp.zeros((16, LANES), F32)
        for part in range(3):
            tmp_ref[part * FIN : (part + 1) * FIN, :] = vec_ref[ROW_IN : ROW_IN + FIN, :]
        tmp_ref[3 * FIN : 3 * FIN + 1, :] = vec_ref[ROW_IN_B : ROW_IN_B + 1, :]
        in_t_ref[...] = jnp.transpose(tmp_ref[0:16, :]).astype(BF16)
        hid = vec_ref[ROW_HID : ROW_HID + D, :]
        hid_ref[...] = hid.astype(BF16)
        hid_t_ref[...] = jnp.transpose(hid).astype(BF16)
        for part in range(2):
            piece = vec_ref[pl.ds(ROW_PAIR + part, D, stride=2), :]
            pair_ref[:, part * D : (part + 1) * D] = piece.astype(BF16)
            pair_t_ref[part * D : (part + 1) * D, :] = jnp.transpose(piece).astype(BF16)
        fetch.wait()
        store_starts(lambda item: count_ref[0, item], starts, items)

    samples = split_samples(func_ref[0], parts_ref)
    chunk = min(CHUNK, tile)

    def forward(start):
        at = slice(start, start + chunk)
        first_in = dot_nn(in_t_ref[...], samples[:, at])
        yield
        first = gelu_value(first_in).astype(BF16)
        yield
        second_in = dot_nn(hid_t_ref[...], first)
        yield
        second = gelu_value(second_in + wide(col_ref[...], chunk)).astype(BF16)
        yield
        pair = dot_nn(pair_t_ref[...], second)
        yield
        vals_ref[:, at] = pair[D:].astype(BF16)
        keys_ref[:, at] = head_softmax(pair[:D]).astype(BF16)

    staggered([forward(start) for start in range(0, tile, chunk)])
    keys = keys_ref[...]
    vals_ones = jnp.concatenate([vals_ref[...], jnp.ones((16, tile), BF16)], axis=0)
    begin = scal_ref[1] * slots + step * tile

    def visit(item, _):
        masked = keys * item_row(starts, item, begin, tile).astype(BF16)
        acc_ref[item] += dot_nt(vals_ones, masked)

    over_items(starts, items, begin, tile, visit)

    @pl.when(step == pl.num_programs(0) - 1)
    def _():
        mask = head_mask()
        msg_ref[items * HD :, :] = jnp.zeros((msg_ref.shape[0] - items * HD, LANES), F32)
        for item in range(items):
            msg_ref[item * HD : (item + 1) * HD, :] = fold_heads(acc_ref[item, :D, :], mask)
            msg_ref[items * HD + item : items * HD + item + 1, :] = acc_ref[item, D : D + 1, :]


def weight_kernel(
    plan,
    scal_ref,
    own_ref,
    other_ref,
    query_ref,
    query_t_ref,
    out_ref,
    out_t_ref,
    up_ref,
    up_t_ref,
    down_ref,
    down_t_ref,
    cols_ref,
    vec_ref,
    tmp_ref,
):
    parts, shard, half = plan
    core = scal_ref[0]
    own_at = pl.multiple_of(8 + core * half, 8)
    other_at = pl.multiple_of(8 + (1 - core) * half, 8)
    for number in range(parts):
        shift = (number * shard) % LANES
        tmp_ref[pl.ds(own_at, half), :] = turned(
            own_ref[number].astype(F32), shift
        )
        tmp_ref[pl.ds(other_at, half), :] = turned(
            other_ref[number].astype(F32), shift
        )
        put_shard(vec_ref, tmp_ref, number, shard, 2 * half)
    query = vec_ref[ROW_QUERY : ROW_QUERY + D, :]
    query_ref[...] = query.astype(BF16)
    query_t_ref[...] = jnp.transpose(query).astype(BF16)
    out = vec_ref[ROW_OUT : ROW_OUT + D, :]
    out_ref[...] = out.astype(BF16)
    out_t_ref[...] = jnp.transpose(out).astype(BF16)
    for expert in range(E):
        for part in range(2):
            up = vec_ref[pl.ds(ROW_UP + expert * 2 * D + part, D, stride=2), :]
            up_ref[expert, :, part * D : (part + 1) * D] = up.astype(BF16)
            up_t_ref[expert, part * D : (part + 1) * D, :D] = jnp.transpose(up).astype(BF16)
            row = ROW_DOWN + expert * FF + part * D
            down = vec_ref[row : row + D, :]
            down_ref[expert, part * D : (part + 1) * D, :] = down.astype(BF16)
            down_t_ref[expert, :, part * D : (part + 1) * D] = jnp.transpose(down).astype(BF16)
    tmp_ref[0:D, :] = jnp.zeros((D, LANES), F32)
    rows = [ROW_GAIN_ONE, ROW_SHIFT_ONE, ROW_OUT_B, ROW_GAIN_TWO, ROW_SHIFT_TWO]
    rows += [ROW_UP_B + number for number in range(2 * E)]
    rows += [ROW_DOWN_B + number for number in range(E)]
    for slot, row in enumerate(rows):
        tmp_ref[slot : slot + 1, :] = vec_ref[row : row + 1, :]
    cols = jnp.transpose(tmp_ref[0:D, :])
    cols_ref[...] = cols
    lane = lax.broadcasted_iota(jnp.int32, (D, 16), 1)
    for expert in range(E):
        for part in range(2):
            bias = jnp.where(lane == COL_UP_B + 2 * expert + part, cols[:, :16], 0.0)
            up_t_ref[expert, part * D : (part + 1) * D, D:] = bias.astype(BF16)


def norm_unit(values):
    centre = values - jnp.sum(values, axis=0, keepdims=True) * (1.0 / D)
    spread = jnp.sum(centre * centre, axis=0, keepdims=True) * (1.0 / D)
    scale = lax.rsqrt(spread + EPS_NORM)
    return centre * scale, scale


def norm_back(grad_unit, unit, scale):
    mean_one = jnp.sum(grad_unit, axis=0, keepdims=True) * (1.0 / D)
    mean_two = jnp.sum(grad_unit * unit, axis=0, keepdims=True) * (1.0 / D)
    return scale * (grad_unit - mean_one - unit * mean_two)


def query_kernel(
    scal_ref,
    token_ref,
    cot_ref,
    query_t_ref,
    cols_ref,
    token_t_ref,
    cot_t_ref,
    unit_ref,
    scale_ref,
    norm_ref,
    soft_ref,
):
    tokens = jnp.transpose(token_ref[...].astype(F32))
    length = tokens.shape[1]
    token_t_ref[...] = tokens.astype(BF16)
    cot_t_ref[...] = jnp.transpose(cot_ref[...])
    unit, scale = norm_unit(tokens)
    unit_ref[...] = unit
    scale_ref[...] = jnp.broadcast_to(scale, scale_ref.shape)
    cols = cols_ref[...]
    norm = (unit * column(cols, COL_GAIN_ONE, length) + column(cols, COL_SHIFT_ONE, length)).astype(
        BF16
    )
    norm_ref[...] = norm
    soft_ref[...] = head_softmax(dot_nn(query_t_ref[...], norm))


def token_kernel(
    plan,
    scal_ref,
    own_ref,
    other_ref,
    gate_ref,
    token_t_ref,
    cot_t_ref,
    unit_ref,
    scale_ref,
    norm_ref,
    soft_ref,
    query_ref,
    out_w_ref,
    out_t_ref,
    up_ref,
    up_t_ref,
    down_ref,
    down_t_ref,
    cols_ref,
    output_ref,
    grad_ref,
    own_msg_ref,
    other_msg_ref,
    g_query_ref,
    g_out_ref,
    g_up_ref,
    g_down_ref,
    g_vec_ref,
    left_ref,
    back_ref,
    acc_ref,
    mix_ref,
    pull_ref,
    grads_ref,
    starts,
):
    tile, items, slots, steps = plan
    step = pl.program_id(0)
    first_row = scal_ref[1] * slots + scal_ref[0] * (tile * steps)

    @pl.when(step == 0)
    def _():
        store_starts(lambda item: scal_ref[2 + item], starts, items)
        acc_ref[...] = jnp.zeros(acc_ref.shape, F32)
        g_query_ref[...] = jnp.zeros(g_query_ref.shape, F32)
        g_out_ref[...] = jnp.zeros(g_out_ref.shape, F32)
        g_up_ref[...] = jnp.zeros(g_up_ref.shape, F32)
        g_down_ref[...] = jnp.zeros(g_down_ref.shape, F32)
        g_vec_ref[...] = jnp.zeros(g_vec_ref.shape, F32)
        mask = head_mask()
        low, high = item_span(starts, items, first_row, first_row + tile * steps)

        def build(item, carry):
            at = pl.multiple_of(item * HD, HD)
            for slot, source in enumerate((own_ref, other_ref)):
                block = spread_heads(source[pl.ds(at, HD), :], mask)
                total = source[pl.ds(items * HD + item, 1), :] * mask
                for kind, piece in enumerate((block, total)):
                    row = (2 * kind + slot) * D
                    high_part = piece.astype(BF16)
                    left_ref[item, row : row + D, :D] = high_part
                    left_ref[item, row : row + D, D:] = (piece - high_part.astype(F32)).astype(BF16)
                    turned_piece = jnp.transpose(piece)
                    if kind == 1:
                        turned_piece = turned_piece * (1.0 / HD)
                    back_ref[item, :, row : row + D] = turned_piece.astype(BF16)
            return carry

        lax.fori_loop(low, high, build, 0)

    cols = cols_ref[...]
    begin = first_row + step * tile
    soft = soft_ref[...]

    def attend(item, lanes, start):
        length = lanes.stop - lanes.start
        masked = soft_ref[:, lanes].astype(BF16) * item_row(starts, item, start, length).astype(BF16)
        return dot_nn(left_ref[item], jnp.concatenate([masked, masked], axis=0))

    def forward(item, opening):
        if opening:
            mix_ref[...] = attend(item, slice(0, tile), begin)
            return

        def add(lanes, start):
            mix_ref[:, lanes] += attend(item, lanes, start)

        over_parts(starts, item, begin, tile, add)

    over_items(starts, items, begin, tile, forward)
    numer_one, numer_two = mix_ref[:D, :], mix_ref[D : 2 * D, :]
    inv_one, inv_two = 1.0 / mix_ref[2 * D : 3 * D, :], 1.0 / mix_ref[3 * D :, :]
    own_one, own_two = numer_one * inv_one, numer_two * inv_two
    attended = (0.5 * (own_one + own_two)).astype(BF16)
    cot = cot_t_ref[...]
    residual = (
        token_t_ref[...].astype(F32)
        + dot_nn(out_t_ref[...], attended)
        + column(cols, COL_OUT_B, tile)
    )
    unit, scale = norm_unit(residual)
    gain_two = column(cols, COL_GAIN_TWO, tile)
    norm = (unit * gain_two + column(cols, COL_SHIFT_TWO, tile)).astype(BF16)
    ones = jnp.ones((16, tile), BF16)
    norm_ones = jnp.concatenate([norm, ones], axis=0)
    gates = gate_ref[...].astype(F32)
    gates = gates / jnp.sum(gates, axis=0, keepdims=True)
    mixture = residual
    grad_norm = jnp.zeros((D, tile), F32)
    for expert in range(E):
        inner = dot_nn(up_t_ref[expert], norm_ones)
        active, slope = gelu_parts(inner)
        active = active.astype(BF16)
        result = dot_nn(down_t_ref[expert], active) + column(cols, COL_DOWN_B + expert, tile)
        gate = gates[expert : expert + 1, :]
        mixture = mixture + gate * result
        grad_result = (gate * cot).astype(BF16)
        g_down_ref[expert] += dot_nt(jnp.concatenate([active, ones], axis=0), grad_result)
        grad_inner = (slope * dot_nn(down_ref[expert], grad_result)).astype(BF16)
        g_up_ref[expert] += dot_nt(norm_ones, grad_inner)
        grad_norm = grad_norm + dot_nn(up_ref[expert], grad_inner)
    output_ref[...] = jnp.transpose(mixture).astype(BF16)
    g_vec_ref[2] += fold_lanes(grad_norm * unit)
    g_vec_ref[3] += fold_lanes(grad_norm)
    grad_residual = cot + norm_back(grad_norm * gain_two, unit, scale)
    grad_proj = grad_residual.astype(BF16)
    g_out_ref[...] += dot_nt(jnp.concatenate([attended, ones], axis=0), grad_proj)
    grad_own = 0.5 * dot_nn(out_w_ref[...], grad_proj)
    grad_one, grad_two = grad_own * inv_one, grad_own * inv_two
    sum_one = -head_sum(grad_one * own_one)
    sum_two = -head_sum(grad_two * own_two)
    grads = jnp.concatenate([grad_one, grad_two, sum_one, sum_two], axis=0).astype(BF16)

    grads_ref[...] = grads

    def pull_back(item, lanes, start):
        length = lanes.stop - lanes.start
        row = item_row(starts, item, start, length)
        part = grads_ref[:, lanes]
        masked = soft_ref[:, lanes].astype(BF16) * row.astype(BF16)
        return dot_nt(part, masked), row * dot_nn(back_ref[item], part)

    def backward(item, opening):
        if opening:
            sums, pull_ref[...] = pull_back(item, slice(0, tile), begin)
            acc_ref[item] += sums
            return

        def add(lanes, start):
            sums, pull = pull_back(item, lanes, start)
            acc_ref[item] += sums
            pull_ref[:, lanes] += pull

        over_parts(starts, item, begin, tile, add)

    over_items(starts, items, begin, tile, backward)
    pull = pull_ref[...]
    grad_query = (soft * (pull - head_sum(pull * soft))).astype(BF16)
    g_query_ref[...] += dot_nt(norm_ref[...], grad_query)
    grad_norm_one = dot_nn(query_ref[...], grad_query)
    unit_one = unit_ref[...]
    g_vec_ref[0] += fold_lanes(grad_norm_one * unit_one)
    g_vec_ref[1] += fold_lanes(grad_norm_one)
    grad_token = grad_residual + norm_back(
        grad_norm_one * column(cols, COL_GAIN_ONE, tile), unit_one, scale_ref[0:1, :]
    )
    grad_ref[...] = jnp.transpose(grad_token)

    @pl.when(step == steps - 1)
    def _():
        mask = head_mask()
        for slot, target in enumerate((own_msg_ref, other_msg_ref)):
            target[items * HD :, :] = jnp.zeros((target.shape[0] - items * HD, LANES), F32)
            for item in range(items):
                full = acc_ref[item, slot * D : (slot + 1) * D, :]
                target[item * HD : (item + 1) * HD, :] = fold_heads(full, mask)
                sums = acc_ref[item, (2 + slot) * D : (3 + slot) * D, :]
                target[items * HD + item : items * HD + item + 1, :] = fold_heads(sums, mask)[0:1]


def pack_kernel(
    plan,
    scal_ref,
    g_query_ref,
    g_out_ref,
    g_up_ref,
    g_down_ref,
    g_vec_ref,
    own_ref,
    other_ref,
    vec_ref,
    tmp_ref,
):
    parts, shard, half = plan
    vec_ref[SHARED_ROWS:, :] = jnp.zeros((vec_ref.shape[0] - SHARED_ROWS, LANES), F32)
    for slot, row in enumerate((ROW_GAIN_ONE, ROW_SHIFT_ONE, ROW_GAIN_TWO, ROW_SHIFT_TWO)):
        vec_ref[row : row + 1, :] = lane_total_row(g_vec_ref[slot])
    vec_ref[ROW_QUERY : ROW_QUERY + D, :] = g_query_ref[...]
    vec_ref[ROW_OUT : ROW_OUT + D + 1, :] = g_out_ref[: D + 1, :]
    for expert in range(E):
        for part in range(2):
            columns = slice(part * D, (part + 1) * D)
            vec_ref[pl.ds(ROW_UP + expert * 2 * D + part, D, stride=2), :] = g_up_ref[
                expert, :D, columns
            ]
            row = ROW_UP_B + 2 * expert + part
            vec_ref[row : row + 1, :] = g_up_ref[expert, D : D + 1, columns]
        row = ROW_DOWN + expert * FF
        vec_ref[row : row + FF, :] = g_down_ref[expert, :FF, :]
        row = ROW_DOWN_B + expert
        vec_ref[row : row + 1, :] = g_down_ref[expert, FF : FF + 1, :]
    core = scal_ref[0]
    own_at = pl.multiple_of(core * half, 8)
    other_at = pl.multiple_of((1 - core) * half, 8)
    for number in range(parts):
        tmp_ref[...] = take_shard(vec_ref, number, shard, 2 * half)
        own_ref[number] = tmp_ref[pl.ds(own_at, half), :]
        other_ref[number] = tmp_ref[pl.ds(other_at, half), :].astype(BF16)


def sample_backward_kernel(
    plan,
    scal_ref,
    msg_ref,
    func_ref,
    keys_hbm,
    vals_hbm,
    in_t_ref,
    hid_t_ref,
    col_ref,
    hid_ref,
    pair_ref,
    send_ref,
    kept_ref,
    vec_ref,
    left_keys_ref,
    left_vals_ref,
    keys_acc_ref,
    vals_acc_ref,
    g_pair_ref,
    g_hid_ref,
    g_in_ref,
    parts_ref,
    pairs_ref,
    seconds_ref,
    firsts_ref,
    first_ref,
    second_ref,
    starts,
    sems,
):
    tile, items, parts, shard, height, slots, steps = plan
    sources = (keys_hbm, vals_hbm)
    fetches = [
        [
            pltpu.make_async_copy(
                source.at[:, step * tile : (step + 1) * tile],
                kept_ref.at[number, :, step * tile : (step + 1) * tile],
                sems.at[number, step],
            )
            for number, source in enumerate(sources)
        ]
        for step in range(steps)
    ]
    for group in fetches:
        for fetch in group:
            fetch.start()

    def prepare():
        store_starts(lambda item: scal_ref[2 + items + item], starts, items)
        g_pair_ref[...] = jnp.zeros(g_pair_ref.shape, F32)
        g_hid_ref[...] = jnp.zeros(g_hid_ref.shape, F32)
        g_in_ref[...] = jnp.zeros(g_in_ref.shape, F32)
        mask = head_mask()
        low, high = item_span(
            starts, items, scal_ref[1] * slots, scal_ref[1] * slots + tile * steps
        )

        def build(item, carry):
            at = pl.multiple_of(item * HD, HD)
            block = spread_heads(msg_ref[pl.ds(at, HD), :], mask)
            high = block.astype(BF16)
            left_vals_ref[item, :, :D] = high
            left_vals_ref[item, :, D:] = (block - high.astype(F32)).astype(BF16)
            row = msg_ref[pl.ds(items * HD + item, 1), :]
            both = jnp.concatenate([block, row, jnp.zeros((D - 1, D), F32)], axis=0)
            both = jnp.transpose(both)[:, : D + 16]
            high = both.astype(BF16)
            left_keys_ref[item, 0] = high
            left_keys_ref[item, 1] = (both - high.astype(F32)).astype(BF16)
            return carry

        @pl.when(high <= low)
        def _():
            last = items - 1
            left_vals_ref[last] = jnp.zeros((D, 2 * D), BF16)
            left_keys_ref[last] = jnp.zeros((2, D, D + 16), BF16)

        lax.fori_loop(low, high, build, 0)

    def work(step):
        def part(number):
            return kept_ref.at[number, :, step * tile : (step + 1) * tile]

        keys_ref, vals_ref = part(0), part(1)
        fetches[step][0].wait()
        fetches[step][1].wait()
        keys = keys_ref[...]
        ones = jnp.ones((16, tile), BF16)
        vals_ones = jnp.concatenate([vals_ref[...], ones], axis=0)
        begin = scal_ref[1] * slots + step * tile

        def visit(item, opening):
            row = item_row(starts, item, begin, tile)
            fresh_keys = row * (
                dot_nn(left_keys_ref[item, 0], vals_ones) + dot_nn(left_keys_ref[item, 1], vals_ones)
            )
            fresh_vals = row * dot_nn(
                left_vals_ref[item], jnp.concatenate([keys, keys], axis=0)
            )
            keys_acc_ref[...] = fresh_keys if opening else keys_acc_ref[...] + fresh_keys
            vals_acc_ref[...] = fresh_vals if opening else vals_acc_ref[...] + fresh_vals

        over_items(starts, items, begin, tile, visit)
        samples = split_samples(func_ref[0, :, step * tile : (step + 1) * tile], parts_ref)
        chunk = min(CHUNK, tile)

        def backward(start):
            at = slice(start, start + chunk)
            first_in = dot_nn(in_t_ref[...], samples[:, at])
            yield
            first, slope_one = gelu_parts(first_in)
            first = first.astype(BF16)
            first_ref[:, at] = first
            yield
            second_in = dot_nn(hid_t_ref[...], first)
            yield
            second, slope_two = gelu_parts(second_in + wide(col_ref[...], chunk))
            second_ref[:, at] = second.astype(BF16)
            soft = keys_ref[:, at].astype(F32)
            grad_keys = keys_acc_ref[:, at]
            grad_in = soft * (grad_keys - head_sum(grad_keys * soft))
            grad_pair = jnp.concatenate([grad_in, vals_acc_ref[:, at]], axis=0).astype(BF16)
            pairs_ref[:, at] = grad_pair
            yield
            grad_second = dot_nn(pair_ref[...], grad_pair)
            yield
            grad_second = (slope_two * grad_second).astype(BF16)
            seconds_ref[:, at] = grad_second
            yield
            grad_first = dot_nn(hid_ref[...], grad_second)
            yield
            firsts_ref[:, at] = (slope_one * grad_first).astype(BF16)

        staggered([backward(start) for start in range(0, tile, chunk)])
        g_pair_ref[...] += dot_nt(second_ref[...], pairs_ref[...])
        first_ones = jnp.concatenate([first_ref[...], ones], axis=0)
        g_hid_ref[...] += dot_nt(first_ones, seconds_ref[...])
        g_in_ref[...] += dot_nt(samples, firsts_ref[...])

    prepare()
    for step in range(steps):
        work(step)
    vec_ref[BRANCH_ROWS:, :] = jnp.zeros((vec_ref.shape[0] - BRANCH_ROWS, LANES), F32)
    vec_ref[ROW_IN : ROW_IN + FIN, :] = (
        g_in_ref[0:FIN, :] + g_in_ref[FIN : 2 * FIN, :] + g_in_ref[2 * FIN : 3 * FIN, :]
    )
    vec_ref[ROW_IN_B : ROW_IN_B + 1, :] = g_in_ref[3 * FIN : 3 * FIN + 1, :]
    vec_ref[ROW_HID : ROW_HID + D + 1, :] = g_hid_ref[: D + 1, :]
    for part in range(2):
        vec_ref[pl.ds(ROW_PAIR + part, D, stride=2), :] = g_pair_ref[
            :, part * D : (part + 1) * D
        ]
    for number in range(parts):
        send_ref[number] = take_shard(vec_ref, number, shard, height).astype(BF16)


def sum_over_points(values, count, besides, early):
    groups = []
    bit = 1
    while bit < count:
        groups.append([bit] if 2 * bit >= count else [bit, 2 * bit, 3 * bit])
        bit *= 4
    for number, masks in enumerate(reversed(groups)):
        pieces = [
            lax.ppermute(values, "pts", [(source, source ^ mask) for source in range(count)])
            for mask in masks
        ]
        if number < len(besides):
            some = early[number]
            before = besides[number - 1] if number else None
            pieces[some], besides[number] = lax.optimization_barrier(
                (pieces[some], besides[number](before))
            )
        values = functools.reduce(jnp.add, pieces, values)
    return values, besides


def copies(block, count):
    return jnp.broadcast_to(block, (count,) + block.shape)


def swap_cores(values):
    return lax.ppermute(values, "branch", [(0, 1), (1, 0)])


def whole(shape, kind=None):
    zeros = (0,) * len(shape)
    return pl.BlockSpec(shape, lambda *_: zeros)


def body(
    tokens,
    funcs,
    item_counts,
    func_counts,
    gate_ints,
    cotangent,
    shared_master,
    shared_m,
    shared_v,
    branch_master,
    branch_m,
    branch_v,
):
    count = lax.axis_size("pts")
    core = lax.axis_index("branch")
    items = item_counts.shape[0]
    place = jnp.stack([core, lax.axis_index("pts")]).astype(jnp.int32)
    chip_rows = tokens.shape[0]
    rows = chip_rows // 2
    slots = funcs.shape[2]
    shared_len = shared_master.shape[0]
    branch_len = branch_master.shape[1]
    half = up_to(-(-shared_len // (2 * LANES)), 16)
    height = up_to(-(-branch_len // LANES), 16)
    msg_rows = items * HD + up_to(items, 8)
    params = pltpu.CompilerParams(vmem_limit_bytes=VMEM_BASE + items * VMEM_ITEM)
    shape = jax.ShapeDtypeStruct

    shared_pad = jnp.pad(shared_master.astype(BF16), (0, 2 * half * LANES - shared_len))
    shared_half = lax.dynamic_slice_in_dim(shared_pad, core * (half * LANES), half * LANES, 0)
    branch_pad = jnp.pad(
        branch_master.astype(BF16), ((0, 0), (0, height * LANES - branch_len))
    )
    recv_branch = lax.all_to_all(copies(branch_pad.reshape(height, LANES), count), "pts", 0, 0)
    shared_send = copies(shared_half.reshape(half, LANES), count)
    recv_branch, shared_send = lax.optimization_barrier((recv_branch, shared_send))
    recv_shared = lax.all_to_all(shared_send, "pts", 0, 0)

    tile = min(SAMPLE_TILE, slots)
    steps = slots // tile
    stream = lambda height_: pl.BlockSpec((height_, tile), lambda i, *_: (0, i))
    vec_rows = up_to(BRANCH_ROWS + 2 * height + 8, 8)
    (
        msg,
        keys,
        vals,
        hid_w,
        pair_w,
        in_t,
        hid_t,
        hid_col,
    ) = pl.pallas_call(
        functools.partial(
            sample_forward_kernel, (tile, items, count, branch_len, height, slots)
        ),
        grid_spec=pltpu.PrefetchScalarGridSpec(
            num_scalar_prefetch=1,
            grid=(steps,),
            in_specs=[
                pl.BlockSpec(memory_space=pl.ANY),
                pl.BlockSpec((count, height, LANES), lambda i, *_: (0, 0, 0)),
                pl.BlockSpec((1, FIN, tile), lambda i, *_: (0, 0, i)),
            ],
            out_specs=[
                whole((msg_rows, LANES)),
                stream(D),
                stream(D),
                whole((D, D)),
                whole((D, 2 * D)),
                whole((D, 16)),
                whole((D, D)),
                whole((D, D)),
            ],
            scratch_shapes=[
                pltpu.VMEM((vec_rows, LANES), F32),
                pltpu.VMEM((8 + 2 * height, LANES), F32),
                pltpu.VMEM((16, tile), F32),
                pltpu.VMEM((2 * D, D), BF16),
                pltpu.VMEM((items, D + 16, D), F32),
                pltpu.SMEM((items + 1,), jnp.int32),
                pltpu.SMEM((1, items), jnp.int32),
                pltpu.SemaphoreType.DMA,
            ],
        ),
        out_shape=[
            pltpu.VMEM((msg_rows, LANES), F32),
            pltpu.HBM((D, slots), BF16),
            pltpu.HBM((D, slots), BF16),
            shape((D, D), BF16),
            shape((D, 2 * D), BF16),
            shape((D, 16), BF16),
            shape((D, D), BF16),
            shape((D, D), F32),
        ],
        compiler_params=params,
        cost_estimate=pl.CostEstimate(
            flops=slots * D * D * 10, bytes_accessed=slots * D * 12, transcendentals=slots * D * 3
        ),
        name="sample_forward",
    )(
        place,
        pltpu.with_memory_space_constraint(func_counts, pltpu.HBM),
        recv_branch,
        funcs,
    )
    in_t, place, item_counts, func_counts = lax.optimization_barrier(
        (in_t, place, item_counts, func_counts)
    )
    scal = jnp.concatenate([place, item_counts, func_counts.reshape(-1)])


    shared_rows = up_to(SHARED_ROWS + 2 * half + 8, 8)

    def make_weights(recv_shared, recv_other):
        return pl.pallas_call(
            functools.partial(weight_kernel, (count, shared_len, half)),
            in_specs=[
                pl.BlockSpec(memory_space=pltpu.SMEM),
                whole(recv_shared.shape),
                whole(recv_shared.shape),
            ],
            out_specs=[
                whole((D, D)),
                whole((D, D)),
                whole((D, D)),
                whole((D, D)),
                whole((E, D, FF)),
                whole((E, FF, D + 16)),
                whole((E, FF, D)),
                whole((E, D, FF)),
                whole((D, D)),
            ],
            out_shape=[
                shape((D, D), BF16),
                shape((D, D), BF16),
                shape((D, D), BF16),
                shape((D, D), BF16),
                shape((E, D, FF), BF16),
                shape((E, FF, D + 16), BF16),
                shape((E, FF, D), BF16),
                shape((E, D, FF), BF16),
                shape((D, D), F32),
            ],
            scratch_shapes=[
                pltpu.VMEM((shared_rows, LANES), F32),
                pltpu.VMEM((max(8 + 2 * half, D) + 8, LANES), F32),
            ],
            compiler_params=params,
            cost_estimate=pl.CostEstimate(flops=0, bytes_accessed=8 << 20, transcendentals=0),
            name="weights",
        )(scal, recv_shared, recv_other)

    token_tile = min(TOKEN_TILE, rows)
    token_steps = rows // token_tile
    row_block = pl.BlockSpec(
        (token_tile, D), lambda i, scal_ref: (scal_ref[0] * token_steps + i, 0)
    )
    token_stream = lambda height_: pl.BlockSpec((height_, token_tile), lambda i, *_: (0, i))

    def make_queries(weights):
        return pl.pallas_call(
            query_kernel,
            grid_spec=pltpu.PrefetchScalarGridSpec(
                num_scalar_prefetch=1,
                grid=(token_steps,),
                in_specs=[row_block, row_block, whole((D, D)), whole((D, D))],
                out_specs=[
                    token_stream(D),
                    token_stream(D),
                    token_stream(D),
                    token_stream(8),
                    token_stream(D),
                    token_stream(D),
                ],
            ),
            out_shape=[
                shape((D, rows), BF16),
                shape((D, rows), F32),
                shape((D, rows), F32),
                shape((8, rows), F32),
                shape((D, rows), BF16),
                shape((D, rows), F32),
            ],
            compiler_params=params,
            cost_estimate=pl.CostEstimate(
                flops=rows * D * D * 2, bytes_accessed=rows * D * 24, transcendentals=rows * D
            ),
            name="queries",
        )(scal, tokens, cotangent, weights[1], weights[8])

    def beside_two(received):
        weights = make_weights(received, swap_cores(received))
        return weights, make_queries(weights)

    summary, (_, (weights, queries)) = sum_over_points(
        msg, count, [lambda _: recv_shared, beside_two], (slice(1), slice(3))
    )
    query_w, query_t, out_w, out_t, up_w, up_t, down_w, down_t, cols = weights
    token_t, cot_t, unit, scale, norm, soft = queries
    summary_other = swap_cores(summary)

    (
        output_own,
        grad_own,
        own_msg,
        other_msg,
        g_query,
        g_out,
        g_up,
        g_down,
        g_vec,
    ) = pl.pallas_call(
        functools.partial(token_kernel, (token_tile, items, chip_rows, token_steps)),
        grid_spec=pltpu.PrefetchScalarGridSpec(
            num_scalar_prefetch=1,
            grid=(token_steps,),
            in_specs=[
                whole((msg_rows, LANES)),
                whole((msg_rows, LANES)),
                pl.BlockSpec((E, token_tile), lambda i, scal_ref: (0, scal_ref[0] * token_steps + i)),
                token_stream(D),
                token_stream(D),
                token_stream(D),
                token_stream(8),
                token_stream(D),
                token_stream(D),
                whole((D, D)),
                whole((D, D)),
                whole((D, D)),
                whole((E, D, FF)),
                whole((E, FF, D + 16)),
                whole((E, FF, D)),
                whole((E, D, FF)),
                whole((D, D)),
            ],
            out_specs=[
                pl.BlockSpec((token_tile, D), lambda i, *_: (i, 0)),
                pl.BlockSpec((token_tile, D), lambda i, *_: (i, 0)),
                whole((msg_rows, LANES)),
                whole((msg_rows, LANES)),
                whole((D, D)),
                whole((D + 16, D)),
                whole((E, D + 16, FF)),
                whole((E, FF + 16, D)),
                whole((4, D, D)),
            ],
            scratch_shapes=[
                pltpu.VMEM((items, 4 * D, 2 * D), BF16),
                pltpu.VMEM((items, D, 4 * D), BF16),
                pltpu.VMEM((items, 4 * D, D), F32),
                pltpu.VMEM((4 * D, token_tile), F32),
                pltpu.VMEM((D, token_tile), F32),
                pltpu.VMEM((4 * D, token_tile), BF16),
                pltpu.SMEM((items + 1,), jnp.int32),
            ],
        ),
        out_shape=[
            shape((rows, D), BF16),
            shape((rows, D), F32),
            pltpu.VMEM((msg_rows, LANES), F32),
            pltpu.VMEM((msg_rows, LANES), F32),
            shape((D, D), F32),
            shape((D + 16, D), F32),
            shape((E, D + 16, FF), F32),
            shape((E, FF + 16, D), F32),
            shape((4, D, D), F32),
        ],
        compiler_params=params,
        cost_estimate=pl.CostEstimate(
            flops=rows * D * FF * 12 * E, bytes_accessed=rows * D * 24, transcendentals=rows * FF * E
        ),
        name="tokens",
    )(
        scal,
        summary,
        summary_other,
        gate_ints.T,
        token_t,
        cot_t,
        unit,
        scale,
        norm,
        soft,
        query_w,
        out_w,
        out_t,
        up_w,
        up_t,
        down_w,
        down_t,
        cols,
    )

    both_msg, parts = lax.optimization_barrier(
        (own_msg + swap_cores(other_msg), (g_query, g_out, g_up, g_down, g_vec))
    )
    half_own, half_other = pl.pallas_call(
        functools.partial(pack_kernel, (count, shared_len, half)),
        in_specs=[pl.BlockSpec(memory_space=pltpu.SMEM)]
        + [whole(piece.shape) for piece in parts],
        out_specs=[whole((count, half, LANES)), whole((count, half, LANES))],
        out_shape=[shape((count, half, LANES), F32), shape((count, half, LANES), BF16)],
        scratch_shapes=[
            pltpu.VMEM((shared_rows, LANES), F32),
            pltpu.VMEM((2 * half, LANES), F32),
        ],
        compiler_params=params,
        cost_estimate=pl.CostEstimate(flops=2 << 30, bytes_accessed=4 << 20, transcendentals=0),
        name="pack",
    )(scal, *parts)

    output_other = swap_cores(output_own)
    grad_other = swap_cores(grad_own)

    def add_halves(packed):
        half_sum = (packed[0] + swap_cores(packed[1]).astype(F32)).astype(BF16)
        return half_sum, output_other, grad_other

    summary_grad, (_, tail) = sum_over_points(
        both_msg, count, [lambda _: [half_own, half_other], add_halves], (slice(3), slice(2, 3))
    )
    half_sum, output_other, grad_other = tail
    keys, vals = (pltpu.with_memory_space_constraint(kept, pltpu.HBM) for kept in (keys, vals))
    back_tile = min(BACK_TILE, slots)
    back_steps = slots // back_tile
    shared_recv = lax.all_to_all(half_sum, "pts", 0, 0)
    grads_send = pl.pallas_call(
        functools.partial(
            sample_backward_kernel,
            (back_tile, items, count, branch_len, height, slots, back_steps),
        ),
        grid_spec=pltpu.PrefetchScalarGridSpec(
            num_scalar_prefetch=1,
            grid=(1,),
            in_specs=[
                whole((msg_rows, LANES)),
                whole((1, FIN, slots)),
                pl.BlockSpec(memory_space=pl.ANY),
                pl.BlockSpec(memory_space=pl.ANY),
                whole((D, 16)),
                whole((D, D)),
                whole((D, D)),
                whole((D, D)),
                whole((D, 2 * D)),
            ],
            out_specs=whole((count, height, LANES)),
            scratch_shapes=[
                pltpu.VMEM((2, D, slots), BF16),
                pltpu.VMEM((vec_rows, LANES), F32),
                pltpu.VMEM((items, 2, D, D + 16), BF16),
                pltpu.VMEM((items, D, 2 * D), BF16),
                pltpu.VMEM((D, back_tile), F32),
                pltpu.VMEM((D, back_tile), F32),
                pltpu.VMEM((D, 2 * D), F32),
                pltpu.VMEM((D + 16, D), F32),
                pltpu.VMEM((16, D), F32),
                pltpu.VMEM((16, back_tile), F32),
                pltpu.VMEM((2 * D, back_tile), BF16),
                pltpu.VMEM((D, back_tile), BF16),
                pltpu.VMEM((D, back_tile), BF16),
                pltpu.VMEM((D, back_tile), BF16),
                pltpu.VMEM((D, back_tile), BF16),
                pltpu.SMEM((items + 1,), jnp.int32),
                pltpu.SemaphoreType.DMA((2, back_steps)),
            ],
        ),
        out_shape=shape((count, height, LANES), BF16),
        compiler_params=pltpu.CompilerParams(
            vmem_limit_bytes=2 * VMEM_BASE + items * VMEM_ITEM
        ),
        cost_estimate=pl.CostEstimate(
            flops=slots * D * D * 300, bytes_accessed=slots * D * 12, transcendentals=0
        ),
        name="sample_backward",
    )(
        scal,
        summary_grad,
        funcs,
        keys,
        vals,
        in_t,
        hid_t,
        hid_col,
        hid_w,
        pair_w,
    )

    grads_send, shared_recv, halves = lax.optimization_barrier(
        (grads_send, shared_recv, (output_own, output_other, grad_own, grad_other))
    )
    output_own, output_other, grad_own, grad_other = halves
    output = jnp.where(
        core == 0,
        jnp.concatenate([output_own, output_other]),
        jnp.concatenate([output_other, output_own]),
    )
    token_grad = jnp.where(
        core == 0,
        jnp.concatenate([grad_own, grad_other]),
        jnp.concatenate([grad_other, grad_own]),
    )
    own_half = jnp.sum(shared_recv.astype(F32), axis=0).reshape(-1)
    other_half = swap_cores(own_half)
    shared_grad = jnp.where(
        core == 0,
        jnp.concatenate([own_half, other_half]),
        jnp.concatenate([other_half, own_half]),
    )[:shared_len]
    branch_recv = lax.all_to_all(grads_send, "pts", 0, 0)
    branch_grad = jnp.sum(branch_recv.astype(F32), axis=0).reshape(1, -1)[:, :branch_len]
    new_branch, new_branch_m, new_branch_v = adam_step(
        branch_master, branch_m, branch_v, branch_grad
    )
    new_shared, new_shared_m, new_shared_v = adam_step(
        shared_master, shared_m, shared_v, shared_grad
    )
    return (
        output,
        token_grad,
        new_shared,
        new_shared_m,
        new_shared_v,
        new_branch,
        new_branch_m,
        new_branch_v,
    )


def solution(mesh):
    in_specs = (
        P("pts", None),
        P("branch", None, "pts"),
        P(),
        P("branch", None),
        P("pts", None),
        P("pts", None),
        P("pts"),
        P("pts"),
        P("pts"),
        P("branch", "pts"),
        P("branch", "pts"),
        P("branch", "pts"),
    )
    out_specs = (
        P("pts", None),
        P("pts", None),
        P("pts"),
        P("pts"),
        P("pts"),
        P("branch", "pts"),
        P("branch", "pts"),
        P("branch", "pts"),
    )
    return jax.shard_map(body, mesh=mesh, in_specs=in_specs, out_specs=out_specs, check_vma=False)
```
